512 devices in a mesh: ctx: 64 (over z, x, y_hi), head: 8 (over y_lo, core).
Axes of the slice: x: 4, y: 8 (y_hi: 2, y_lo: 4; y = y_hi * 4 + y_lo), z: 8, core: 2. Of those that a mesh axis runs over, the one named last changes fastest.
Arguments:
- query_raw: bfloat16 [8192, 8192], P('ctx', 'head'), may hold values from -6 to 6
- key_before_norm: bfloat16 [8192, 1024], P('ctx', 'head'), may hold values from -6 to 6
- values: bfloat16 [8192, 1024], P('ctx', 'head'), may hold values from -6 to 6
- attention_output_gradient: bfloat16 [8192, 8192], P('ctx', 'head'), may hold values from -6 to 6
- q_gain: float32 [128], replicated, may hold values from 0.5 to 1.5
- k_gain: float32 [128], replicated, may hold values from 0.5 to 1.5
- tok_pos: int32 [8192], P('ctx'), may hold values from 0 to 8191, as said below
Outputs:
- grad_query_raw: bfloat16 [8192, 8192], P('ctx', 'head')
- grad_key_raw: bfloat16 [8192, 1024], P('ctx', 'head')
- value_gradient_rows: bfloat16 [8192, 1024], P('ctx', 'head')
- query_norm_gain_gradient: float32 [128], replicated
- key_norm_gain_gradient: float32 [128], replicated
The draws below stay inside these ranges and needn't reach their ends.
Inputs may be any that keep to these rules, and one draw needn't show every extreme that they name: `tok_pos`: each position appears once. The rows of one device are two runs of 64 consecutive positions in ascending order: run number p and run number 8192 / 64 - 1 - p, where p differs from device to device.
All inputs are finite; a program needn't handle non-finite values.
Results may differ from the reference program's by a relative error of at most 0.0099.
Values may be sent and summed in bfloat16 or wider, within the bound.
A program may use at most 64 MiB of HBM per device.

```python
import jax
import jax.numpy as jnp
from jax import lax

QUERY_HEADS = 64
KEY_VALUE_HEADS = 8
HEAD_SIZE = 128
TOK_DEV = 128
SPAN = 64
SEQUENCE_TOKENS = 8192


def draw_tok_pos(key, part):
    key = jax.random.fold_in(key, 11)
    device_total = SEQUENCE_TOKENS // TOK_DEV
    order = jax.random.permutation(key, device_total).astype(jnp.int32)
    row_index = jnp.arange(SEQUENCE_TOKENS, dtype=jnp.int32)
    owner = row_index // TOK_DEV
    second_run = row_index // SPAN % 2
    early = order[owner]
    run_number = jnp.where(second_run == 0, early, 2 * device_total - 1 - early)
    return (run_number * SPAN + row_index % SPAN).astype(jnp.int32)


def block_scale(own_key, extent, split, smallest, high):
    def one(position, shards_of):
        heights = jax.random.uniform(jax.random.fold_in(jax.random.fold_in(own_key, 6), position), (shards_of,), jnp.float32, smallest / len(split), high / len(split))
        return jnp.repeat(jnp.exp(heights), extent[position] // shards_of).reshape((-1,) + (1,) * (len(extent) - position - 1))

    level = one(*split[0])
    for cut in split[1:]:
        level = level * one(*cut)
    return level


def gaussian(rng, extent, deviation, bound, split=(), kind=jnp.bfloat16):
    level = block_scale(rng, extent, split, -0.22, 0.18) if split else 1.0
    drawn = jax.random.normal(rng, extent, jnp.float32) * deviation * level
    return jnp.minimum(jnp.maximum(drawn, -bound), bound).astype(kind)


def setup_inputs(seed: int = 0) -> dict:
    streams_of = jax.random.split(jax.random.key(seed), 8)
    return {
        "query_raw": gaussian(streams_of[0], (SEQUENCE_TOKENS, QUERY_HEADS * HEAD_SIZE), 1.0, 6.0, ((0, 64), (1, 8))),
        "key_before_norm": gaussian(streams_of[1], (SEQUENCE_TOKENS, KEY_VALUE_HEADS * HEAD_SIZE), 1.0, 6.0, ((0, 64), (1, 8))),
        "values": gaussian(streams_of[2], (SEQUENCE_TOKENS, KEY_VALUE_HEADS * HEAD_SIZE), 1.0, 6.0, ((0, 64), (1, 8))),
        "attention_output_gradient": gaussian(streams_of[3], (SEQUENCE_TOKENS, QUERY_HEADS * HEAD_SIZE), 1.0, 6.0, ((0, 64), (1, 8))),
        "q_gain": jnp.clip(1.0 + 0.1 * jax.random.normal(streams_of[4], (HEAD_SIZE,), jnp.float32), 0.5, 1.5),
        "k_gain": jnp.clip(1.0 + 0.1 * jax.random.normal(streams_of[5], (HEAD_SIZE,), jnp.float32), 0.5, 1.5),
        "tok_pos": draw_tok_pos(jax.random.fold_in(streams_of[7], 71), 0),
    }


norm_epsilon = 1e-06
rope_base = 1000000.0

def rope_tables(positions, width):
    half_width = width // 2
    exponent = jnp.arange(half_width, dtype=jnp.float32) * (2.0 / width)
    frequency = jnp.power(jnp.float32(rope_base), -exponent)
    angles = positions.astype(jnp.float32)[:, None] * frequency[None, :]
    return (jnp.cos(angles)[:, None, :], jnp.sin(angles)[:, None, :])

def rotate(values_in, cosine, sine_table):
    half_width = values_in.shape[-1] // 2
    first_half = values_in[..., :half_width]
    second_half = values_in[..., half_width:]
    return jnp.concatenate([first_half * cosine - second_half * sine_table, second_half * cosine + first_half * sine_table], axis=-1)

def unrotate(incoming, cosine, sine_table):
    half_width = incoming.shape[-1] // 2
    first_half = incoming[..., :half_width]
    second_half = incoming[..., half_width:]
    return jnp.concatenate([first_half * cosine + second_half * sine_table, second_half * cosine - first_half * sine_table], axis=-1)

def apply_norm_forward(raw_heads):
    inverse = lax.rsqrt(lax.optimization_barrier(jnp.mean(raw_heads * raw_heads, axis=-1, keepdims=True)) + norm_epsilon)
    return (raw_heads * inverse, inverse)

def norm_backward(incoming, normed, inverse, gain_vector):
    scaled = incoming * gain_vector
    grad_raw = inverse * (scaled - normed * lax.optimization_barrier(jnp.mean(scaled * normed, axis=-1, keepdims=True)))
    grad_gain = lax.optimization_barrier(jnp.sum(incoming * normed, axis=(0, 1)))
    return (grad_raw, grad_gain)

def round_trip(array_in):
    rounded = lax.optimization_barrier(array_in.astype(jnp.bfloat16))
    return rounded.astype(jnp.float32)

def reference(query_raw, key_before_norm, values, attention_output_gradient, q_gain, k_gain, tok_pos):
    sequence_token_count = query_raw.shape[0]
    queries_per_group = QUERY_HEADS // KEY_VALUE_HEADS
    score_scale = HEAD_SIZE ** (-0.5)
    cosine, sine_table = rope_tables(tok_pos, HEAD_SIZE)
    q_normed, q_inverse = apply_norm_forward(query_raw.astype(jnp.float32).reshape(sequence_token_count, QUERY_HEADS, HEAD_SIZE))
    query_rotated = rotate(q_normed * q_gain, cosine, sine_table).astype(jnp.bfloat16)
    key_after_norm, key_inverse_norm = apply_norm_forward(key_before_norm.astype(jnp.float32).reshape(sequence_token_count, KEY_VALUE_HEADS, HEAD_SIZE))
    k_rot = rotate(key_after_norm * k_gain, cosine, sine_table).astype(jnp.bfloat16)
    query_groups = query_rotated.reshape(sequence_token_count, KEY_VALUE_HEADS, queries_per_group, HEAD_SIZE).transpose(1, 2, 0, 3)
    gradient_groups = attention_output_gradient.reshape(sequence_token_count, KEY_VALUE_HEADS, queries_per_group, HEAD_SIZE).transpose(1, 2, 0, 3)
    k_heads = k_rot.transpose(1, 0, 2)
    value_heads = values.reshape(sequence_token_count, KEY_VALUE_HEADS, HEAD_SIZE).transpose(1, 0, 2)
    block_count = sequence_token_count // TOK_DEV

    def per_head(entries):
        q_head, g_head, k_head, v_head = entries
        k_float = k_head.astype(jnp.float32)
        v_float = v_head.astype(jnp.float32)

        def per_block(carried, block_index):
            acc_key, acc_value = carried
            row_start = block_index * TOK_DEV
            query_block = lax.dynamic_slice_in_dim(q_head, row_start, TOK_DEV, 1).astype(jnp.float32)
            grad_block = lax.dynamic_slice_in_dim(g_head, row_start, TOK_DEV, 1).astype(jnp.float32)
            pos_block = lax.dynamic_slice_in_dim(tok_pos, row_start, TOK_DEV, 0)
            scores = jnp.einsum('gbd,nd->gbn', query_block, k_float) * score_scale
            visible = tok_pos[None, None, :] <= pos_block[None, :, None]
            exp_scores = jnp.where(visible, jnp.exp(scores), 0.0)
            grad_probs = jnp.einsum('gbd,nd->gbn', grad_block, v_float)
            exp_total = lax.optimization_barrier(jnp.sum(exp_scores, axis=-1))
            delta_rows = lax.optimization_barrier(jnp.sum(exp_scores * grad_probs, axis=-1)) / exp_total
            softmax_probs = jnp.where(visible, jnp.exp(scores - jnp.log(exp_total)[..., None]), 0.0)
            grad_scores = softmax_probs * (grad_probs - delta_rows[..., None])
            probs_round = round_trip(softmax_probs)
            scores_round = round_trip(grad_scores)
            grad_query = jnp.einsum('gbn,nd->gbd', scores_round, k_float) * score_scale
            acc_key = acc_key + jnp.einsum('gbn,gbd->nd', scores_round, query_block) * score_scale
            acc_value = acc_value + jnp.einsum('gbn,gbd->nd', probs_round, grad_block)
            return ((acc_key, acc_value), grad_query)
        start_acc = jnp.zeros((sequence_token_count, HEAD_SIZE), jnp.float32)
        finals, grad_query = lax.scan(per_block, (start_acc, start_acc), jnp.arange(block_count, dtype=jnp.int32))
        return (grad_query, finals[0], finals[1])
    grad_query, grad_key, value_gradient_head = lax.map(per_head, (query_groups, gradient_groups, k_heads, value_heads))
    grad_query = grad_query.transpose(1, 3, 0, 2, 4).reshape(sequence_token_count, QUERY_HEADS, HEAD_SIZE)
    grad_key = grad_key.transpose(1, 0, 2)
    query_norm_backward, query_norm_gain_gradient = norm_backward(unrotate(grad_query, cosine, sine_table), q_normed, q_inverse, q_gain)
    key_norm_backward, key_norm_gain_gradient = norm_backward(unrotate(grad_key, cosine, sine_table), key_after_norm, key_inverse_norm, k_gain)
    value_gradient_rows = value_gradient_head.transpose(1, 0, 2).reshape(sequence_token_count, KEY_VALUE_HEADS * HEAD_SIZE).astype(jnp.bfloat16)
    return (query_norm_backward.reshape(sequence_token_count, QUERY_HEADS * HEAD_SIZE).astype(jnp.bfloat16), key_norm_backward.reshape(sequence_token_count, KEY_VALUE_HEADS * HEAD_SIZE).astype(jnp.bfloat16), value_gradient_rows, query_norm_gain_gradient, key_norm_gain_gradient)
```

```python
import functools

import jax
import jax.numpy as jnp
from jax import lax
from jax.experimental import pallas as pl
from jax.experimental.pallas import tpu as pltpu
from jax.sharding import PartitionSpec as P

D = 128
HALF = 64
X, Y, Z = 4, 2, 8
HEADS = 8
EPS = 1e-06
BASE = 1000000.0
SCALE = D ** (-0.5)
LOG2E = 1.4426950408889634
KROWS = 144
F32, BF16 = jnp.float32, jnp.bfloat16
NT = (((1,), (1,)), ((), ()))
NN = (((1,), (0,)), ((), ()))
TN = (((0,), (0,)), ((), ()))


def dot(a, b, dims):
    return lax.dot_general(a, b, dims, preferred_element_type=F32)


def message_table():
    names = ["YK", "YV", "XKR", "XKL", "XKR2", "XKL2"]
    for way in "RL":
        for step in (1, 2, 3):
            names += [f"ZK{way}{step}{half}" for half in (0, 1)]
        names.append(f"ZK{way}4{1 if way == 'R' else 0}")
        names += [f"ZV{way}{step}" for step in (1, 2, 3, 4)]
    for s in range(8):
        names += [f"XVR{s}", f"XVL{s}", f"XVR2{s}", f"XVL2{s}"]
    for way in "RL":
        names.append(f"RK{way}1{1 if way == 'R' else 0}")
        for step in (2, 3, 4):
            names += [f"RK{way}{step}{half}" for half in (0, 1)]
        names += [f"RV{way}{step}" for step in (1, 2, 3, 4)]
        names += [f"RVX1{way}{t}" for t in range(8)]
        names += [f"RVX2{way}{t}" for t in range(8)]
    names += ["RKX1", "RKX2", "RKX3", "RKY", "RVY"]
    return {name: index for index, name in enumerate(names)}


MSG = message_table()


class Part:
    def __init__(self, ref, index=None):
        self.ref, self.index = ref, index

    def make(self):
        return self.ref if self.index is None else self.ref.at[self.index]

    @property
    def at(self):
        return Maker(self.ref)

    def __getitem__(self, index):
        return self.make()[index]

    def __setitem__(self, index, value):
        self.make()[index] = value


class Maker:
    def __init__(self, ref):
        self.ref = ref

    def __getitem__(self, index):
        return Part(self.ref, index)


def body(
    heads_axis, q_ref, k_ref, v_ref, g_ref, qg_ref, kg_ref, cos_ref, sin_ref, p_ref, swap_ref,
    dq_ref, dk_ref, dv_ref, gain_ref,
    kb, vb, e_a, g_a, e_b, g_b, e_d, g_d, qc, gc, sums, stats, dqacc, dkd, dvd,
    dkb, dvb, rk, rvx1, rvx2, rvz, rkx, rky, rvy, ysend, gbuf, gsum,
    ssem, rsem, gssem, grsem,
):
    kb, vb, dkb, dvb, rk, rvx1, rvx2, rvz, rkx, rky, rvy, ysend = (
        Part(ref) for ref in (kb, vb, dkb, dvb, rk, rvx1, rvx2, rvz, rkx, rky, rvy, ysend)
    )
    ctx = lax.axis_index("ctx")
    head = lax.axis_index("head")
    z, x, y = ctx // (X * Y), (ctx // Y) % X, ctx % Y
    w = ctx % (X * Y)
    oy = 1 - y

    zpos = [lax.rem(z + off, Z) for off in range(Z)]
    xpos = [lax.rem(x + off, X) for off in range(X)]

    def zm(off):
        return zpos[off % Z] if isinstance(off, int) else lax.rem(z + off + Z, Z)

    def xm(off):
        return xpos[off % X]


    def dev(zz, xx, yy):
        return ((zz * X + xx) * Y + yy, head)

    def peers():
        out = []
        for j in range(1, 8):
            out.append((lax.rem(z + j, Z) * (X * Y) + w, head))
        for j in range(1, 8):
            out.append((z * (X * Y) + lax.rem(w + j, X * Y), head))
        for j in range(1, heads_axis):
            out.append((ctx, lax.rem(head + j, heads_axis)))
        return out

    barrier = pltpu.get_barrier_semaphore()
    all_peers = peers()
    for peer in all_peers:
        pl.semaphore_signal(barrier, inc=1, device_id=peer, device_id_type=pl.DeviceIdType.MESH)

    started = []

    def copy(name, src, dst, to):
        i = MSG[name]
        return pltpu.make_async_remote_copy(
            src_ref=src.make(), dst_ref=dst.make(), send_sem=ssem.at[i], recv_sem=rsem.at[i],
            device_id=to, device_id_type=pl.DeviceIdType.MESH,
        )

    def send(name, src, dst, to):
        copy(name, src, dst, to).start()
        started.append((name, src, dst, to))

    def arrived(name, dst):
        copy(name, dst, dst, (ctx, head)).wait_recv()

    right_z, left_z = dev(zm(1), x, y), dev(zm(-1), x, y)
    right_x, left_x = dev(z, xm(1), y), dev(z, xm(-1), y)
    side = {"R": (right_z, -1), "L": (left_z, 1)}

    swapped = swap_ref[0:1, :] > 0.5
    p_me = p_ref[...]

    def halves(v):
        first, second = v[:HALF], v[HALF:]
        return jnp.where(swapped, second, first), jnp.where(swapped, first, second)

    def rope(v):
        return v * cos_ref[...] + pltpu.roll(v, HALF, 1) * sin_ref[...]

    def unrope(v):
        return v * cos_ref[...] - pltpu.roll(v, HALF, 1) * sin_ref[...]

    def normed(v):
        inverse = lax.rsqrt(jnp.mean(v * v, axis=-1, keepdims=True) + EPS)
        return v * inverse, inverse

    kn, _ = normed(k_ref[...].astype(F32))
    k_lo, k_hi = halves(rope(kn * kg_ref[...]))
    v_lo, v_hi = halves(v_ref[...].astype(F32))
    kb[z, x, y, 0:HALF] = k_lo.astype(BF16)
    kb[z, x, y, HALF:D] = k_hi.astype(BF16)
    kb[z, x, y, D:KROWS] = jnp.concatenate([p_me, p_me], axis=0).astype(BF16)
    vb[x, z, y, 0:HALF] = v_lo.astype(BF16)
    vb[x, z, y, HALF:D] = v_hi.astype(BF16)

    pl.semaphore_wait(barrier, len(all_peers))

    partner = dev(z, x, oy)
    send("YV", vb.at[x, z, y], vb.at[x, z, y], partner)
    send("YK", kb.at[z, x, y], kb.at[z, x, y], partner)

    for h in range(HEADS):
        cols = slice(h * D, (h + 1) * D)
        rows = slice(h * HALF, (h + 1) * HALF)
        qn, _ = normed(q_ref[:, cols].astype(F32))
        lo, hi = halves(rope(qn * qg_ref[...]))
        qc[rows, 0:D] = lo.astype(BF16)
        qc[rows, D:] = hi.astype(BF16)
        lo, hi = halves(g_ref[:, cols].astype(F32))
        gc[rows, 0:D] = lo.astype(BF16)
        gc[rows, D:] = hi.astype(BF16)

    arrived("YV", vb.at[x, z, oy])
    for way in "RL":
        to, _ = side[way]
        send(f"ZV{way}1", vb.at[x, z], vb.at[x, z], to)
    arrived("YK", kb.at[z, x, oy])
    send("XKR", kb.at[z, x], kb.at[z, x], right_x)
    send("XKL", kb.at[z, x], kb.at[z, x], left_x)
    send("XVR0", vb.at[x, z], vb.at[x, z], right_x)
    send("XVL0", vb.at[x, z], vb.at[x, z], left_x)

    zero = jnp.zeros((HALF, D), BF16)

    def diagonal(buffer_lo, buffer_hi):
        return jnp.concatenate(
            [
                jnp.concatenate([buffer_lo, zero], axis=1),
                jnp.concatenate([zero, buffer_hi], axis=1),
            ],
            axis=0,
        )

    def own_k():
        return diagonal(kb[z, x, y, 0:HALF], kb[z, x, y, HALF:D])

    def own_v():
        return diagonal(vb[x, z, y, 0:HALF], vb[x, z, y, HALF:D])

    scores = dot(own_k(), qc[...], NT)
    key_row = lax.broadcasted_iota(jnp.int32, (D, 8 * HALF), 0) % HALF
    query_lane = lax.broadcasted_iota(jnp.int32, (D, 8 * HALF), 1) % HALF
    exps = jnp.where(key_row <= query_lane, jnp.exp2(scores * (SCALE * LOG2E)), 0.0)
    probs_grad = dot(own_v(), gc[...], NT)
    e_d[...] = exps
    g_d[...] = probs_grad
    both = exps * probs_grad
    for part in range(2):
        rows = slice(part * HALF, (part + 1) * HALF)
        sums[part] = exps[rows].reshape(8, 8, 8 * HALF).sum(0)
        sums[2 + part] = both[rows].reshape(8, 8, 8 * HALF).sum(0)

    arrived("XKR", kb.at[z, xm(-1)])
    send("XKR2", kb.at[z, xm(-1), 0], kb.at[z, xm(-1), 0], right_x)
    arrived("XKL", kb.at[z, xm(1)])
    send("XKL2", kb.at[z, xm(1), 1], kb.at[z, xm(1), 1], left_x)
    arrived("XKR2", kb.at[z, xm(2), 0])
    arrived("XKL2", kb.at[z, xm(2), 1])

    def kpart(zz, half):
        return kb.at[zz, pl.ds(2 * half, 2)]

    for half in range(2):
        for way in "RL":
            to, _ = side[way]
            send(f"ZK{way}1{half}", kpart(z, half), kpart(z, half), to)

    def offset_of(s):
        h = (s + 1) // 2
        return h * (1 - 2 * (s % 2))

    def v_progress(s):
        if s == 0:
            for way, nb in (("R", -1), ("L", 1)):
                arrived(f"XV{way}0", vb.at[xm(nb), z])
                pick = 0 if way == "R" else 1
                src = vb.at[xm(nb), z, pick]
                send(f"XV{way}20", src, src, right_x if way == "R" else left_x)
        d = s + 1
        if d <= 4:
            for way in "RL":
                to, sign = side[way]
                src = zm(sign * d)
                if d < 4:
                    arrived(f"ZV{way}{d}", vb.at[x, src])
                    nxt = vb.at[x, src]
                    if d == 3:
                        nxt = vb.at[x, src, 1 if way == "R" else 0]
                    send(f"ZV{way}{d + 1}", nxt, nxt, to)
                    c = 2 * d - 1 if way == "R" else 2 * d
                    send(f"XVR{c}", vb.at[x, src], vb.at[x, src], right_x)
                    send(f"XVL{c}", vb.at[x, src], vb.at[x, src], left_x)
                else:
                    arrived(f"ZV{way}4", vb.at[x, src, 1 if way == "R" else 0])
            if d == 4:
                src = vb.at[x, zm(4)]
                send("XVR7", src, src, right_x)
                send("XVL7", src, src, left_x)
        if s < 7:
            c = s + 1
            zz = zm(offset_of(c))
            for way, nb in (("R", -1), ("L", 1)):
                arrived(f"XV{way}{c}", vb.at[xm(nb), zz])
                src = vb.at[xm(nb), zz, 0 if way == "R" else 1]
                send(f"XV{way}2{c}", src, src, right_x if way == "R" else left_x)
        zz = zm(offset_of(s))
        arrived(f"XVR2{s}", vb.at[xm(2), zz, 0])
        arrived(f"XVL2{s}", vb.at[xm(2), zz, 1])

    def k_progress(s, half):
        if s == 0:
            return
        d = (s + 1) // 2
        if s < 7:
            way = "R" if s % 2 else "L"
            to, sign = side[way]
            src = kpart(zm(sign * d), half)
            arrived(f"ZK{way}{d}{half}", src)
            if d < 3 or half == (1 if way == "R" else 0):
                send(f"ZK{way}{d + 1}{half}", src, src, to)
        else:
            way = "R" if half == 1 else "L"
            arrived(f"ZK{way}4{half}", kpart(zm(4), half))

    def block_masks(zz, half):
        pj = kb[zz, pl.ds(2 * half, 2), :, D:KROWS, :].reshape(4, 16, D).astype(F32)[:, 0:8, :]
        early = jnp.where(pj < p_me[None], 1.0, 0.0)
        other = jnp.where(pj == p_me[None], 0.0, 1.0)
        return early, other

    def wide(v):
        return jnp.concatenate([v, v, v, v], axis=-1)

    def lows(buffer):
        return buffer[0].reshape(4, HALF, D), buffer[1].reshape(4, HALF, D)

    def k_halves(zz, half):
        return (
            kb[zz, pl.ds(2 * half, 2), :, 0:HALF, :].reshape(4, HALF, D),
            kb[zz, pl.ds(2 * half, 2), :, HALF:D, :].reshape(4, HALF, D),
        )

    def v_halves(zz, half):
        return (
            vb[pl.ds(2 * half, 2), zz, :, 0:HALF, :].reshape(4, HALF, D),
            vb[pl.ds(2 * half, 2), zz, :, HALF:D, :].reshape(4, HALF, D),
        )

    def joined(lo, hi, early):
        e = early[:, 0:1, :].astype(BF16)
        return jnp.concatenate([lo * e, hi * (1.0 - e).astype(BF16)], axis=-1).reshape(4 * HALF, 2 * D)

    def pass_one(s, half, u):
        zz = zm(offset_of(s))
        early, other = block_masks(zz, half)
        klo, khi = k_halves(zz, half)
        vlo, vhi = v_halves(zz, half)
        ex = jnp.exp2(dot(klo.reshape(4 * HALF, D), qc[:, D:], NT) * (SCALE * LOG2E))
        gp = dot(vlo.reshape(4 * HALF, D), gc[:, D:], NT)
        e_a[u] = ex
        g_a[u] = gp
        sums[1] += ex.reshape(32, 8, 8 * HALF).sum(0)
        sums[3] += (ex * gp).reshape(32, 8, 8 * HALF).sum(0)
        ex = jnp.exp2(dot(joined(klo, khi, early), qc[...], NT) * (SCALE * LOG2E))
        ex = (ex.reshape(4, HALF, 8 * HALF) * wide(other[:, 0:1, :]))
        gp = dot(joined(vlo, vhi, early), gc[...], NT).reshape(4, HALF, 8 * HALF)
        e_b[u] = ex.reshape(4 * HALF, 8 * HALF)
        g_b[u] = gp.reshape(4 * HALF, 8 * HALF)
        part = ex.reshape(4, 8, 8, 8 * HALF).sum(1)
        partg = (ex * gp).reshape(4, 8, 8, 8 * HALF).sum(1)
        ew = wide(early)
        sums[0] += (part * ew).sum(0)
        sums[1] += (part * (1.0 - ew)).sum(0)
        sums[2] += (partg * ew).sum(0)
        sums[3] += (partg * (1.0 - ew)).sum(0)

    def first_loop(u, carry):
        s, half = u // 2, u % 2
        for case in range(16):
            @pl.when(u == case)
            def _(case=case):
                if case % 2 == 0:
                    v_progress(case // 2)
                k_progress(case // 2, case % 2)
        pass_one(s, half, u)
        return carry

    lax.fori_loop(0, 16, first_loop, 0)

    for part in range(2):
        inv = 1.0 / jnp.sum(sums[part], axis=0, keepdims=True)
        stats[part] = jnp.broadcast_to(inv, (8, 8 * HALF))
        stats[2 + part] = jnp.broadcast_to(
            jnp.sum(sums[2 + part], axis=0, keepdims=True) * inv, (8, 8 * HALF)
        )

    rowsel = lax.broadcasted_iota(jnp.int32, (D, 8 * HALF), 0) < HALF
    pr = e_d[...] * jnp.where(rowsel, stats[0, 0:1], stats[1, 0:1])
    gs = (pr * (g_d[...] - jnp.where(rowsel, stats[2, 0:1], stats[3, 0:1]))).astype(BF16)
    pr = pr.astype(BF16)
    top = lax.broadcasted_iota(jnp.int32, (D, D), 0) < HALF
    full = dot(pr, gc[...], NN)
    dvd[...] = jnp.where(top, full[:, 0:D], full[:, D:])
    full = dot(gs, qc[...], NN)
    dkd[...] = jnp.where(top, full[:, 0:D], full[:, D:]) * SCALE
    dqacc[...] = dot(own_k(), gs, TN)

    def pass_two(s, half, u):
        zz = zm(offset_of(s))
        early, _ = block_masks(zz, half)
        klo, khi = k_halves(zz, half)
        pr = e_a[u] * stats[1, 0:1]
        gs = (pr * (g_a[u] - stats[3, 0:1])).astype(BF16)
        pr = pr.astype(BF16)
        dva = dot(pr, gc[:, D:], NN).reshape(4, HALF, D)
        dka = dot(gs, qc[:, D:], NN).reshape(4, HALF, D)
        dqacc[D:, :] += dot(klo.reshape(4 * HALF, D), gs, TN)
        ew = wide(early[:, 0:1, :]) > 0.5
        invb = jnp.where(ew, stats[0, 0:1][None], stats[1, 0:1][None])
        delb = jnp.where(ew, stats[2, 0:1][None], stats[3, 0:1][None])
        pr = e_b[u].reshape(4, HALF, 8 * HALF) * invb
        gs = (pr * (g_b[u].reshape(4, HALF, 8 * HALF) - delb)).astype(BF16).reshape(4 * HALF, 8 * HALF)
        pr = pr.astype(BF16).reshape(4 * HALF, 8 * HALF)
        dvc = dot(pr, gc[...], NN).reshape(4, HALF, 2 * D)
        dkc = dot(gs, qc[...], NN).reshape(4, HALF, 2 * D)
        dqacc[...] += dot(joined(klo, khi, early), gs, TN)
        e1 = early[:, 0:1, :]
        pair = pl.ds(2 * half, 2)
        shape = (2, 2, HALF, D)
        dkb[zz, pair, :, 0:HALF, :] = ((dka + dkc[..., 0:D] * e1) * SCALE).astype(BF16).reshape(shape)
        dkb[zz, pair, :, HALF:D, :] = (dkc[..., D:] * ((1.0 - e1) * SCALE)).astype(BF16).reshape(shape)
        dvb[zz, pair, :, 0:HALF, :] = (dva + dvc[..., 0:D] * e1).astype(BF16).reshape(shape)
        dvb[zz, pair, :, HALF:D, :] = (dvc[..., D:] * (1.0 - e1)).astype(BF16).reshape(shape)

    def added(ref, *others):
        total = ref[...].astype(F32)
        for other in others:
            total = total + other[...].astype(F32)
        return total

    def add_into(ref, *others):
        ref[...] = added(ref, *others).astype(BF16)

    def dkpart(zz, half):
        return dkb.at[zz, pl.ds(2 * half, 2)]

    def k_reduce(t, half):
        s = 7 - t
        off = offset_of(s)
        zz = zm(off)
        part = dkpart(zz, half)
        if t == 0:
            wi, way = (0, "R") if half == 1 else (1, "L")
            send(f"RK{way}1{half}", part, rk.at[wi, 0, half], side[way][0])
        elif t < 7:
            way = "R" if off > 0 else "L"
            wi = 0 if way == "R" else 1
            step = 4 - abs(off)
            if step > 1 or half == (1 if way == "R" else 0):
                arrived(f"RK{way}{step}{half}", rk.at[wi, step - 1, half])
                add_into(part, rk.at[wi, step - 1, half])
            send(f"RK{way}{step + 1}{half}", part, rk.at[wi, step, half], side[way][0])
        else:
            for wi, way in enumerate("RL"):
                arrived(f"RK{way}4{half}", rk.at[wi, 3, half])
            add_into(part, rk.at[0, 3, half], rk.at[1, 3, half])

    def v_reduce(t):
        if t < 8:
            zz = zm(offset_of(7 - t))
            send(f"RVX1R{t}", dvb.at[zz, xm(2), 0], rvx1.at[0, t], right_x)
            send(f"RVX1L{t}", dvb.at[zz, xm(2), 1], rvx1.at[1, t], left_x)
        if 1 <= t <= 8:
            c = t - 1
            zz = zm(offset_of(7 - c))
            arrived(f"RVX1R{c}", rvx1.at[0, c])
            add_into(dvb.at[zz, xm(1), 0], rvx1.at[0, c])
            send(f"RVX2R{c}", dvb.at[zz, xm(1)], rvx2.at[0, c], right_x)
            arrived(f"RVX1L{c}", rvx1.at[1, c])
            add_into(dvb.at[zz, xm(-1), 1], rvx1.at[1, c])
            send(f"RVX2L{c}", dvb.at[zz, xm(-1)], rvx2.at[1, c], left_x)
        if 2 <= t <= 9:
            c = t - 2
            off = offset_of(7 - c)
            zz = zm(off)
            arrived(f"RVX2R{c}", rvx2.at[0, c])
            arrived(f"RVX2L{c}", rvx2.at[1, c])
            if c == 0:
                add_into(dvb.at[zz, x], rvx2.at[0, c], rvx2.at[1, c])
                send("RVR1", dvb.at[zz, x, 1], rvz.at[0, 0, 1], right_z)
                send("RVL1", dvb.at[zz, x, 0], rvz.at[1, 0, 0], left_z)
            elif c < 7:
                way = "R" if off > 0 else "L"
                wi = 0 if way == "R" else 1
                step = 4 - abs(off)
                add_into(dvb.at[zz, x], rvx2.at[0, c], rvx2.at[1, c])
                if step == 1:
                    side_half = 1 if way == "R" else 0
                    arrived(f"RV{way}1", rvz.at[wi, 0, side_half])
                    add_into(dvb.at[zz, x, side_half], rvz.at[wi, 0, side_half])
                else:
                    arrived(f"RV{way}{step}", rvz.at[wi, step - 1])
                    add_into(dvb.at[zz, x], rvz.at[wi, step - 1])
                send(f"RV{way}{step + 1}", dvb.at[zz, x], rvz.at[wi, step], side[way][0])
            else:
                arrived("RVR4", rvz.at[0, 3])
                arrived("RVL4", rvz.at[1, 3])
                add_into(dvb.at[zz, x], rvx2.at[0, c], rvx2.at[1, c], rvz.at[0, 3], rvz.at[1, 3])

    def second_loop(i, carry):
        t, half = i // 2, i % 2
        s = 7 - t
        pass_two(s, half, 2 * s + half)
        for case in range(16):
            @pl.when(i == case)
            def _(case=case):
                k_reduce(case // 2, case % 2)
                if case % 2 == 1:
                    v_reduce(case // 2)
        return carry

    lax.fori_loop(0, 16, second_loop, 0)
    for j in (1, 2, 3):
        send(f"RKX{j}", dkb.at[z, xm(j)], rkx.at[j - 1], dev(z, xm(j), y))
    v_reduce(8)

    def stored(lo, hi):
        return jnp.concatenate(
            [jnp.where(swapped, hi, lo), jnp.where(swapped, lo, hi)], axis=0
        )

    def norm_back(g, xn, inverse, gain):
        s = g * gain
        return inverse * (s - xn * jnp.mean(s * xn, axis=-1, keepdims=True))

    turned = jnp.transpose(dqacc[...]) * SCALE
    gain_sum = jnp.zeros((1, D), F32)
    for h in range(HEADS):
        cols = slice(h * D, (h + 1) * D)
        rows = slice(h * HALF, (h + 1) * HALF)
        gq = unrope(stored(turned[rows, 0:D], turned[rows, D:]))
        qn, inverse = normed(q_ref[:, cols].astype(F32))
        gain_sum = gain_sum + jnp.sum(gq * qn, axis=0, keepdims=True)
        dq_ref[:, cols] = norm_back(gq, qn, inverse, qg_ref[...]).astype(BF16)

    for j in (1, 2, 3):
        arrived(f"RKX{j}", rkx.at[j - 1])
    ysend[0] = added(dkb.at[z, x, oy], rkx.at[0, oy], rkx.at[1, oy], rkx.at[2, oy]).astype(BF16)
    send("RKY", ysend.at[0], rky, partner)
    v_reduce(9)
    send("RVY", dvb.at[z, x, oy], rvy, partner)
    dk_own = added(dkb.at[z, x, y], rkx.at[0, y], rkx.at[1, y], rkx.at[2, y]) + dkd[...]
    arrived("RKY", rky)
    dk_own = dk_own + rky[...].astype(F32)
    gk = unrope(stored(dk_own[:HALF], dk_own[HALF:]))
    kn, inverse = normed(k_ref[...].astype(F32))
    key_gain = jnp.sum(gk * kn, axis=0, keepdims=True)
    dk_ref[...] = norm_back(gk, kn, inverse, kg_ref[...]).astype(BF16)

    mine = jnp.concatenate([gain_sum, key_gain, jnp.zeros((6, D), F32)], axis=0)
    groups = (
        (z, Z, lambda j: (lax.rem(z + j, Z) * (X * Y) + w, head)),
        (w, X * Y, lambda j: (z * (X * Y) + lax.rem(w + j, X * Y), head)),
        (head, heads_axis, lambda j: (ctx, lax.rem(head + j, heads_axis))),
    )
    for stage, (me, size, peer) in enumerate(groups):
        gsum[stage] = mine
        gbuf[stage, me] = mine
        copies = []
        for j in range(1, size):
            c = pltpu.make_async_remote_copy(
                src_ref=gsum.at[stage], dst_ref=gbuf.at[stage, me],
                send_sem=gssem.at[stage, j], recv_sem=grsem.at[stage, j],
                device_id=peer(j), device_id_type=pl.DeviceIdType.MESH,
            )
            c.start()
            copies.append(c)
        if stage == 0:
            arrived("RVY", rvy)
            dv_own = added(dvb.at[z, x, y], rvy) + dvd[...]
            dv_ref[...] = stored(dv_own[:HALF], dv_own[HALF:]).astype(BF16)
        for c in copies:
            c.wait()
        mine = gbuf[stage, 0]
        for j in range(1, size):
            mine = mine + gbuf[stage, j]
    gain_ref[...] = mine

    for name, src, dst, to in started:
        copy(name, src, dst, to).wait_send()


def shards(heads_axis, query_raw, key_before_norm, values, grads, q_gain, k_gain, tok_pos):
    first, second = tok_pos[0], tok_pos[HALF]
    run = (jnp.minimum(first, second) // HALF).astype(F32)
    p = jnp.full((8, D), run, F32)
    swap = jnp.full((8, D), (first > second).astype(F32), F32)
    frequency = jnp.power(F32(BASE), -(jnp.arange(HALF, dtype=F32) * (2.0 / D)))
    angles = tok_pos.astype(F32)[:, None] * frequency[None, :]
    cosine, sine = jnp.cos(angles), jnp.sin(angles)
    cos2 = jnp.concatenate([cosine, cosine], axis=-1)
    sin2 = jnp.concatenate([-sine, sine], axis=-1)
    vmem = pl.BlockSpec(memory_space=pltpu.VMEM)
    Q = HEADS * HALF
    count = len(MSG)
    dq, dk, dv, gains = pl.pallas_call(
        functools.partial(body, heads_axis),
        out_shape=(
            jax.ShapeDtypeStruct((D, HEADS * D), BF16),
            jax.ShapeDtypeStruct((D, D), BF16),
            jax.ShapeDtypeStruct((D, D), BF16),
            jax.ShapeDtypeStruct((8, D), F32),
        ),
        in_specs=[vmem] * 10,
        out_specs=(vmem,) * 4,
        scratch_shapes=[
            pltpu.VMEM((Z, X, Y, KROWS, D), BF16),
            pltpu.VMEM((X, Z, Y, D, D), BF16),
            pltpu.VMEM((16, 4 * HALF, Q), F32),
            pltpu.VMEM((16, 4 * HALF, Q), F32),
            pltpu.VMEM((16, 4 * HALF, Q), F32),
            pltpu.VMEM((16, 4 * HALF, Q), F32),
            pltpu.VMEM((D, Q), F32),
            pltpu.VMEM((D, Q), F32),
            pltpu.VMEM((Q, 2 * D), BF16),
            pltpu.VMEM((Q, 2 * D), BF16),
            pltpu.VMEM((4, 8, Q), F32),
            pltpu.VMEM((4, 8, Q), F32),
            pltpu.VMEM((2 * D, Q), F32),
            pltpu.VMEM((D, D), F32),
            pltpu.VMEM((D, D), F32),
            pltpu.VMEM((Z, X, Y, D, D), BF16),
            pltpu.VMEM((Z, X, Y, D, D), BF16),
            pltpu.VMEM((2, 4, 2, 2, 2, D, D), BF16),
            pltpu.VMEM((2, 8, D, D), BF16),
            pltpu.VMEM((2, 8, 2, D, D), BF16),
            pltpu.VMEM((2, 4, 2, D, D), BF16),
            pltpu.VMEM((3, 2, D, D), BF16),
            pltpu.VMEM((D, D), BF16),
            pltpu.VMEM((D, D), BF16),
            pltpu.VMEM((1, D, D), BF16),
            pltpu.VMEM((3, 8, 8, D), F32),
            pltpu.VMEM((3, 8, D), F32),
            pltpu.SemaphoreType.DMA((count,)),
            pltpu.SemaphoreType.DMA((count,)),
            pltpu.SemaphoreType.DMA((3, 8)),
            pltpu.SemaphoreType.DMA((3, 8)),
        ],
        compiler_params=pltpu.CompilerParams(
            collective_id=0, has_side_effects=True, vmem_limit_bytes=60 * 1024 * 1024
        ),
    )(
        query_raw, key_before_norm, values, grads,
        q_gain.reshape(1, D), k_gain.reshape(1, D), cos2, sin2, p, swap,
    )
    return dq, dk, dv, gains[0], gains[1]


def solution(mesh):
    split = P("ctx", "head")
    return jax.shard_map(
        functools.partial(shards, mesh.shape["head"]),
        mesh=mesh,
        in_specs=(split, split, split, split, P(), P(), P("ctx")),
        out_specs=(split, split, split, P(), P()),
        check_vma=False,
    )
```

```python
import functools

import jax
import jax.numpy as jnp
from jax import lax
from jax.experimental import pallas as pl
from jax.experimental.pallas import tpu as pltpu
from jax.sharding import PartitionSpec as P

D = 128
HALF = 64
X, Y, Z = 4, 2, 8
HEADS = 8
Q = HEADS * HALF
EPS = 1e-06
BASE = 1000000.0
SCALE = D ** (-0.5)
LOG2E = 1.4426950408889634
KROWS = 144
F32, BF16 = jnp.float32, jnp.bfloat16
NT = (((1,), (1,)), ((), ()))
NN = (((1,), (0,)), ((), ()))
TN = (((0,), (0,)), ((), ()))


def dot(a, b, dims):
    return lax.dot_general(a, b, dims, preferred_element_type=F32)


def message_table():
    names = ["Y", "QR", "QL", "GR", "GL", "Q2", "G2"]
    for way in "RL":
        for step in (1, 2, 3):
            names += [f"Z{way}{step}{r}" for r in (0, 1)]
        names.append(f"Z{way}4{0 if way == 'R' else 1}")
        names.append(f"S{way}1{0 if way == 'R' else 1}")
        for step in (2, 3, 4):
            names += [f"S{way}{step}{r}" for r in (0, 1)]
    for j in range(4):
        names += [f"ST{j}{m}" for m in (1, 2, 3)]
    names += ["DQ1", "DQ2", "DQ3", "SY"]
    return {name: index for index, name in enumerate(names)}


MSG = message_table()


class Part:
    def __init__(self, ref, index=None):
        self.ref, self.index = ref, index

    def make(self):
        return self.ref if self.index is None else self.ref.at[self.index]

    @property
    def at(self):
        return Maker(self.ref)

    def __getitem__(self, index):
        return self.make()[index]

    def __setitem__(self, index, value):
        self.make()[index] = value


class Maker:
    def __init__(self, ref):
        self.ref = ref

    def __getitem__(self, index):
        return Part(self.ref, index)


def rel_of(j):
    return j + (j // 2) * (5 - 2 * j)


def body(
    heads_axis, q_ref, k_ref, v_ref, g_ref, qg_ref, kg_ref, cos_ref, sin_ref, p_ref, swap_ref,
    dq_ref, dk_ref, dv_ref, gain_ref,
    kv, qc, gc, e_a, g_a, e_b, g_b, e_d, g_d, sums, stbuf, stats, dqacc, dkd, dvd, dkacc, dvacc,
    dkv, ring, dqs, dqr, ysend, yrecv, gbuf, gsum,
    ssem, rsem, gssem, grsem,
):
    kv, qc, gc, stbuf, dkv, ring, dqs, dqr, ysend, yrecv = (
        Part(ref) for ref in (kv, qc, gc, stbuf, dkv, ring, dqs, dqr, ysend, yrecv)
    )
    ctx = lax.axis_index("ctx")
    head = lax.axis_index("head")
    z, x, y = ctx // (X * Y), (ctx // Y) % X, ctx % Y
    w = ctx % (X * Y)
    ys = (y, 1 - y)

    zpos = [lax.rem(z + off, Z) for off in range(Z)]
    xpos = [lax.rem(x + off, X) for off in range(X)]

    def zm(off):
        return zpos[off % Z]

    def xm(off):
        return xpos[off % X]

    def dev(zz, xx, yy):
        return ((zz * X + xx) * Y + yy, head)

    groups = (
        (z, Z, lambda j: (lax.rem(z + j, Z) * (X * Y) + w, head)),
        (w, X * Y, lambda j: (z * (X * Y) + lax.rem(w + j, X * Y), head)),
        (head, heads_axis, lambda j: (ctx, lax.rem(head + j, heads_axis))),
    )
    all_peers = [peer(j) for _, size, peer in groups for j in range(1, size)]

    barrier = pltpu.get_barrier_semaphore()
    for peer in all_peers:
        pl.semaphore_signal(barrier, inc=1, device_id=peer, device_id_type=pl.DeviceIdType.MESH)

    started = []

    def copy(name, src, dst, to):
        i = MSG[name]
        return pltpu.make_async_remote_copy(
            src_ref=src.make(), dst_ref=dst.make(), send_sem=ssem.at[i], recv_sem=rsem.at[i],
            device_id=to, device_id_type=pl.DeviceIdType.MESH,
        )

    def send(name, src, dst, to):
        copy(name, src, dst, to).start()
        started.append((name, src, dst, to))

    def arrived(name, dst):
        copy(name, dst, dst, (ctx, head)).wait_recv()

    xdev = [dev(z, xpos[m], y) for m in range(X)]
    right_x, left_x = dev(z, xm(1), y), dev(z, xm(-1), y)
    partner = dev(z, x, ys[1])
    side = {"R": (dev(zm(1), x, y), -1), "L": (dev(zm(-1), x, y), 1)}
    last = {"R": 0, "L": 1}

    swapped = swap_ref[0:1, :] > 0.5
    p_me = p_ref[...]
    p_rows = jnp.concatenate([p_me, p_me], axis=0).astype(BF16)

    def halves(v):
        first, second = v[:HALF], v[HALF:]
        return jnp.where(swapped, second, first), jnp.where(swapped, first, second)

    def rope(v):
        return v * cos_ref[...] + pltpu.roll(v, HALF, 1) * sin_ref[...]

    def unrope(v):
        return v * cos_ref[...] - pltpu.roll(v, HALF, 1) * sin_ref[...]

    def normed(v):
        inverse = lax.rsqrt(jnp.mean(v * v, axis=-1, keepdims=True) + EPS)
        return v * inverse, inverse

    kn, _ = normed(k_ref[...].astype(F32))
    k_lo, k_hi = halves(rope(kn * kg_ref[...]))
    v_lo, v_hi = halves(v_ref[...].astype(F32))
    kv[z, y, 0:HALF] = k_lo.astype(BF16)
    kv[z, y, HALF:D] = k_hi.astype(BF16)
    kv[z, y, D:KROWS] = p_rows
    kv[z, y, KROWS:KROWS + HALF] = v_lo.astype(BF16)
    kv[z, y, KROWS + HALF:KROWS + D] = v_hi.astype(BF16)
    for h in range(HEADS):
        rows = slice(h * HALF, (h + 1) * HALF)
        lo, hi = halves(g_ref[:, h * D:(h + 1) * D].astype(F32))
        gc[x, rows, 0:D] = lo.astype(BF16)
        gc[x, rows, D:] = hi.astype(BF16)

    pl.semaphore_wait(barrier, len(all_peers))

    send("Y", kv.at[z, y], kv.at[z, y], partner)
    send("GL", gc.at[x], gc.at[x], left_x)
    send("GR", gc.at[x], gc.at[x], right_x)
    for way in "RL":
        send(f"Z{way}10", kv.at[z, y], kv.at[z, y], side[way][0])

    for h in range(HEADS):
        rows = slice(h * HALF, (h + 1) * HALF)
        qn, _ = normed(q_ref[:, h * D:(h + 1) * D].astype(F32))
        lo, hi = halves(rope(qn * qg_ref[...]))
        qc[x, rows, 0:D] = lo.astype(BF16)
        qc[x, rows, D:] = hi.astype(BF16)
    qc[x, Q:, 0:D] = p_rows
    qc[x, Q:, D:] = p_rows
    send("QR", qc.at[x], qc.at[x], right_x)
    send("QL", qc.at[x], qc.at[x], left_x)

    zero = jnp.zeros((HALF, D), BF16)

    def diagonal(lo, hi):
        return jnp.concatenate(
            [jnp.concatenate([lo, zero], axis=1), jnp.concatenate([zero, hi], axis=1)], axis=0
        )

    def own_k():
        return diagonal(kv[z, y, 0:HALF], kv[z, y, HALF:D])

    scores = dot(own_k(), qc[x, 0:Q], NT)
    key_row = lax.broadcasted_iota(jnp.int32, (D, Q), 0) % HALF
    query_lane = lax.broadcasted_iota(jnp.int32, (D, Q), 1) % HALF
    exps = jnp.where(key_row <= query_lane, jnp.exp2(scores * (SCALE * LOG2E)), 0.0)
    own_v = diagonal(kv[z, y, KROWS:KROWS + HALF], kv[z, y, KROWS + HALF:KROWS + D])
    probs_grad = dot(own_v, gc[x], NT)
    e_d[...] = exps
    g_d[...] = probs_grad
    both = exps * probs_grad
    for part in range(2):
        rows = slice(part * HALF, (part + 1) * HALF)
        sums[part] = exps[rows].reshape(8, 8, Q).sum(0)
        sums[2 + part] = both[rows].reshape(8, 8, Q).sum(0)

    arrived("Y", kv.at[z, ys[1]])
    for way in "RL":
        send(f"Z{way}11", kv.at[z, ys[1]], kv.at[z, ys[1]], side[way][0])

    def kv_progress(d):
        for r in (0, 1):
            for way in "RL":
                to, sign = side[way]
                if d == 4 and r != last[way]:
                    continue
                block = kv.at[zm(sign * d), ys[r]]
                arrived(f"Z{way}{d}{r}", block)
                if d < 3 or (d == 3 and r == last[way]):
                    send(f"Z{way}{d + 1}{r}", block, block, to)

    def block_rows(k, first, count):
        near = lax.rem(z + k, Z)
        far = lax.rem(z + (Z - 1) - k, Z)
        return jnp.concatenate(
            [kv[near, :, first:first + count, :], kv[far, :, first:first + count, :]], axis=0
        )

    def block_masks(k, b):
        pj = block_rows(k, D, 16).astype(F32)[:, 0:8, :]
        pq = qc[b, Q:, 0:D].astype(F32)[None, 0:8]
        early = jnp.where(pj < pq, 1.0, 0.0)
        other = jnp.where(pj == pq, 0.0, 1.0)
        return early, other

    def wide(v):
        return jnp.concatenate([v, v, v, v], axis=-1)

    def joined(lo, hi, early):
        e = early[:, 0:1, :].astype(BF16)
        return jnp.concatenate([lo * e, hi * (1.0 - e).astype(BF16)], axis=-1).reshape(4 * HALF, 2 * D)

    def pass_one(k, b, u):
        early, other = block_masks(k, b)
        klo, khi = block_rows(k, 0, HALF), block_rows(k, HALF, HALF)
        vlo, vhi = block_rows(k, KROWS, HALF), block_rows(k, KROWS + HALF, HALF)
        ex = jnp.exp2(dot(klo.reshape(4 * HALF, D), qc[b, 0:Q, D:], NT) * (SCALE * LOG2E))
        gp = dot(vlo.reshape(4 * HALF, D), gc[b, :, D:], NT)
        e_a[u] = ex
        g_a[u] = gp
        sums[1] += ex.reshape(32, 8, Q).sum(0)
        sums[3] += (ex * gp).reshape(32, 8, Q).sum(0)
        ex = jnp.exp2(dot(joined(klo, khi, early), qc[b, 0:Q], NT) * (SCALE * LOG2E))
        ex = ex.reshape(4, HALF, Q) * wide(other[:, 0:1, :])
        gp = dot(joined(vlo, vhi, early), gc[b], NT).reshape(4, HALF, Q)
        e_b[u] = ex.reshape(4 * HALF, Q)
        g_b[u] = gp.reshape(4 * HALF, Q)
        part = ex.reshape(4, 8, 8, Q).sum(1)
        partg = (ex * gp).reshape(4, 8, 8, Q).sum(1)
        ew = wide(early)
        sums[0] += (part * ew).sum(0)
        sums[1] += (part * (1.0 - ew)).sum(0)
        sums[2] += (partg * ew).sum(0)
        sums[3] += (partg * (1.0 - ew)).sum(0)

    def query_progress(j, k):
        if j == 0:
            kv_progress(k + 1)
            if k == 3:
                arrived("GL", gc.at[xm(1)])
                send("G2", gc.at[xm(1)], gc.at[xm(1)], left_x)
                arrived("QR", qc.at[xm(-1)])
                send("Q2", qc.at[xm(-1)], qc.at[xm(-1)], right_x)
        if k == 0:
            if j == 1:
                arrived("QL", qc.at[xm(1)])
            elif j == 2:
                arrived("GR", gc.at[xm(-1)])
            elif j == 3:
                arrived("Q2", qc.at[xm(2)])
                arrived("G2", gc.at[xm(2)])

    def statistics_out(j):
        b = xm(rel_of(j))
        slot = stbuf.at[b, x]
        slot[...] = jnp.concatenate(
            [jnp.sum(sums[...], axis=1), jnp.zeros((4, Q), F32)], axis=0
        )
        for m in (1, 2, 3):
            send(f"ST{j}{m}", slot, slot, xdev[m])
        sums[...] = jnp.zeros((4, 8, Q), F32)

    def first_loop(i, carry):
        j, k = i // 4, i % 4
        for case in range(16):
            @pl.when(i == case)
            def _(case=case):
                query_progress(case // 4, case % 4)
        rel = rel_of(j)
        pass_one(k, lax.rem(x + rel, X), k * 4 + rel)
        for case in range(4):
            @pl.when(i == 4 * case + 3)
            def _(case=case):
                statistics_out(case)
        return carry

    lax.fori_loop(0, 16, first_loop, 0)

    for j in range(4):
        for m in (1, 2, 3):
            arrived(f"ST{j}{m}", stbuf.at[xm(rel_of(j) - m), xm(-m)])
    for b in range(4):
        total = stbuf[b, 0]
        for s in range(1, 4):
            total = total + stbuf[b, s]
        inv = 1.0 / total[0:2]
        stats[b] = jnp.concatenate([inv, total[2:4] * inv, jnp.zeros((4, Q), F32)], axis=0)

    rowsel = lax.broadcasted_iota(jnp.int32, (D, Q), 0) < HALF
    pr = e_d[...] * jnp.where(rowsel, stats[x, 0:1], stats[x, 1:2])
    gs = (pr * (g_d[...] - jnp.where(rowsel, stats[x, 2:3], stats[x, 3:4]))).astype(BF16)
    pr = pr.astype(BF16)
    top = lax.broadcasted_iota(jnp.int32, (D, D), 0) < HALF
    full = dot(pr, gc[x], NN)
    dvd[...] = jnp.where(top, full[:, 0:D], full[:, D:])
    full = dot(gs, qc[x, 0:Q], NN)
    dkd[...] = jnp.where(top, full[:, 0:D], full[:, D:]) * SCALE
    for m in (1, 2, 3):
        dqacc[m] = jnp.zeros((2 * D, Q), F32)
    dqacc[0] = dot(own_k(), gs, TN)

    def pass_two(k, b, rel, u):
        early, _ = block_masks(k, b)
        klo, khi = block_rows(k, 0, HALF), block_rows(k, HALF, HALF)
        pr = e_a[u] * stats[b, 1:2]
        gs = (pr * (g_a[u] - stats[b, 3:4])).astype(BF16)
        pr = pr.astype(BF16)
        dva = dot(pr, gc[b, :, D:], NN).reshape(4, HALF, D)
        dka = dot(gs, qc[b, 0:Q, D:], NN).reshape(4, HALF, D)
        dqacc[rel, D:, :] += dot(klo.reshape(4 * HALF, D), gs, TN)
        ew = wide(early[:, 0:1, :]) > 0.5
        invb = jnp.where(ew, stats[b, 0:1][None], stats[b, 1:2][None])
        delb = jnp.where(ew, stats[b, 2:3][None], stats[b, 3:4][None])
        pr = e_b[u].reshape(4, HALF, Q) * invb
        gs = (pr * (g_b[u].reshape(4, HALF, Q) - delb)).astype(BF16).reshape(4 * HALF, Q)
        pr = pr.astype(BF16).reshape(4 * HALF, Q)
        dvc = dot(pr, gc[b], NN).reshape(4, HALF, 2 * D)
        dkc = dot(gs, qc[b, 0:Q], NN).reshape(4, HALF, 2 * D)
        dqacc[rel] += dot(joined(klo, khi, early), gs, TN)
        e1 = early[:, 0:1, :]
        dkacc[:, 0:HALF] += dka + dkc[..., 0:D] * e1
        dkacc[:, HALF:] += dkc[..., D:] * (1.0 - e1)
        dvacc[:, 0:HALF] += dva + dvc[..., 0:D] * e1
        dvacc[:, HALF:] += dvc[..., D:] * (1.0 - e1)

    def clear():
        dkacc[...] = jnp.zeros((4, D, D), F32)
        dvacc[...] = jnp.zeros((4, D, D), F32)

    def reduce_step(k):
        for place, zz in enumerate((zm(k), zm(-k - 1))):
            rows = slice(2 * place, 2 * place + 2)
            dkv[zz, :, 0:D, :] = (dkacc[rows] * SCALE).astype(BF16)
            dkv[zz, :, D:, :] = dvacc[rows].astype(BF16)
        if k > 0:
            clear()
        if k == 3:
            for wi, way in enumerate("RL"):
                r = last[way]
                send(f"S{way}1{r}", dkv.at[zm(4), ys[r]], ring.at[wi, 0, r], side[way][0])
            return
        off = k + 1
        step = 4 - off
        for r in (0, 1):
            for wi, way in enumerate("RL"):
                zz = zm(off if way == "R" else -off)
                part = dkv.at[zz, ys[r]]
                if step > 1 or r == last[way]:
                    came = ring.at[wi, step - 1, r]
                    arrived(f"S{way}{step}{r}", came)
                    part[...] = (part[...].astype(F32) + came[...].astype(F32)).astype(BF16)
                send(f"S{way}{step + 1}{r}", part, ring.at[wi, step, r], side[way][0])

    clear()

    def second_loop(i, carry):
        k, j = 3 - i // 4, 3 - i % 4
        rel = rel_of(j)
        pass_two(k, lax.rem(x + rel, X), rel, k * 4 + rel)
        for case in range(12, 15):
            @pl.when(i == case)
            def _(case=case):
                m = rel_of(3 - case % 4)
                dqs[m - 1] = dqacc[m].astype(BF16)
                send(f"DQ{m}", dqs.at[m - 1], dqr.at[m - 1], xdev[m])
        for case in range(4):
            @pl.when(i == 4 * case + 3)
            def _(case=case):
                reduce_step(3 - case)
        return carry

    lax.fori_loop(0, 16, second_loop, 0)

    def own_sum(r):
        total = dkv[z, ys[r]].astype(F32)
        for wi in (0, 1):
            total = total + ring[wi, 3, r].astype(F32)
        return total

    for r in (1, 0):
        for way in "RL":
            wi = 0 if way == "R" else 1
            arrived(f"S{way}4{r}", ring.at[wi, 3, r])
        if r == 1:
            ysend[...] = own_sum(1).astype(BF16)
            send("SY", ysend, yrecv, partner)

    def stored(lo, hi):
        return jnp.concatenate(
            [jnp.where(swapped, hi, lo), jnp.where(swapped, lo, hi)], axis=0
        )

    def norm_back(g, xn, inverse, gain):
        s = g * gain
        return inverse * (s - xn * jnp.mean(s * xn, axis=-1, keepdims=True))

    whole = dqacc[0]
    for m in (1, 2, 3):
        arrived(f"DQ{m}", dqr.at[m - 1])
        whole = whole + dqr[m - 1].astype(F32)
    turned = jnp.transpose(whole) * SCALE
    gain_sum = jnp.zeros((1, D), F32)
    for h in range(HEADS):
        cols = slice(h * D, (h + 1) * D)
        rows = slice(h * HALF, (h + 1) * HALF)
        gq = unrope(stored(turned[rows, 0:D], turned[rows, D:]))
        qn, inverse = normed(q_ref[:, cols].astype(F32))
        gain_sum = gain_sum + jnp.sum(gq * qn, axis=0, keepdims=True)
        dq_ref[:, cols] = norm_back(gq, qn, inverse, qg_ref[...]).astype(BF16)

    arrived("SY", yrecv)
    own = own_sum(0) + yrecv[...].astype(F32)
    dk_own = own[0:D] + dkd[...]
    gk = unrope(stored(dk_own[:HALF], dk_own[HALF:]))
    kn, inverse = normed(k_ref[...].astype(F32))
    key_gain = jnp.sum(gk * kn, axis=0, keepdims=True)

    mine = jnp.concatenate([gain_sum, key_gain, jnp.zeros((6, D), F32)], axis=0)
    for stage, (me, size, peer) in enumerate(groups):
        gsum[stage] = mine
        gbuf[stage, me] = mine
        copies = []
        for j in range(1, size):
            c = pltpu.make_async_remote_copy(
                src_ref=gsum.at[stage], dst_ref=gbuf.at[stage, me],
                send_sem=gssem.at[stage, j], recv_sem=grsem.at[stage, j],
                device_id=peer(j), device_id_type=pl.DeviceIdType.MESH,
            )
            c.start()
            copies.append(c)
        if stage == 0:
            dk_ref[...] = norm_back(gk, kn, inverse, kg_ref[...]).astype(BF16)
            dv_own = own[D:] + dvd[...]
            dv_ref[...] = stored(dv_own[:HALF], dv_own[HALF:]).astype(BF16)
        for c in copies:
            c.wait()
        mine = gbuf[stage, 0]
        for j in range(1, size):
            mine = mine + gbuf[stage, j]
    gain_ref[...] = mine

    for name, src, dst, to in started:
        copy(name, src, dst, to).wait_send()


def shards(heads_axis, query_raw, key_before_norm, values, grads, q_gain, k_gain, tok_pos):
    first, second = tok_pos[0], tok_pos[HALF]
    run = (jnp.minimum(first, second) // HALF).astype(F32)
    p = jnp.full((8, D), run, F32)
    swap = jnp.full((8, D), (first > second).astype(F32), F32)
    frequency = jnp.power(F32(BASE), -(jnp.arange(HALF, dtype=F32) * (2.0 / D)))
    angles = tok_pos.astype(F32)[:, None] * frequency[None, :]
    cosine, sine = jnp.cos(angles), jnp.sin(angles)
    cos2 = jnp.concatenate([cosine, cosine], axis=-1)
    sin2 = jnp.concatenate([-sine, sine], axis=-1)
    vmem = pl.BlockSpec(memory_space=pltpu.VMEM)
    count = len(MSG)
    dq, dk, dv, gains = pl.pallas_call(
        functools.partial(body, heads_axis),
        out_shape=(
            jax.ShapeDtypeStruct((D, HEADS * D), BF16),
            jax.ShapeDtypeStruct((D, D), BF16),
            jax.ShapeDtypeStruct((D, D), BF16),
            jax.ShapeDtypeStruct((8, D), F32),
        ),
        in_specs=[vmem] * 10,
        out_specs=(vmem,) * 4,
        scratch_shapes=[
            pltpu.VMEM((Z, Y, KROWS + D, D), BF16),
            pltpu.VMEM((X, Q + 16, 2 * D), BF16),
            pltpu.VMEM((X, Q, 2 * D), BF16),
            pltpu.VMEM((16, 4 * HALF, Q), F32),
            pltpu.VMEM((16, 4 * HALF, Q), F32),
            pltpu.VMEM((16, 4 * HALF, Q), F32),
            pltpu.VMEM((16, 4 * HALF, Q), F32),
            pltpu.VMEM((D, Q), F32),
            pltpu.VMEM((D, Q), F32),
            pltpu.VMEM((4, 8, Q), F32),
            pltpu.VMEM((X, X, 8, Q), F32),
            pltpu.VMEM((X, 8, Q), F32),
            pltpu.VMEM((X, 2 * D, Q), F32),
            pltpu.VMEM((D, D), F32),
            pltpu.VMEM((D, D), F32),
            pltpu.VMEM((4, D, D), F32),
            pltpu.VMEM((4, D, D), F32),
            pltpu.VMEM((Z, Y, 2 * D, D), BF16),
            pltpu.VMEM((2, 4, 2, 2 * D, D), BF16),
            pltpu.VMEM((3, 2 * D, Q), BF16),
            pltpu.VMEM((3, 2 * D, Q), BF16),
            pltpu.VMEM((2 * D, D), BF16),
            pltpu.VMEM((2 * D, D), BF16),
            pltpu.VMEM((3, 8, 8, D), F32),
            pltpu.VMEM((3, 8, D), F32),
            pltpu.SemaphoreType.DMA((count,)),
            pltpu.SemaphoreType.DMA((count,)),
            pltpu.SemaphoreType.DMA((3, 8)),
            pltpu.SemaphoreType.DMA((3, 8)),
        ],
        compiler_params=pltpu.CompilerParams(
            collective_id=0, has_side_effects=True, vmem_limit_bytes=60 * 1024 * 1024
        ),
    )(
        query_raw, key_before_norm, values, grads,
        q_gain.reshape(1, D), k_gain.reshape(1, D), cos2, sin2, p, swap,
    )
    return dq, dk, dv, gains[0], gains[1]


def solution(mesh):
    split = P("ctx", "head")
    return jax.shard_map(
        functools.partial(shards, mesh.shape["head"]),
        mesh=mesh,
        in_specs=(split, split, split, split, P(), P(), P("ctx")),
        out_specs=(split, split, split, P(), P()),
        check_vma=False,
    )
```

```python
import functools

import jax
import jax.numpy as jnp
import numpy as np
from jax import lax
from jax.experimental import pallas as pl
from jax.experimental.pallas import tpu as pltpu
from jax.sharding import PartitionSpec as P

D = 128
HALF = 64
X, Y, Z = 4, 2, 8
HEADS = 8
Q = HEADS * HALF
EPS = 1e-06
BASE = 1000000.0
SCALE = D ** (-0.5)
LOG2E = 1.4426950408889634
KROWS = 144
F32, BF16 = jnp.float32, jnp.bfloat16
NT = (((1,), (1,)), ((), ()))
NN = (((1,), (0,)), ((), ()))
TN = (((0,), (0,)), ((), ()))


def dot(a, b, dims):
    return lax.dot_general(a, b, dims, preferred_element_type=F32)


def message_table():
    names = ["Y", "QR", "QL", "GR", "GL", "Q2", "G2"]
    for way in "RL":
        for step in (1, 2, 3):
            names += [f"Z{way}{step}{r}" for r in (0, 1)]
        names.append(f"Z{way}4{0 if way == 'R' else 1}")
        names.append(f"S{way}1{0 if way == 'R' else 1}")
        for step in (2, 3, 4):
            names += [f"S{way}{step}{r}" for r in (0, 1)]
    for j in range(4):
        names += [f"ST{j}{m}" for m in (1, 2, 3)]
    names += ["DQ1", "DQ2", "DQ3", "SY"]
    return {name: index for index, name in enumerate(names)}


MSG = message_table()


class Part:
    def __init__(self, ref, index=None):
        self.ref, self.index = ref, index

    def make(self):
        return self.ref if self.index is None else self.ref.at[self.index]

    @property
    def at(self):
        return Maker(self.ref)

    def __getitem__(self, index):
        return self.make()[index]

    def __setitem__(self, index, value):
        self.make()[index] = value


class Maker:
    def __init__(self, ref):
        self.ref = ref

    def __getitem__(self, index):
        return Part(self.ref, index)


def rel_of(j):
    return j + (j // 2) * (5 - 2 * j)


def body(
    heads_axis, q_ref, k_ref, v_ref, g_ref, qg_ref, kg_ref, pos_ref, freq_ref,
    dq_ref, dk_ref, dv_ref, gain_ref,
    cos_ref, sin_ref, kv, qc, gc, e_a, g_a, e_b, g_b, e_d, g_d, sums, stbuf, stats, dqacc, dkd, dvd, dkacc, dvacc,
    dkv, ring, dqs, dqr, ysend, yrecv, gbuf, gsum,
    ssem, rsem, gssem, grsem,
):
    kv, qc, gc, stbuf, dkv, ring, dqs, dqr, ysend, yrecv = (
        Part(ref) for ref in (kv, qc, gc, stbuf, dkv, ring, dqs, dqr, ysend, yrecv)
    )
    ctx = lax.axis_index("ctx")
    head = lax.axis_index("head")
    z, x, y = ctx // (X * Y), (ctx // Y) % X, ctx % Y
    w = ctx % (X * Y)
    ys = (y, 1 - y)

    zpos = [lax.rem(z + off, Z) for off in range(Z)]
    xpos = [lax.rem(x + off, X) for off in range(X)]

    def zm(off):
        return zpos[off % Z]

    def xm(off):
        return xpos[off % X]

    def dev(zz, xx, yy):
        return ((zz * X + xx) * Y + yy, head)

    groups = (
        (z, Z, lambda j: (lax.rem(z + j, Z) * (X * Y) + w, head)),
        (w, X * Y, lambda j: (z * (X * Y) + lax.rem(w + j, X * Y), head)),
        (head, heads_axis, lambda j: (ctx, lax.rem(head + j, heads_axis))),
    )
    all_peers = [peer(j) for _, size, peer in groups for j in range(1, size)]

    barrier = pltpu.get_barrier_semaphore()
    for peer in all_peers:
        pl.semaphore_signal(barrier, inc=1, device_id=peer, device_id_type=pl.DeviceIdType.MESH)

    started = []

    def copy(name, src, dst, to):
        i = MSG[name]
        return pltpu.make_async_remote_copy(
            src_ref=src.make(), dst_ref=dst.make(), send_sem=ssem.at[i], recv_sem=rsem.at[i],
            device_id=to, device_id_type=pl.DeviceIdType.MESH,
        )

    def send(name, src, dst, to):
        copy(name, src, dst, to).start()
        started.append((name, src, dst, to))

    def arrived(name, dst):
        copy(name, dst, dst, (ctx, head)).wait_recv()

    xdev = [dev(z, xpos[m], y) for m in range(X)]
    right_x, left_x = dev(z, xm(1), y), dev(z, xm(-1), y)
    partner = dev(z, x, ys[1])
    side = {"R": (dev(zm(1), x, y), -1), "L": (dev(zm(-1), x, y), 1)}
    last = {"R": 0, "L": 1}

    positions = jnp.broadcast_to(pos_ref[...].astype(F32), (8, D))
    in_first = lax.broadcasted_iota(jnp.int32, (8, D), 1) < HALF
    first_top = jnp.max(jnp.where(in_first, positions, -1.0), axis=1, keepdims=True)
    second_top = jnp.max(jnp.where(in_first, -1.0, positions), axis=1, keepdims=True)
    swapped = jnp.broadcast_to(first_top > second_top, (8, D))[0:1]
    lowest = jnp.min(positions, axis=1, keepdims=True)
    p_me = jnp.broadcast_to(jnp.floor(lowest * (1.0 / HALF)), (8, D))
    p_rows = jnp.concatenate([p_me, p_me], axis=0).astype(BF16)

    def halves(v):
        first, second = v[:HALF], v[HALF:]
        return jnp.where(swapped, second, first), jnp.where(swapped, first, second)

    def rope(v):
        return v * cos_ref[...] + pltpu.roll(v, HALF, 1) * sin_ref[...]

    def unrope(v):
        return v * cos_ref[...] - pltpu.roll(v, HALF, 1) * sin_ref[...]

    def normed(v):
        inverse = lax.rsqrt(jnp.mean(v * v, axis=-1, keepdims=True) + EPS)
        return v * inverse, inverse

    for h in range(HEADS):
        rows = slice(h * HALF, (h + 1) * HALF)
        lo, hi = halves(g_ref[:, h * D:(h + 1) * D].astype(F32))
        gc[x, rows, 0:D] = lo.astype(BF16)
        gc[x, rows, D:] = hi.astype(BF16)

    pl.semaphore_wait(barrier, len(all_peers))

    send("GL", gc.at[x], gc.at[x], left_x)
    send("GR", gc.at[x], gc.at[x], right_x)

    angles = jnp.transpose(jnp.broadcast_to(positions[0:1], (D, D))) * freq_ref[...]
    cos_ref[...] = jnp.cos(angles)
    turn = jnp.sin(angles)
    sin_ref[...] = jnp.where(lax.broadcasted_iota(jnp.int32, (D, D), 1) < HALF, -turn, turn)

    kn, _ = normed(k_ref[...].astype(F32))
    k_lo, k_hi = halves(rope(kn * kg_ref[...]))
    v_lo, v_hi = halves(v_ref[...].astype(F32))
    kv[z, y, 0:HALF] = k_lo.astype(BF16)
    kv[z, y, HALF:D] = k_hi.astype(BF16)
    kv[z, y, D:KROWS] = p_rows
    kv[z, y, KROWS:KROWS + HALF] = v_lo.astype(BF16)
    kv[z, y, KROWS + HALF:KROWS + D] = v_hi.astype(BF16)
    send("Y", kv.at[z, y], kv.at[z, y], partner)
    for way in "RL":
        send(f"Z{way}10", kv.at[z, y], kv.at[z, y], side[way][0])

    for h in range(HEADS):
        rows = slice(h * HALF, (h + 1) * HALF)
        qn, _ = normed(q_ref[:, h * D:(h + 1) * D].astype(F32))
        lo, hi = halves(rope(qn * qg_ref[...]))
        qc[x, rows, 0:D] = lo.astype(BF16)
        qc[x, rows, D:] = hi.astype(BF16)
    qc[x, Q:, 0:D] = p_rows
    qc[x, Q:, D:] = p_rows
    send("QR", qc.at[x], qc.at[x], right_x)
    send("QL", qc.at[x], qc.at[x], left_x)

    zero = jnp.zeros((HALF, D), BF16)

    def diagonal(lo, hi):
        return jnp.concatenate(
            [jnp.concatenate([lo, zero], axis=1), jnp.concatenate([zero, hi], axis=1)], axis=0
        )

    def own_k():
        return diagonal(kv[z, y, 0:HALF], kv[z, y, HALF:D])

    scores = dot(own_k(), qc[x, 0:Q], NT)
    key_row = lax.broadcasted_iota(jnp.int32, (D, Q), 0) % HALF
    query_lane = lax.broadcasted_iota(jnp.int32, (D, Q), 1) % HALF
    exps = jnp.where(key_row <= query_lane, jnp.exp2(scores * (SCALE * LOG2E)), 0.0)
    own_v = diagonal(kv[z, y, KROWS:KROWS + HALF], kv[z, y, KROWS + HALF:KROWS + D])
    probs_grad = dot(own_v, gc[x], NT)
    e_d[...] = exps
    g_d[...] = probs_grad
    both = exps * probs_grad
    for j in (1, 2, 3):
        sums[j] = jnp.zeros((4, 8, Q), F32)
    for part in range(2):
        rows = slice(part * HALF, (part + 1) * HALF)
        sums[0, part] = exps[rows].reshape(8, 8, Q).sum(0)
        sums[0, 2 + part] = both[rows].reshape(8, 8, Q).sum(0)

    def kv_progress(r, d):
        for way in "RL":
            to, sign = side[way]
            if d == 4 and r != last[way]:
                continue
            block = kv.at[zm(sign * d), ys[r]]
            arrived(f"Z{way}{d}{r}", block)
            if d < 3 or (d == 3 and r == last[way]):
                send(f"Z{way}{d + 1}{r}", block, block, to)

    def y_progress():
        arrived("Y", kv.at[z, ys[1]])
        for way in "RL":
            send(f"Z{way}11", kv.at[z, ys[1]], kv.at[z, ys[1]], side[way][0])

    def gradient_forward():
        arrived("GL", gc.at[xm(1)])
        send("G2", gc.at[xm(1)], gc.at[xm(1)], left_x)

    def query_forward():
        arrived("QR", qc.at[xm(-1)])
        send("Q2", qc.at[xm(-1)], qc.at[xm(-1)], right_x)

    def far_queries():
        arrived("Q2", qc.at[xm(2)])
        arrived("G2", gc.at[xm(2)])

    def key_event(r, d):
        return lambda: kv_progress(r, d)

    events = {
        0: (key_event(0, 1), y_progress, key_event(0, 2), gradient_forward, key_event(1, 1)),
        1: (
            key_event(0, 3), key_event(1, 2), query_forward,
            lambda: arrived("QL", qc.at[xm(1)]),
        ),
        2: (lambda: arrived("GR", gc.at[xm(-1)]),),
        3: (key_event(0, 4),),
        6: (key_event(1, 3),),
        9: (key_event(1, 4),),
        12: (far_queries,),
    }

    def block_rows(k, first, count):
        near = lax.rem(z + k, Z)
        far = lax.rem(z + (Z - 1) - k, Z)
        return jnp.concatenate(
            [kv[near, :, first:first + count, :], kv[far, :, first:first + count, :]], axis=0
        )

    def block_masks(k, b):
        pj = block_rows(k, D, 16).astype(F32)[:, 0:8, :]
        pq = qc[b, Q:, 0:D].astype(F32)[None, 0:8]
        early = jnp.where(pj < pq, 1.0, 0.0)
        other = jnp.where(pj == pq, 0.0, 1.0)
        return early, other

    def wide(v):
        return jnp.concatenate([v, v, v, v], axis=-1)

    def joined(lo, hi, early):
        e = early[:, 0:1, :].astype(BF16)
        return jnp.concatenate([lo * e, hi * (1.0 - e).astype(BF16)], axis=-1).reshape(4 * HALF, 2 * D)

    def pass_one(k, j, b, u):
        early, other = block_masks(k, b)
        klo, khi = block_rows(k, 0, HALF), block_rows(k, HALF, HALF)
        vlo, vhi = block_rows(k, KROWS, HALF), block_rows(k, KROWS + HALF, HALF)
        ex = jnp.exp2(dot(klo.reshape(4 * HALF, D), qc[b, 0:Q, D:], NT) * (SCALE * LOG2E))
        gp = dot(vlo.reshape(4 * HALF, D), gc[b, :, D:], NT)
        e_a[u] = ex
        g_a[u] = gp
        sums[j, 1] += ex.reshape(32, 8, Q).sum(0)
        sums[j, 3] += (ex * gp).reshape(32, 8, Q).sum(0)
        ex = jnp.exp2(dot(joined(klo, khi, early), qc[b, 0:Q], NT) * (SCALE * LOG2E))
        ex = ex.reshape(4, HALF, Q) * wide(other[:, 0:1, :])
        gp = dot(joined(vlo, vhi, early), gc[b], NT).reshape(4, HALF, Q)
        e_b[u] = ex.reshape(4 * HALF, Q)
        g_b[u] = gp.reshape(4 * HALF, Q)
        part = ex.reshape(4, 8, 8, Q).sum(1)
        partg = (ex * gp).reshape(4, 8, 8, Q).sum(1)
        ew = wide(early)
        sums[j, 0] += (part * ew).sum(0)
        sums[j, 1] += (part * (1.0 - ew)).sum(0)
        sums[j, 2] += (partg * ew).sum(0)
        sums[j, 3] += (partg * (1.0 - ew)).sum(0)

    def statistics_out(j):
        b = xm(rel_of(j))
        slot = stbuf.at[b, x]
        slot[...] = jnp.concatenate(
            [jnp.sum(sums[j], axis=1), jnp.zeros((4, Q), F32)], axis=0
        )
        for m in (1, 2, 3):
            send(f"ST{j}{m}", slot, slot, xdev[m])

    def first_loop(i, carry):
        far = i // 12
        k = (1 - far) * (i // 3) + far * (i - 12)
        j = (1 - far) * (i % 3) + far * 3
        for case, steps in events.items():
            @pl.when(i == case)
            def _(steps=steps):
                for step in steps:
                    step()
        rel = rel_of(j)
        pass_one(k, j, lax.rem(x + rel, X), k * 4 + rel)
        for case, done in ((9, 0), (10, 1), (11, 2), (15, 3)):
            @pl.when(i == case)
            def _(done=done):
                statistics_out(done)
        return carry

    lax.fori_loop(0, 16, first_loop, 0)

    for j in range(4):
        for m in (1, 2, 3):
            arrived(f"ST{j}{m}", stbuf.at[xm(rel_of(j) - m), xm(-m)])
    for b in range(4):
        total = stbuf[b, 0]
        for s in range(1, 4):
            total = total + stbuf[b, s]
        inv = 1.0 / total[0:2]
        stats[b] = jnp.concatenate([inv, total[2:4] * inv, jnp.zeros((4, Q), F32)], axis=0)

    rowsel = lax.broadcasted_iota(jnp.int32, (D, Q), 0) < HALF
    pr = e_d[...] * jnp.where(rowsel, stats[x, 0:1], stats[x, 1:2])
    gs = (pr * (g_d[...] - jnp.where(rowsel, stats[x, 2:3], stats[x, 3:4]))).astype(BF16)
    pr = pr.astype(BF16)
    top = lax.broadcasted_iota(jnp.int32, (D, D), 0) < HALF
    full = dot(pr, gc[x], NN)
    dvd[...] = jnp.where(top, full[:, 0:D], full[:, D:])
    full = dot(gs, qc[x, 0:Q], NN)
    dkd[...] = jnp.where(top, full[:, 0:D], full[:, D:]) * SCALE
    for m in (1, 2, 3):
        dqacc[m] = jnp.zeros((2 * D, Q), F32)
    for k in range(4):
        dkacc[k] = jnp.zeros((4, D, D), F32)
        dvacc[k] = jnp.zeros((4, D, D), F32)
    dqacc[0] = dot(own_k(), gs, TN)

    def pass_two(k, b, rel, u):
        early, _ = block_masks(k, b)
        klo, khi = block_rows(k, 0, HALF), block_rows(k, HALF, HALF)
        pr = e_a[u] * stats[b, 1:2]
        gs = (pr * (g_a[u] - stats[b, 3:4])).astype(BF16)
        pr = pr.astype(BF16)
        dva = dot(pr, gc[b, :, D:], NN).reshape(4, HALF, D)
        dka = dot(gs, qc[b, 0:Q, D:], NN).reshape(4, HALF, D)
        dqacc[rel, D:, :] += dot(klo.reshape(4 * HALF, D), gs, TN)
        ew = wide(early[:, 0:1, :]) > 0.5
        invb = jnp.where(ew, stats[b, 0:1][None], stats[b, 1:2][None])
        delb = jnp.where(ew, stats[b, 2:3][None], stats[b, 3:4][None])
        pr = e_b[u].reshape(4, HALF, Q) * invb
        gs = (pr * (g_b[u].reshape(4, HALF, Q) - delb)).astype(BF16).reshape(4 * HALF, Q)
        pr = pr.astype(BF16).reshape(4 * HALF, Q)
        dvc = dot(pr, gc[b], NN).reshape(4, HALF, 2 * D)
        dkc = dot(gs, qc[b, 0:Q], NN).reshape(4, HALF, 2 * D)
        dqacc[rel] += dot(joined(klo, khi, early), gs, TN)
        e1 = early[:, 0:1, :]
        dkacc[k, :, 0:HALF] += dka + dkc[..., 0:D] * e1
        dkacc[k, :, HALF:] += dkc[..., D:] * (1.0 - e1)
        dvacc[k, :, 0:HALF] += dva + dvc[..., 0:D] * e1
        dvacc[k, :, HALF:] += dvc[..., D:] * (1.0 - e1)

    def reduce_step(k):
        for place, zz in enumerate((zm(k), zm(-k - 1))):
            rows = slice(2 * place, 2 * place + 2)
            dkv[zz, :, 0:D, :] = (dkacc[k, rows] * SCALE).astype(BF16)
            dkv[zz, :, D:, :] = dvacc[k, rows].astype(BF16)
        if k == 3:
            for wi, way in enumerate("RL"):
                r = last[way]
                send(f"S{way}1{r}", dkv.at[zm(4), ys[r]], ring.at[wi, 0, r], side[way][0])
            return
        off = k + 1
        step = 4 - off
        for r in (0, 1):
            for wi, way in enumerate("RL"):
                zz = zm(off if way == "R" else -off)
                part = dkv.at[zz, ys[r]]
                if step > 1 or r == last[way]:
                    came = ring.at[wi, step - 1, r]
                    arrived(f"S{way}{step}{r}", came)
                    part[...] = (part[...].astype(F32) + came[...].astype(F32)).astype(BF16)
                send(f"S{way}{step + 1}{r}", part, ring.at[wi, step, r], side[way][0])


    def queries_out(m):
        dqs[m - 1] = dqacc[m].astype(BF16)
        send(f"DQ{m}", dqs.at[m - 1], dqr.at[m - 1], xdev[m])

    def second_loop(i, carry):
        near = (i + 12) // 16
        k = (1 - near) * (3 - i) + near * (3 - (i + 8) // 3 + 4)
        j = (1 - near) * 3 + near * (2 - (i + 8) % 3)
        rel = rel_of(j)
        pass_two(k, lax.rem(x + rel, X), rel, k * 4 + rel)
        for case, m in ((3, 2), (13, 3), (14, 1)):
            @pl.when(i == case)
            def _(m=m):
                queries_out(m)
        for case in range(4):
            @pl.when(i == 3 * case + 6)
            def _(case=case):
                reduce_step(3 - case)
        return carry

    lax.fori_loop(0, 16, second_loop, 0)

    def own_sum(r):
        total = dkv[z, ys[r]].astype(F32)
        for wi in (0, 1):
            total = total + ring[wi, 3, r].astype(F32)
        return total

    for r in (1, 0):
        for way in "RL":
            wi = 0 if way == "R" else 1
            arrived(f"S{way}4{r}", ring.at[wi, 3, r])
        if r == 1:
            ysend[...] = own_sum(1).astype(BF16)
            send("SY", ysend, yrecv, partner)

    def stored(lo, hi):
        return jnp.concatenate(
            [jnp.where(swapped, hi, lo), jnp.where(swapped, lo, hi)], axis=0
        )

    def norm_back(g, xn, inverse, gain):
        s = g * gain
        return inverse * (s - xn * jnp.mean(s * xn, axis=-1, keepdims=True))

    whole = dqacc[0]
    for m in (1, 2, 3):
        arrived(f"DQ{m}", dqr.at[m - 1])
        whole = whole + dqr[m - 1].astype(F32)
    turned = jnp.transpose(whole) * SCALE
    gain_sum = jnp.zeros((1, D), F32)
    for h in range(HEADS):
        cols = slice(h * D, (h + 1) * D)
        rows = slice(h * HALF, (h + 1) * HALF)
        gq = unrope(stored(turned[rows, 0:D], turned[rows, D:]))
        qn, inverse = normed(q_ref[:, cols].astype(F32))
        gain_sum = gain_sum + jnp.sum(gq * qn, axis=0, keepdims=True)
        dq_ref[:, cols] = norm_back(gq, qn, inverse, qg_ref[...]).astype(BF16)

    arrived("SY", yrecv)
    own = own_sum(0) + yrecv[...].astype(F32)
    dk_own = own[0:D] + dkd[...]
    gk = unrope(stored(dk_own[:HALF], dk_own[HALF:]))
    kn, inverse = normed(k_ref[...].astype(F32))
    key_gain = jnp.sum(gk * kn, axis=0, keepdims=True)

    mine = jnp.concatenate([gain_sum, key_gain, jnp.zeros((6, D), F32)], axis=0)
    for stage, (me, size, peer) in enumerate(groups):
        gsum[stage] = mine
        gbuf[stage, me] = mine
        copies = []
        for j in range(1, size):
            c = pltpu.make_async_remote_copy(
                src_ref=gsum.at[stage], dst_ref=gbuf.at[stage, me],
                send_sem=gssem.at[stage, j], recv_sem=grsem.at[stage, j],
                device_id=peer(j), device_id_type=pl.DeviceIdType.MESH,
            )
            c.start()
            copies.append(c)
        if stage == 0:
            dk_ref[...] = norm_back(gk, kn, inverse, kg_ref[...]).astype(BF16)
            dv_own = own[D:] + dvd[...]
            dv_ref[...] = stored(dv_own[:HALF], dv_own[HALF:]).astype(BF16)
        for c in copies:
            c.wait()
        mine = gbuf[stage, 0]
        for j in range(1, size):
            mine = mine + gbuf[stage, j]
    gain_ref[...] = mine

    for name, src, dst, to in started:
        copy(name, src, dst, to).wait_send()


def shards(heads_axis, query_raw, key_before_norm, values, grads, q_gain, k_gain, tok_pos):
    frequency = np.power(np.float32(BASE), -(np.arange(HALF, dtype=np.float32) * np.float32(2.0 / D)))
    frequency = jnp.asarray(np.tile(frequency.astype(np.float32), 2).reshape(1, D))
    vmem = pl.BlockSpec(memory_space=pltpu.VMEM)
    count = len(MSG)
    dq, dk, dv, gains = pl.pallas_call(
        functools.partial(body, heads_axis),
        out_shape=(
            jax.ShapeDtypeStruct((D, HEADS * D), BF16),
            jax.ShapeDtypeStruct((D, D), BF16),
            jax.ShapeDtypeStruct((D, D), BF16),
            jax.ShapeDtypeStruct((8, D), F32),
        ),
        in_specs=[vmem] * 8,
        out_specs=(vmem,) * 4,
        scratch_shapes=[
            pltpu.VMEM((D, D), F32),
            pltpu.VMEM((D, D), F32),
            pltpu.VMEM((Z, Y, KROWS + D, D), BF16),
            pltpu.VMEM((X, Q + 16, 2 * D), BF16),
            pltpu.VMEM((X, Q, 2 * D), BF16),
            pltpu.VMEM((16, 4 * HALF, Q), F32),
            pltpu.VMEM((16, 4 * HALF, Q), F32),
            pltpu.VMEM((16, 4 * HALF, Q), F32),
            pltpu.VMEM((16, 4 * HALF, Q), F32),
            pltpu.VMEM((D, Q), F32),
            pltpu.VMEM((D, Q), F32),
            pltpu.VMEM((4, 4, 8, Q), F32),
            pltpu.VMEM((X, X, 8, Q), F32),
            pltpu.VMEM((X, 8, Q), F32),
            pltpu.VMEM((X, 2 * D, Q), F32),
            pltpu.VMEM((D, D), F32),
            pltpu.VMEM((D, D), F32),
            pltpu.VMEM((4, 4, D, D), F32),
            pltpu.VMEM((4, 4, D, D), F32),
            pltpu.VMEM((Z, Y, 2 * D, D), BF16),
            pltpu.VMEM((2, 4, 2, 2 * D, D), BF16),
            pltpu.VMEM((3, 2 * D, Q), BF16),
            pltpu.VMEM((3, 2 * D, Q), BF16),
            pltpu.VMEM((2 * D, D), BF16),
            pltpu.VMEM((2 * D, D), BF16),
            pltpu.VMEM((3, 8, 8, D), F32),
            pltpu.VMEM((3, 8, D), F32),
            pltpu.SemaphoreType.DMA((count,)),
            pltpu.SemaphoreType.DMA((count,)),
            pltpu.SemaphoreType.DMA((3, 8)),
            pltpu.SemaphoreType.DMA((3, 8)),
        ],
        compiler_params=pltpu.CompilerParams(
            collective_id=0, has_side_effects=True, vmem_limit_bytes=60 * 1024 * 1024
        ),
    )(
        query_raw, key_before_norm, values, grads,
        q_gain.reshape(1, D), k_gain.reshape(1, D), tok_pos.reshape(1, D), frequency,
    )
    return dq, dk, dv, gains[0], gains[1]


def solution(mesh):
    split = P("ctx", "head")
    return jax.shard_map(
        functools.partial(shards, mesh.shape["head"]),
        mesh=mesh,
        in_specs=(split, split, split, split, P(), P(), P("ctx")),
        out_specs=(split, split, split, P(), P()),
        check_vma=False,
    )
```

```python
import functools

import jax
import jax.numpy as jnp
import numpy as np
from jax import lax
from jax.experimental import pallas as pl
from jax.experimental.pallas import tpu as pltpu
from jax.sharding import PartitionSpec as P

D = 128
HALF = 64
X, Y, Z = 4, 2, 8
HEADS = 8
Q = HEADS * HALF
EPS = 1e-06
BASE = 1000000.0
SCALE = D ** (-0.5)
LOG2E = 1.4426950408889634
KROWS = 144
F32, BF16 = jnp.float32, jnp.bfloat16
NT = (((1,), (1,)), ((), ()))
NN = (((1,), (0,)), ((), ()))
TN = (((0,), (0,)), ((), ()))


def dot(a, b, dims):
    return lax.dot_general(a, b, dims, preferred_element_type=F32)


def message_table():
    names = ["Y", "QR", "QL", "GR", "GL", "Q2", "G2"]
    for way in "RL":
        for step in (1, 2, 3):
            names += [f"Z{way}{step}{r}" for r in (0, 1)]
        names.append(f"Z{way}4{0 if way == 'R' else 1}")
        names.append(f"S{way}1{0 if way == 'R' else 1}")
        for step in (2, 3, 4):
            names += [f"S{way}{step}{r}" for r in (0, 1)]
    for j in range(4):
        names += [f"ST{j}{m}" for m in (1, 2, 3)]
    names += ["DQ1", "DQ2", "DQ3", "SY"]
    return {name: index for index, name in enumerate(names)}


MSG = message_table()


class Part:
    def __init__(self, ref, index=None):
        self.ref, self.index = ref, index

    def make(self):
        return self.ref if self.index is None else self.ref.at[self.index]

    @property
    def at(self):
        return Maker(self.ref)

    def __getitem__(self, index):
        return self.make()[index]

    def __setitem__(self, index, value):
        self.make()[index] = value


class Maker:
    def __init__(self, ref):
        self.ref = ref

    def __getitem__(self, index):
        return Part(self.ref, index)


def rel_of(j):
    return j + (j // 2) * (5 - 2 * j)


def body(
    heads_axis, q_ref, k_ref, v_ref, g_ref, qg_ref, kg_ref, pos_ref, freq_ref,
    dq_ref, dk_ref, dv_ref, gain_ref,
    cos_ref, sin_ref, kv, qc, gc, e_a, g_a, e_b, g_b, e_d, g_d, sums, stbuf, stats, dqacc, dkacc, dvacc, ct_ref, st_ref, qcos, qsin, freq_col,
    dkv, ring, dqs, dqr, ysend, yrecv, gbuf, gsum,
    ssem, rsem, gssem, grsem,
):
    kv, qc, gc, stbuf, dkv, ring, dqs, dqr, ysend, yrecv = (
        Part(ref) for ref in (kv, qc, gc, stbuf, dkv, ring, dqs, dqr, ysend, yrecv)
    )
    ctx = lax.axis_index("ctx")
    head = lax.axis_index("head")
    z, x, y = ctx // (X * Y), (ctx // Y) % X, ctx % Y
    w = ctx % (X * Y)
    ys = (y, 1 - y)

    zpos = [lax.rem(z + off, Z) for off in range(Z)]
    xpos = [lax.rem(x + off, X) for off in range(X)]

    def zm(off):
        return zpos[off % Z]

    def xm(off):
        return xpos[off % X]

    def dev(zz, xx, yy):
        return ((zz * X + xx) * Y + yy, head)

    groups = (
        (z, Z, lambda j: (lax.rem(z + j, Z) * (X * Y) + w, head)),
        (w, X * Y, lambda j: (z * (X * Y) + lax.rem(w + j, X * Y), head)),
        (head, heads_axis, lambda j: (ctx, lax.rem(head + j, heads_axis))),
    )
    all_peers = [peer(j) for _, size, peer in groups for j in range(1, size)]

    barrier = pltpu.get_barrier_semaphore()
    for peer in all_peers:
        pl.semaphore_signal(barrier, inc=1, device_id=peer, device_id_type=pl.DeviceIdType.MESH)

    started = []

    def copy(name, src, dst, to):
        i = MSG[name]
        return pltpu.make_async_remote_copy(
            src_ref=src.make(), dst_ref=dst.make(), send_sem=ssem.at[i], recv_sem=rsem.at[i],
            device_id=to, device_id_type=pl.DeviceIdType.MESH,
        )

    def send(name, src, dst, to):
        copy(name, src, dst, to).start()
        started.append((name, src, dst, to))

    def arrived(name, dst):
        copy(name, dst, dst, (ctx, head)).wait_recv()

    xdev = [dev(z, xpos[m], y) for m in range(X)]
    right_x, left_x = dev(z, xm(1), y), dev(z, xm(-1), y)
    partner = dev(z, x, ys[1])
    side = {"R": (dev(zm(1), x, y), -1), "L": (dev(zm(-1), x, y), 1)}
    last = {"R": 0, "L": 1}

    positions = jnp.broadcast_to(pos_ref[...].astype(F32), (8, D))
    in_first = lax.broadcasted_iota(jnp.int32, (8, D), 1) < HALF
    first_top = jnp.max(jnp.where(in_first, positions, -1.0), axis=1, keepdims=True)
    second_top = jnp.max(jnp.where(in_first, -1.0, positions), axis=1, keepdims=True)
    swapped = jnp.broadcast_to(first_top > second_top, (8, D))[0:1]
    lowest = jnp.min(positions, axis=1, keepdims=True)
    p_me = jnp.broadcast_to(jnp.floor(lowest * (1.0 / HALF)), (8, D))
    p_rows = jnp.concatenate([p_me, p_me], axis=0).astype(BF16)

    def halves(v):
        first, second = v[:HALF], v[HALF:]
        return jnp.where(swapped, second, first), jnp.where(swapped, first, second)

    def rope(v):
        return v * cos_ref[...] + pltpu.roll(v, HALF, 1) * sin_ref[...]

    def unrope(v):
        return v * cos_ref[...] - pltpu.roll(v, HALF, 1) * sin_ref[...]

    def normed(v):
        inverse = lax.rsqrt(jnp.mean(v * v, axis=-1, keepdims=True) + EPS)
        return v * inverse, inverse

    for h in range(HEADS):
        rows = slice(h * HALF, (h + 1) * HALF)
        lo, hi = halves(g_ref[:, h * D:(h + 1) * D].astype(F32))
        gc[x, rows, 0:D] = lo.astype(BF16)
        gc[x, rows, D:] = hi.astype(BF16)

    pl.semaphore_wait(barrier, len(all_peers))

    send("GL", gc.at[x], gc.at[x], left_x)
    send("GR", gc.at[x], gc.at[x], right_x)

    angles = jnp.transpose(jnp.broadcast_to(positions[0:1], (D, D))) * freq_ref[...]
    cos_ref[...] = jnp.cos(angles)
    turn = jnp.sin(angles)
    sin_ref[...] = jnp.where(lax.broadcasted_iota(jnp.int32, (D, D), 1) < HALF, -turn, turn)

    kn, _ = normed(k_ref[...].astype(F32))
    k_lo, k_hi = halves(rope(kn * kg_ref[...]))
    v_lo, v_hi = halves(v_ref[...].astype(F32))
    kv[z, y, 0:HALF] = k_lo.astype(BF16)
    kv[z, y, HALF:D] = k_hi.astype(BF16)
    kv[z, y, D:KROWS] = p_rows
    kv[z, y, KROWS:KROWS + HALF] = v_lo.astype(BF16)
    kv[z, y, KROWS + HALF:KROWS + D] = v_hi.astype(BF16)
    send("Y", kv.at[z, y], kv.at[z, y], partner)
    for way in "RL":
        send(f"Z{way}10", kv.at[z, y], kv.at[z, y], side[way][0])

    for h in range(HEADS):
        rows = slice(h * HALF, (h + 1) * HALF)
        qn, _ = normed(q_ref[:, h * D:(h + 1) * D].astype(F32))
        lo, hi = halves(rope(qn * qg_ref[...]))
        qc[x, rows, 0:D] = lo.astype(BF16)
        qc[x, rows, D:] = hi.astype(BF16)
    qc[x, Q:, 0:D] = p_rows
    qc[x, Q:, D:] = p_rows
    send("QR", qc.at[x], qc.at[x], right_x)
    send("QL", qc.at[x], qc.at[x], left_x)

    zero = jnp.zeros((HALF, D), BF16)

    def diagonal(lo, hi):
        return jnp.concatenate(
            [jnp.concatenate([lo, zero], axis=1), jnp.concatenate([zero, hi], axis=1)], axis=0
        )

    def own_k():
        return diagonal(kv[z, y, 0:HALF], kv[z, y, HALF:D])

    scores = dot(own_k(), qc[x, 0:Q], NT)
    key_row = lax.broadcasted_iota(jnp.int32, (D, Q), 0) % HALF
    query_lane = lax.broadcasted_iota(jnp.int32, (D, Q), 1) % HALF
    exps = jnp.where(key_row <= query_lane, jnp.exp2(scores * (SCALE * LOG2E)), 0.0)
    own_v = diagonal(kv[z, y, KROWS:KROWS + HALF], kv[z, y, KROWS + HALF:KROWS + D])
    probs_grad = dot(own_v, gc[x], NT)
    e_d[...] = exps
    g_d[...] = probs_grad
    both = exps * probs_grad
    for j in (1, 2, 3):
        sums[j] = jnp.zeros((4, 8, Q), F32)
    for part in range(2):
        rows = slice(part * HALF, (part + 1) * HALF)
        sums[0, part] = exps[rows].reshape(8, 8, Q).sum(0)
        sums[0, 2 + part] = both[rows].reshape(8, 8, Q).sum(0)

    def kv_progress(r, d):
        for way in "RL":
            to, sign = side[way]
            if d == 4 and r != last[way]:
                continue
            block = kv.at[zm(sign * d), ys[r]]
            arrived(f"Z{way}{d}{r}", block)
            if d < 3 or (d == 3 and r == last[way]):
                send(f"Z{way}{d + 1}{r}", block, block, to)

    def y_progress():
        arrived("Y", kv.at[z, ys[1]])
        for way in "RL":
            send(f"Z{way}11", kv.at[z, ys[1]], kv.at[z, ys[1]], side[way][0])

    def gradient_forward():
        arrived("GL", gc.at[xm(1)])
        send("G2", gc.at[xm(1)], gc.at[xm(1)], left_x)

    def query_forward():
        arrived("QR", qc.at[xm(-1)])
        send("Q2", qc.at[xm(-1)], qc.at[xm(-1)], right_x)

    def far_queries():
        arrived("Q2", qc.at[xm(2)])
        arrived("G2", gc.at[xm(2)])

    def key_event(r, d):
        return lambda: kv_progress(r, d)

    events = {
        0: (key_event(0, 1), y_progress, key_event(0, 2), gradient_forward, key_event(1, 1)),
        1: (
            key_event(0, 3), key_event(1, 2), query_forward,
            lambda: arrived("QL", qc.at[xm(1)]),
        ),
        2: (lambda: arrived("GR", gc.at[xm(-1)]),),
        3: (key_event(0, 4),),
        6: (key_event(1, 3),),
        9: (key_event(1, 4),),
        12: (far_queries,),
    }

    def block_rows(k, first, count):
        near = lax.rem(z + k, Z)
        far = lax.rem(z + (Z - 1) - k, Z)
        return jnp.concatenate(
            [kv[near, :, first:first + count, :], kv[far, :, first:first + count, :]], axis=0
        )

    def block_masks(k, b):
        pj = block_rows(k, D, 16).astype(F32)[:, 0:8, :]
        pq = qc[b, Q:, 0:D].astype(F32)[None, 0:8]
        early = jnp.where(pj < pq, 1.0, 0.0)
        other = jnp.where(pj == pq, 0.0, 1.0)
        return early, other

    def wide(v):
        return jnp.concatenate([v, v, v, v], axis=-1)

    def joined(lo, hi, early):
        e = early[:, 0:1, :].astype(BF16)
        return jnp.concatenate([lo * e, hi * (1.0 - e).astype(BF16)], axis=-1).reshape(4 * HALF, 2 * D)

    def pass_one(k, j, b, u):
        early, other = block_masks(k, b)
        klo, khi = block_rows(k, 0, HALF), block_rows(k, HALF, HALF)
        vlo, vhi = block_rows(k, KROWS, HALF), block_rows(k, KROWS + HALF, HALF)
        ex = jnp.exp2(dot(klo.reshape(4 * HALF, D), qc[b, 0:Q, D:], NT) * (SCALE * LOG2E))
        gp = dot(vlo.reshape(4 * HALF, D), gc[b, :, D:], NT)
        e_a[u] = ex
        g_a[u] = gp
        sums[j, 1] += ex.reshape(32, 8, Q).sum(0)
        sums[j, 3] += (ex * gp).reshape(32, 8, Q).sum(0)
        ex = jnp.exp2(dot(joined(klo, khi, early), qc[b, 0:Q], NT) * (SCALE * LOG2E))
        ex = ex.reshape(4, HALF, Q) * wide(other[:, 0:1, :])
        gp = dot(joined(vlo, vhi, early), gc[b], NT).reshape(4, HALF, Q)
        e_b[u] = ex.reshape(4 * HALF, Q)
        g_b[u] = gp.reshape(4 * HALF, Q)
        part = ex.reshape(4, 8, 8, Q).sum(1)
        partg = (ex * gp).reshape(4, 8, 8, Q).sum(1)
        ew = wide(early)
        sums[j, 0] += (part * ew).sum(0)
        sums[j, 1] += (part * (1.0 - ew)).sum(0)
        sums[j, 2] += (partg * ew).sum(0)
        sums[j, 3] += (partg * (1.0 - ew)).sum(0)

    def statistics_out(j):
        b = xm(rel_of(j))
        slot = stbuf.at[b, x]
        slot[...] = jnp.concatenate(
            [jnp.sum(sums[j], axis=1), jnp.zeros((4, Q), F32)], axis=0
        )
        for m in (1, 2, 3):
            send(f"ST{j}{m}", slot, slot, xdev[m])

    def first_loop(i, carry):
        far = i // 12
        k = (1 - far) * (i // 3) + far * (i - 12)
        j = (1 - far) * (i % 3) + far * 3
        for case, steps in events.items():
            @pl.when(i == case)
            def _(steps=steps):
                for step in steps:
                    step()
        rel = rel_of(j)
        pass_one(k, j, lax.rem(x + rel, X), k * 4 + rel)
        for case, done in ((9, 0), (10, 1), (11, 2), (15, 3)):
            @pl.when(i == case)
            def _(done=done):
                statistics_out(done)
        return carry

    lax.fori_loop(0, 16, first_loop, 0)

    token_row = (lax.broadcasted_iota(jnp.int32, (D, D), 0) % HALF).astype(F32)
    twice = token_row * (2.0 * freq_ref[...])
    ct_ref[...] = jnp.cos(twice)
    st_ref[...] = jnp.sin(twice)
    freq_col[...] = jnp.transpose(jnp.broadcast_to(freq_ref[...], (D, D)))[0:HALF]
    token_lane = (lax.broadcasted_iota(jnp.int32, (HALF, D), 1) % HALF).astype(F32)

    def query_tables(rel, carry):
        early_run = jnp.max(qc[lax.rem(x + rel, X), Q:, 0:D].astype(F32), axis=0, keepdims=True)
        for part in range(2):
            run = early_run if part == 0 else (2 * X * Y * Z - 1) - early_run
            angle = (run * HALF + token_lane) * (2.0 * freq_col[...])
            qcos[rel, part] = jnp.cos(angle)
            qsin[rel, part] = jnp.sin(angle)
        return carry

    lax.fori_loop(0, X, query_tables, 0)

    for j in range(4):
        for m in (1, 2, 3):
            arrived(f"ST{j}{m}", stbuf.at[xm(rel_of(j) - m), xm(-m)])
    for b in range(4):
        total = stbuf[b, 0]
        for s in range(1, 4):
            total = total + stbuf[b, s]
        inv = 1.0 / total[0:2]
        stats[b] = jnp.concatenate([inv, total[2:4] * inv, jnp.zeros((4, Q), F32)], axis=0)

    rowsel = lax.broadcasted_iota(jnp.int32, (D, Q), 0) < HALF
    pr = e_d[...] * jnp.where(rowsel, stats[x, 0:1], stats[x, 1:2])
    gs = (pr * (g_d[...] - jnp.where(rowsel, stats[x, 2:3], stats[x, 3:4]))).astype(BF16)
    pr = pr.astype(BF16)
    top = lax.broadcasted_iota(jnp.int32, (D, D), 0) < HALF
    for k in range(4):
        dkacc[k] = jnp.zeros((4, D, D), F32)
        dvacc[k] = jnp.zeros((4, D, D), F32)
    full = dot(pr, gc[x], NN)
    dvacc[0, y] = jnp.where(top, full[:, 0:D], full[:, D:])
    full = dot(gs, qc[x, 0:Q], NN)
    dkacc[0, y] = jnp.where(top, full[:, 0:D], full[:, D:])
    for m in (1, 2, 3):
        dqacc[m] = jnp.zeros((2 * D, Q), F32)
    dqacc[0] = dot(own_k(), gs, TN)

    def pass_two(k, b, rel, u):
        early, _ = block_masks(k, b)
        klo, khi = block_rows(k, 0, HALF), block_rows(k, HALF, HALF)
        pr = e_a[u] * stats[b, 1:2]
        gs = (pr * (g_a[u] - stats[b, 3:4])).astype(BF16)
        pr = pr.astype(BF16)
        dva = dot(pr, gc[b, :, D:], NN).reshape(4, HALF, D)
        dka = dot(gs, qc[b, 0:Q, D:], NN).reshape(4, HALF, D)
        dqacc[rel, D:, :] += dot(klo.reshape(4 * HALF, D), gs, TN)
        ew = wide(early[:, 0:1, :]) > 0.5
        invb = jnp.where(ew, stats[b, 0:1][None], stats[b, 1:2][None])
        delb = jnp.where(ew, stats[b, 2:3][None], stats[b, 3:4][None])
        pr = e_b[u].reshape(4, HALF, Q) * invb
        gs = (pr * (g_b[u].reshape(4, HALF, Q) - delb)).astype(BF16).reshape(4 * HALF, Q)
        pr = pr.astype(BF16).reshape(4 * HALF, Q)
        dvc = dot(pr, gc[b], NN).reshape(4, HALF, 2 * D)
        dkc = dot(gs, qc[b, 0:Q], NN).reshape(4, HALF, 2 * D)
        dqacc[rel] += dot(joined(klo, khi, early), gs, TN)
        e1 = early[:, 0:1, :]
        dkacc[k, :, 0:HALF] += dka + dkc[..., 0:D] * e1
        dkacc[k, :, HALF:] += dkc[..., D:] * (1.0 - e1)
        dvacc[k, :, 0:HALF] += dva + dvc[..., 0:D] * e1
        dvacc[k, :, HALF:] += dvc[..., D:] * (1.0 - e1)

    def reduce_step(k):
        for place, zz in enumerate((zm(k), zm(-k - 1))):
            if zz is zpos[0]:
                continue
            rows = slice(2 * place, 2 * place + 2)
            dkv[zz, :, 0:D, :] = (dkacc[k, rows] * SCALE).astype(BF16)
            dkv[zz, :, D:, :] = dvacc[k, rows].astype(BF16)
        if k == 3:
            for wi, way in enumerate("RL"):
                r = last[way]
                send(f"S{way}1{r}", dkv.at[zm(4), ys[r]], ring.at[wi, 0, r], side[way][0])
            return
        off = k + 1
        step = 4 - off
        for r in (0, 1):
            for wi, way in enumerate("RL"):
                zz = zm(off if way == "R" else -off)
                part = dkv.at[zz, ys[r]]
                if step > 1 or r == last[way]:
                    came = ring.at[wi, step - 1, r]
                    arrived(f"S{way}{step}{r}", came)
                    part[...] = (part[...].astype(F32) + came[...].astype(F32)).astype(BF16)
                send(f"S{way}{step + 1}{r}", part, ring.at[wi, step, r], side[way][0])


    def queries_out(m):
        dqs[m - 1] = dqacc[m].astype(BF16)
        send(f"DQ{m}", dqs.at[m - 1], dqr.at[m - 1], xdev[m])

    def second_loop(i, carry):
        near = (i + 12) // 16
        k = (1 - near) * (3 - i) + near * (3 - (i + 8) // 3 + 4)
        j = (1 - near) * 3 + near * (2 - (i + 8) % 3)
        rel = rel_of(j)
        pass_two(k, lax.rem(x + rel, X), rel, k * 4 + rel)
        for case, m in ((3, 2), (13, 3), (14, 1)):
            @pl.when(i == case)
            def _(m=m):
                queries_out(m)
        for case in range(4):
            @pl.when(i == 3 * case + 6)
            def _(case=case):
                reduce_step(3 - case)
        return carry

    lax.fori_loop(0, 16, second_loop, 0)

    first_lanes = lax.broadcasted_iota(jnp.int32, (1, D), 1) < HALF

    def key_share(k, carry):
        plain, cosined, sined = carry
        grad = dkacc[k].reshape(4 * D, D)
        rot = block_rows(k, 0, D).astype(F32).reshape(4 * D, D)
        straight = (grad * rot).reshape(4, 2, HALF, D)
        crossed = (grad * pltpu.roll(rot, HALF, 1)).reshape(4, 2, HALF, D)
        ct, st = ct_ref[0:HALF], st_ref[0:HALF]
        early_run = block_rows(k, D, 16).astype(F32)[:, 0:1, :]
        late_run = (2 * X * Y * Z - 1) - early_run
        run = jnp.concatenate([early_run[:, None], late_run[:, None]], axis=1)
        angle = run * (2.0 * HALF * freq_ref[...])
        cp, sp = jnp.cos(angle), jnp.sin(angle)

        def over_tokens(v):
            return jnp.sum(v, axis=2, keepdims=True)

        plain = plain + jnp.sum(over_tokens(straight), axis=(0, 1))
        cosined = cosined + jnp.sum(
            cp * over_tokens(straight * ct) - sp * over_tokens(straight * st), axis=(0, 1)
        )
        sined = sined + jnp.sum(
            sp * over_tokens(crossed * ct) + cp * over_tokens(crossed * st), axis=(0, 1)
        )
        return plain, cosined, sined

    none = jnp.zeros((1, D), F32)
    plain, cosined, sined = lax.fori_loop(0, 4, key_share, (none, none, none))

    def swap_lanes(v):
        return pltpu.roll(jnp.broadcast_to(v, (8, D)), HALF, 1)[0:1]

    both_sines = sined + swap_lanes(sined)
    key_gain = plain + swap_lanes(plain) + cosined - swap_lanes(cosined)
    key_gain = key_gain + jnp.where(first_lanes, both_sines, -both_sines)
    key_gain = key_gain * (0.5 * SCALE) / kg_ref[...]

    row_id = lax.broadcasted_iota(jnp.int32, (2 * D, 2 * D), 0)
    lane_id = lax.broadcasted_iota(jnp.int32, (2 * D, 2 * D), 1)
    identity = jnp.where(row_id == lane_id, 1.0, 0.0).astype(BF16)

    def over_heads(v):
        return v[:, 0:D] + v[:, D:2 * D] + v[:, 2 * D:3 * D] + v[:, 3 * D:]

    def query_share(rel, carry):
        plain, turned = carry
        rot = dot(identity, qc[lax.rem(x + rel, X), 0:Q], NT)
        grad = dqacc[rel]
        for part in range(2):
            a, b = grad[part * D:part * D + HALF], grad[part * D + HALF:part * D + D]
            e, f = rot[part * D:part * D + HALF], rot[part * D + HALF:part * D + D]
            ae, bf = over_heads(a * e), over_heads(b * f)
            plain = plain + ae + bf
            turned = turned + qcos[rel, part] * (ae - bf) + qsin[rel, part] * over_heads(a * f + b * e)
        return plain, turned

    none = jnp.zeros((HALF, D), F32)
    plain, turned = lax.fori_loop(0, X, query_share, (none, none))
    query_gain = jnp.transpose(jnp.concatenate([plain + turned, plain - turned], axis=0))
    query_gain = jnp.sum(query_gain, axis=0, keepdims=True) * (0.5 * SCALE) / qg_ref[...]

    def gain_copies(stage):
        me, size, peer = groups[stage]
        return [
            pltpu.make_async_remote_copy(
                src_ref=gsum.at[stage], dst_ref=gbuf.at[stage, me],
                send_sem=gssem.at[stage, j], recv_sem=grsem.at[stage, j],
                device_id=peer(j), device_id_type=pl.DeviceIdType.MESH,
            )
            for j in range(1, size)
        ]

    def gain_start(stage, mine):
        gsum[stage] = mine
        gbuf[stage, groups[stage][0]] = mine
        copies = gain_copies(stage)
        for c in copies:
            c.start()
        return copies

    def gain_finish(stage, copies):
        for c in copies:
            c.wait()
        total = gbuf[stage, 0]
        for j in range(1, groups[stage][1]):
            total = total + gbuf[stage, j]
        return total

    copies = gain_start(0, jnp.concatenate([query_gain, key_gain, jnp.zeros((6, D), F32)], axis=0))

    def own_sum(r):
        total = jnp.concatenate([dkacc[0, ys[r]] * SCALE, dvacc[0, ys[r]]], axis=0)
        for wi in (0, 1):
            total = total + ring[wi, 3, r].astype(F32)
        return total

    for r in (1, 0):
        for way in "RL":
            wi = 0 if way == "R" else 1
            arrived(f"S{way}4{r}", ring.at[wi, 3, r])
        if r == 1:
            ysend[...] = own_sum(1).astype(BF16)
            send("SY", ysend, yrecv, partner)

    copies = gain_start(1, gain_finish(0, copies))

    def stored(lo, hi):
        return jnp.concatenate(
            [jnp.where(swapped, hi, lo), jnp.where(swapped, lo, hi)], axis=0
        )

    def norm_back(g, xn, inverse, gain):
        s = g * gain
        return inverse * (s - xn * jnp.mean(s * xn, axis=-1, keepdims=True))

    whole = dqacc[0]
    for m in (1, 2, 3):
        arrived(f"DQ{m}", dqr.at[m - 1])
        whole = whole + dqr[m - 1].astype(F32)
    turned = jnp.transpose(whole) * SCALE
    for h in range(HEADS):
        cols = slice(h * D, (h + 1) * D)
        rows = slice(h * HALF, (h + 1) * HALF)
        gq = unrope(stored(turned[rows, 0:D], turned[rows, D:]))
        qn, inverse = normed(q_ref[:, cols].astype(F32))
        dq_ref[:, cols] = norm_back(gq, qn, inverse, qg_ref[...]).astype(BF16)

    copies = gain_start(2, gain_finish(1, copies))

    arrived("SY", yrecv)
    own = own_sum(0) + yrecv[...].astype(F32)
    gk = unrope(stored(own[:HALF], own[HALF:D]))
    kn, inverse = normed(k_ref[...].astype(F32))
    dk_ref[...] = norm_back(gk, kn, inverse, kg_ref[...]).astype(BF16)
    dv_ref[...] = stored(own[D:D + HALF], own[D + HALF:]).astype(BF16)

    gain_ref[...] = gain_finish(2, copies)

    for name, src, dst, to in started:
        copy(name, src, dst, to).wait_send()


def shards(heads_axis, query_raw, key_before_norm, values, grads, q_gain, k_gain, tok_pos):
    frequency = np.power(np.float32(BASE), -(np.arange(HALF, dtype=np.float32) * np.float32(2.0 / D)))
    frequency = jnp.asarray(np.tile(frequency.astype(np.float32), 2).reshape(1, D))
    vmem = pl.BlockSpec(memory_space=pltpu.VMEM)
    count = len(MSG)
    dq, dk, dv, gains = pl.pallas_call(
        functools.partial(body, heads_axis),
        out_shape=(
            jax.ShapeDtypeStruct((D, HEADS * D), BF16),
            jax.ShapeDtypeStruct((D, D), BF16),
            jax.ShapeDtypeStruct((D, D), BF16),
            jax.ShapeDtypeStruct((8, D), F32),
        ),
        in_specs=[vmem] * 8,
        out_specs=(vmem,) * 4,
        scratch_shapes=[
            pltpu.VMEM((D, D), F32),
            pltpu.VMEM((D, D), F32),
            pltpu.VMEM((Z, Y, KROWS + D, D), BF16),
            pltpu.VMEM((X, Q + 16, 2 * D), BF16),
            pltpu.VMEM((X, Q, 2 * D), BF16),
            pltpu.VMEM((16, 4 * HALF, Q), F32),
            pltpu.VMEM((16, 4 * HALF, Q), F32),
            pltpu.VMEM((16, 4 * HALF, Q), F32),
            pltpu.VMEM((16, 4 * HALF, Q), F32),
            pltpu.VMEM((D, Q), F32),
            pltpu.VMEM((D, Q), F32),
            pltpu.VMEM((4, 4, 8, Q), F32),
            pltpu.VMEM((X, X, 8, Q), F32),
            pltpu.VMEM((X, 8, Q), F32),
            pltpu.VMEM((X, 2 * D, Q), F32),
            pltpu.VMEM((4, 4, D, D), F32),
            pltpu.VMEM((4, 4, D, D), F32),
            pltpu.VMEM((D, D), F32),
            pltpu.VMEM((D, D), F32),
            pltpu.VMEM((X, 2, HALF, D), F32),
            pltpu.VMEM((X, 2, HALF, D), F32),
            pltpu.VMEM((HALF, D), F32),
            pltpu.VMEM((Z, Y, 2 * D, D), BF16),
            pltpu.VMEM((2, 4, 2, 2 * D, D), BF16),
            pltpu.VMEM((3, 2 * D, Q), BF16),
            pltpu.VMEM((3, 2 * D, Q), BF16),
            pltpu.VMEM((2 * D, D), BF16),
            pltpu.VMEM((2 * D, D), BF16),
            pltpu.VMEM((3, 8, 8, D), F32),
            pltpu.VMEM((3, 8, D), F32),
            pltpu.SemaphoreType.DMA((count,)),
            pltpu.SemaphoreType.DMA((count,)),
            pltpu.SemaphoreType.DMA((3, 8)),
            pltpu.SemaphoreType.DMA((3, 8)),
        ],
        compiler_params=pltpu.CompilerParams(
            collective_id=0, has_side_effects=True, vmem_limit_bytes=60 * 1024 * 1024
        ),
    )(
        query_raw, key_before_norm, values, grads,
        q_gain.reshape(1, D), k_gain.reshape(1, D), tok_pos.reshape(1, D), frequency,
    )
    return dq, dk, dv, gains[0], gains[1]


def solution(mesh):
    split = P("ctx", "head")
    return jax.shard_map(
        functools.partial(shards, mesh.shape["head"]),
        mesh=mesh,
        in_specs=(split, split, split, split, P(), P(), P("ctx")),
        out_specs=(split, split, split, P(), P()),
        check_vma=False,
    )
```

```python
import functools

import jax
import jax.numpy as jnp
import numpy as np
from jax import lax
from jax.experimental import pallas as pl
from jax.experimental.pallas import tpu as pltpu
from jax.sharding import PartitionSpec as P

D = 128
HALF = 64
X, Y, Z = 4, 2, 8
HEADS = 8
Q = HEADS * HALF
EPS = 1e-06
BASE = 1000000.0
SCALE = D ** (-0.5)
LOG2E = 1.4426950408889634
KROWS = 144
F32, BF16 = jnp.float32, jnp.bfloat16
NT = (((1,), (1,)), ((), ()))
NN = (((1,), (0,)), ((), ()))
TN = (((0,), (0,)), ((), ()))


def dot(a, b, dims):
    return lax.dot_general(a, b, dims, preferred_element_type=F32)


def message_table():
    names = ["Y0", "Y1", "QR", "QL", "GR", "GL", "Q2", "G2"]
    for way in "RL":
        for step in (1, 2, 3):
            names += [f"Z{way}{step}{r}{h}" for r in (0, 1) for h in (0, 1)]
        names += [f"Z{way}4{0 if way == 'R' else 1}{h}" for h in (0, 1)]
        names.append(f"S{way}1{0 if way == 'R' else 1}")
        for step in (2, 3, 4):
            names += [f"S{way}{step}{r}" for r in (0, 1)]
    for j in range(4):
        names += [f"ST{j}{m}" for m in (1, 2, 3)]
    names += ["DQ1", "DQ2", "DQ3", "SY"]
    return {name: index for index, name in enumerate(names)}


MSG = message_table()


class Part:
    def __init__(self, ref, index=None):
        self.ref, self.index = ref, index

    def make(self):
        return self.ref if self.index is None else self.ref.at[self.index]

    @property
    def at(self):
        return Maker(self.ref)

    def __getitem__(self, index):
        return self.make()[index]

    def __setitem__(self, index, value):
        self.make()[index] = value


class Maker:
    def __init__(self, ref):
        self.ref = ref

    def __getitem__(self, index):
        return Part(self.ref, index)


def rel_of(j):
    return j + (j // 2) * (5 - 2 * j)


def body(
    heads_axis, q_ref, k_ref, v_ref, g_ref, qg_ref, kg_ref, pos_ref, freq_ref,
    dq_ref, dk_ref, dv_ref, qgain_ref, kgain_ref,
    cos_ref, sin_ref, kv, qc, gc, e_a, g_a, e_b, g_b, e_d, g_d, sums, stbuf, stats, dqacc, dkacc, dvacc, ct_ref, st_ref, qcos, qsin, freq_col,
    dkv, ring, dqs, dqr, ysend, yrecv, gbuf, gsum,
    ssem, rsem, gssem, grsem,
):
    kv, qc, gc, stbuf, dkv, ring, dqs, dqr, ysend, yrecv = (
        Part(ref) for ref in (kv, qc, gc, stbuf, dkv, ring, dqs, dqr, ysend, yrecv)
    )
    ctx = lax.axis_index("ctx")
    head = lax.axis_index("head")
    z, x, y = ctx // (X * Y), (ctx // Y) % X, ctx % Y
    w = ctx % (X * Y)
    ys = (y, 1 - y)

    zpos = [lax.rem(z + off, Z) for off in range(Z)]
    xpos = [lax.rem(x + off, X) for off in range(X)]

    def zm(off):
        return zpos[off % Z]

    def xm(off):
        return xpos[off % X]

    def dev(zz, xx, yy):
        return ((zz * X + xx) * Y + yy, head)

    groups = (
        (z, Z, lambda j: (lax.rem(z + j, Z) * (X * Y) + w, head)),
        (w, X * Y, lambda j: (z * (X * Y) + lax.rem(w + j, X * Y), head)),
        (head, heads_axis, lambda j: (ctx, lax.rem(head + j, heads_axis))),
    )
    all_peers = [peer(j) for _, size, peer in groups for j in range(1, size)]

    barrier = pltpu.get_barrier_semaphore()
    for peer in all_peers:
        pl.semaphore_signal(barrier, inc=1, device_id=peer, device_id_type=pl.DeviceIdType.MESH)

    started = []

    def copy(name, src, dst, to):
        i = MSG[name]
        return pltpu.make_async_remote_copy(
            src_ref=src.make(), dst_ref=dst.make(), send_sem=ssem.at[i], recv_sem=rsem.at[i],
            device_id=to, device_id_type=pl.DeviceIdType.MESH,
        )

    def send(name, src, dst, to):
        copy(name, src, dst, to).start()
        started.append((name, src, dst, to))

    def arrived(name, dst):
        copy(name, dst, dst, (ctx, head)).wait_recv()

    xdev = [dev(z, xpos[m], y) for m in range(X)]
    right_x, left_x = dev(z, xm(1), y), dev(z, xm(-1), y)
    partner = dev(z, x, ys[1])
    side = {"R": (dev(zm(1), x, y), -1), "L": (dev(zm(-1), x, y), 1)}
    last = {"R": 0, "L": 1}

    positions = jnp.broadcast_to(pos_ref[...].astype(F32), (8, D))
    in_first = lax.broadcasted_iota(jnp.int32, (8, D), 1) < HALF
    first_top = jnp.max(jnp.where(in_first, positions, -1.0), axis=1, keepdims=True)
    second_top = jnp.max(jnp.where(in_first, -1.0, positions), axis=1, keepdims=True)
    swapped = jnp.broadcast_to(first_top > second_top, (8, D))[0:1]
    lowest = jnp.min(positions, axis=1, keepdims=True)
    p_me = jnp.broadcast_to(jnp.floor(lowest * (1.0 / HALF)), (8, D))
    p_rows = jnp.concatenate([p_me, p_me], axis=0).astype(BF16)

    def halves(v):
        first, second = v[:HALF], v[HALF:]
        return jnp.where(swapped, second, first), jnp.where(swapped, first, second)

    def rope(v):
        return v * cos_ref[...] + pltpu.roll(v, HALF, 1) * sin_ref[...]

    def unrope(v):
        return v * cos_ref[...] - pltpu.roll(v, HALF, 1) * sin_ref[...]

    def normed(v):
        inverse = lax.rsqrt(jnp.mean(v * v, axis=-1, keepdims=True) + EPS)
        return v * inverse, inverse


    angles = jnp.transpose(jnp.broadcast_to(positions[0:1], (D, D))) * freq_ref[...]
    cos_ref[...] = jnp.cos(angles)
    turn = jnp.sin(angles)
    sin_ref[...] = jnp.where(lax.broadcasted_iota(jnp.int32, (D, D), 1) < HALF, -turn, turn)

    kn, _ = normed(k_ref[...].astype(F32))
    k_lo, k_hi = halves(rope(kn * kg_ref[...]))
    v_lo, v_hi = halves(v_ref[...].astype(F32))
    kv[z, y, 0:HALF] = k_lo.astype(BF16)
    kv[z, y, HALF:D] = k_hi.astype(BF16)
    kv[z, y, D:KROWS] = p_rows
    kv[z, y, KROWS:KROWS + HALF] = v_lo.astype(BF16)
    kv[z, y, KROWS + HALF:KROWS + D] = v_hi.astype(BF16)
    pl.semaphore_wait(barrier, len(all_peers))

    def kv_part(zz, yy, h):
        return kv.at[zz, yy, pl.ds(0, KROWS) if h == 0 else pl.ds(KROWS, D)]

    for h in (0, 1):
        part = kv_part(z, y, h)
        send(f"Y{h}", part, part, partner)
        for way in "RL":
            send(f"Z{way}10{h}", part, part, side[way][0])

    for h in range(HEADS):
        rows = slice(h * HALF, (h + 1) * HALF)
        lo, hi = halves(g_ref[:, h * D:(h + 1) * D].astype(F32))
        gc[x, rows, 0:D] = lo.astype(BF16)
        gc[x, rows, D:] = hi.astype(BF16)

    send("GL", gc.at[x], gc.at[x], left_x)
    send("GR", gc.at[x], gc.at[x], right_x)

    for h in range(HEADS):
        rows = slice(h * HALF, (h + 1) * HALF)
        qn, _ = normed(q_ref[:, h * D:(h + 1) * D].astype(F32))
        lo, hi = halves(rope(qn * qg_ref[...]))
        qc[x, rows, 0:D] = lo.astype(BF16)
        qc[x, rows, D:] = hi.astype(BF16)
    qc[x, Q:, 0:D] = p_rows
    qc[x, Q:, D:] = p_rows
    send("QR", qc.at[x], qc.at[x], right_x)
    send("QL", qc.at[x], qc.at[x], left_x)

    zero = jnp.zeros((HALF, D), BF16)

    def diagonal(lo, hi):
        return jnp.concatenate(
            [jnp.concatenate([lo, zero], axis=1), jnp.concatenate([zero, hi], axis=1)], axis=0
        )

    def own_k():
        return diagonal(kv[z, y, 0:HALF], kv[z, y, HALF:D])

    scores = dot(own_k(), qc[x, 0:Q], NT)
    key_row = lax.broadcasted_iota(jnp.int32, (D, Q), 0) % HALF
    query_lane = lax.broadcasted_iota(jnp.int32, (D, Q), 1) % HALF
    exps = jnp.where(key_row <= query_lane, jnp.exp2(scores * (SCALE * LOG2E)), 0.0)
    own_v = diagonal(kv[z, y, KROWS:KROWS + HALF], kv[z, y, KROWS + HALF:KROWS + D])
    probs_grad = dot(own_v, gc[x], NT)
    e_d[...] = exps
    g_d[...] = probs_grad
    both = exps * probs_grad
    for j in (1, 2, 3):
        sums[j] = jnp.zeros((4, 8, Q), F32)
    for part in range(2):
        rows = slice(part * HALF, (part + 1) * HALF)
        sums[0, part] = exps[rows].reshape(8, 8, Q).sum(0)
        sums[0, 2 + part] = both[rows].reshape(8, 8, Q).sum(0)

    def kv_progress(r, d):
        for h in (0, 1):
            for way in "RL":
                to, sign = side[way]
                if d == 4 and r != last[way]:
                    continue
                part = kv_part(zm(sign * d), ys[r], h)
                arrived(f"Z{way}{d}{r}{h}", part)
                if d < 3 or (d == 3 and r == last[way]):
                    send(f"Z{way}{d + 1}{r}{h}", part, part, to)

    def y_progress():
        for h in (0, 1):
            part = kv_part(z, ys[1], h)
            arrived(f"Y{h}", part)
            for way in "RL":
                send(f"Z{way}11{h}", part, part, side[way][0])

    def gradient_forward():
        arrived("GL", gc.at[xm(1)])
        send("G2", gc.at[xm(1)], gc.at[xm(1)], left_x)

    def query_forward():
        arrived("QR", qc.at[xm(-1)])
        send("Q2", qc.at[xm(-1)], qc.at[xm(-1)], right_x)

    def far_queries():
        arrived("Q2", qc.at[xm(2)])
        arrived("G2", gc.at[xm(2)])

    def key_event(r, d):
        return lambda: kv_progress(r, d)

    events = {
        0: (key_event(0, 1), y_progress, key_event(0, 2), gradient_forward, key_event(1, 1)),
        1: (
            key_event(0, 3), key_event(1, 2), query_forward,
            lambda: arrived("QL", qc.at[xm(1)]),
        ),
        2: (lambda: arrived("GR", gc.at[xm(-1)]),),
        3: (key_event(0, 4),),
        6: (key_event(1, 3),),
        9: (key_event(1, 4),),
        12: (far_queries,),
    }

    def block_rows(k, first, count):
        near = lax.rem(z + k, Z)
        far = lax.rem(z + (Z - 1) - k, Z)
        return jnp.concatenate(
            [kv[near, :, first:first + count, :], kv[far, :, first:first + count, :]], axis=0
        )

    def block_masks(k, b):
        pj = block_rows(k, D, 16).astype(F32)[:, 0:8, :]
        pq = qc[b, Q:, 0:D].astype(F32)[None, 0:8]
        early = jnp.where(pj < pq, 1.0, 0.0)
        other = jnp.where(pj == pq, 0.0, 1.0)
        return early, other

    def wide(v):
        return jnp.concatenate([v, v, v, v], axis=-1)

    def joined(lo, hi, early):
        e = early[:, 0:1, :].astype(BF16)
        return jnp.concatenate([lo * e, hi * (1.0 - e).astype(BF16)], axis=-1).reshape(4 * HALF, 2 * D)

    def pass_one(k, j, b, u):
        early, other = block_masks(k, b)
        klo, khi = block_rows(k, 0, HALF), block_rows(k, HALF, HALF)
        vlo, vhi = block_rows(k, KROWS, HALF), block_rows(k, KROWS + HALF, HALF)
        ex = jnp.exp2(dot(klo.reshape(4 * HALF, D), qc[b, 0:Q, D:], NT) * (SCALE * LOG2E))
        gp = dot(vlo.reshape(4 * HALF, D), gc[b, :, D:], NT)
        e_a[u] = ex
        g_a[u] = gp
        sums[j, 1] += ex.reshape(32, 8, Q).sum(0)
        sums[j, 3] += (ex * gp).reshape(32, 8, Q).sum(0)
        ex = jnp.exp2(dot(joined(klo, khi, early), qc[b, 0:Q], NT) * (SCALE * LOG2E))
        ex = ex.reshape(4, HALF, Q) * wide(other[:, 0:1, :])
        gp = dot(joined(vlo, vhi, early), gc[b], NT).reshape(4, HALF, Q)
        e_b[u] = ex.reshape(4 * HALF, Q)
        g_b[u] = gp.reshape(4 * HALF, Q)
        part = ex.reshape(4, 8, 8, Q).sum(1)
        partg = (ex * gp).reshape(4, 8, 8, Q).sum(1)
        ew = wide(early)
        sums[j, 0] += (part * ew).sum(0)
        sums[j, 1] += (part * (1.0 - ew)).sum(0)
        sums[j, 2] += (partg * ew).sum(0)
        sums[j, 3] += (partg * (1.0 - ew)).sum(0)

    def statistics_out(j):
        b = xm(rel_of(j))
        slot = stbuf.at[b, x]
        slot[...] = jnp.concatenate(
            [jnp.sum(sums[j], axis=1), jnp.zeros((4, Q), F32)], axis=0
        )
        for m in (1, 2, 3):
            send(f"ST{j}{m}", slot, slot, xdev[m])

    def first_loop(i, carry):
        far = i // 12
        k = (1 - far) * (i // 3) + far * (i - 12)
        j = (1 - far) * (i % 3) + far * 3
        for case, steps in events.items():
            @pl.when(i == case)
            def _(steps=steps):
                for step in steps:
                    step()
        rel = rel_of(j)
        pass_one(k, j, lax.rem(x + rel, X), k * 4 + rel)
        for case, done in ((9, 0), (10, 1), (11, 2), (15, 3)):
            @pl.when(i == case)
            def _(done=done):
                statistics_out(done)
        return carry

    lax.fori_loop(0, 16, first_loop, 0)

    token_row = (lax.broadcasted_iota(jnp.int32, (D, D), 0) % HALF).astype(F32)
    twice = token_row * (2.0 * freq_ref[...])
    ct_ref[...] = jnp.cos(twice)
    st_ref[...] = jnp.sin(twice)
    freq_col[...] = jnp.transpose(jnp.broadcast_to(freq_ref[...], (D, D)))[0:HALF]
    token_lane = (lax.broadcasted_iota(jnp.int32, (HALF, D), 1) % HALF).astype(F32)

    def query_tables(rel, carry):
        early_run = jnp.max(qc[lax.rem(x + rel, X), Q:, 0:D].astype(F32), axis=0, keepdims=True)
        for part in range(2):
            run = early_run if part == 0 else (2 * X * Y * Z - 1) - early_run
            angle = (run * HALF + token_lane) * (2.0 * freq_col[...])
            qcos[rel, part] = jnp.cos(angle)
            qsin[rel, part] = jnp.sin(angle)
        return carry

    lax.fori_loop(0, X, query_tables, 0)

    for j in range(4):
        for m in (1, 2, 3):
            arrived(f"ST{j}{m}", stbuf.at[xm(rel_of(j) - m), xm(-m)])
    for b in range(4):
        total = stbuf[b, 0]
        for s in range(1, 4):
            total = total + stbuf[b, s]
        inv = 1.0 / total[0:2]
        stats[b] = jnp.concatenate([inv, total[2:4] * inv, jnp.zeros((4, Q), F32)], axis=0)

    rowsel = lax.broadcasted_iota(jnp.int32, (D, Q), 0) < HALF
    pr = e_d[...] * jnp.where(rowsel, stats[x, 0:1], stats[x, 1:2])
    gs = (pr * (g_d[...] - jnp.where(rowsel, stats[x, 2:3], stats[x, 3:4]))).astype(BF16)
    pr = pr.astype(BF16)
    top = lax.broadcasted_iota(jnp.int32, (D, D), 0) < HALF
    for k in range(4):
        dkacc[k] = jnp.zeros((4, D, D), F32)
        dvacc[k] = jnp.zeros((4, D, D), F32)
    full = dot(pr, gc[x], NN)
    dvacc[0, y] = jnp.where(top, full[:, 0:D], full[:, D:])
    full = dot(gs, qc[x, 0:Q], NN)
    dkacc[0, y] = jnp.where(top, full[:, 0:D], full[:, D:])
    for m in (1, 2, 3):
        dqacc[m] = jnp.zeros((2 * D, Q), F32)
    dqacc[0] = dot(own_k(), gs, TN)

    def pass_two(k, b, rel, u):
        early, _ = block_masks(k, b)
        klo, khi = block_rows(k, 0, HALF), block_rows(k, HALF, HALF)
        pr = e_a[u] * stats[b, 1:2]
        gs = (pr * (g_a[u] - stats[b, 3:4])).astype(BF16)
        pr = pr.astype(BF16)
        dva = dot(pr, gc[b, :, D:], NN).reshape(4, HALF, D)
        dka = dot(gs, qc[b, 0:Q, D:], NN).reshape(4, HALF, D)
        dqacc[rel, D:, :] += dot(klo.reshape(4 * HALF, D), gs, TN)
        ew = wide(early[:, 0:1, :]) > 0.5
        invb = jnp.where(ew, stats[b, 0:1][None], stats[b, 1:2][None])
        delb = jnp.where(ew, stats[b, 2:3][None], stats[b, 3:4][None])
        pr = e_b[u].reshape(4, HALF, Q) * invb
        gs = (pr * (g_b[u].reshape(4, HALF, Q) - delb)).astype(BF16).reshape(4 * HALF, Q)
        pr = pr.astype(BF16).reshape(4 * HALF, Q)
        dvc = dot(pr, gc[b], NN).reshape(4, HALF, 2 * D)
        dkc = dot(gs, qc[b, 0:Q], NN).reshape(4, HALF, 2 * D)
        dqacc[rel] += dot(joined(klo, khi, early), gs, TN)
        e1 = early[:, 0:1, :]
        dkacc[k, :, 0:HALF] += dka + dkc[..., 0:D] * e1
        dkacc[k, :, HALF:] += dkc[..., D:] * (1.0 - e1)
        dvacc[k, :, 0:HALF] += dva + dvc[..., 0:D] * e1
        dvacc[k, :, HALF:] += dvc[..., D:] * (1.0 - e1)

    def pair_done(k):
        for place, zz in enumerate((zm(k), zm(-k - 1))):
            if zz is zpos[0]:
                continue
            rows = slice(2 * place, 2 * place + 2)
            dkv[zz, :, 0:D, :] = (dkacc[k, rows] * SCALE).astype(BF16)
            dkv[zz, :, D:, :] = dvacc[k, rows].astype(BF16)
        if k == 3:
            for wi, way in enumerate("RL"):
                r = last[way]
                send(f"S{way}1{r}", dkv.at[zm(4), ys[r]], ring.at[wi, 0, r], side[way][0])

    def ring_step(step, r):
        off = 4 - step
        for wi, way in enumerate("RL"):
            part = dkv.at[zm(off if way == "R" else -off), ys[r]]
            if step > 1 or r == last[way]:
                came = ring.at[wi, step - 1, r]
                arrived(f"S{way}{step}{r}", came)
                part[...] = (part[...].astype(F32) + came[...].astype(F32)).astype(BF16)
            send(f"S{way}{step + 1}{r}", part, ring.at[wi, step, r], side[way][0])

    def queries_out(m):
        dqs[m - 1] = dqacc[m].astype(BF16)
        send(f"DQ{m}", dqs.at[m - 1], dqr.at[m - 1], xdev[m])

    def second_loop(i, carry):
        near = (i + 12) // 16
        k = (1 - near) * (3 - i) + near * (3 - (i + 8) // 3 + 4)
        j = (1 - near) * 3 + near * (2 - (i + 8) % 3)
        rel = rel_of(j)
        pass_two(k, lax.rem(x + rel, X), rel, k * 4 + rel)
        for case, m in ((3, 2), (13, 3), (14, 1)):
            @pl.when(i == case)
            def _(m=m):
                queries_out(m)
        for case in range(4):
            @pl.when(i == 3 * case + 6)
            def _(case=case):
                pair_done(3 - case)
                if case == 2:
                    ring_step(1, 1)
                    ring_step(1, 0)
        return carry

    lax.fori_loop(0, 16, second_loop, 0)

    first_lanes = lax.broadcasted_iota(jnp.int32, (1, D), 1) < HALF

    def key_share(k, carry):
        plain, cosined, sined = carry
        grad = dkacc[k].reshape(4 * D, D)
        rot = block_rows(k, 0, D).astype(F32).reshape(4 * D, D)
        straight = (grad * rot).reshape(4, 2, HALF, D)
        crossed = (grad * pltpu.roll(rot, HALF, 1)).reshape(4, 2, HALF, D)
        ct, st = ct_ref[0:HALF], st_ref[0:HALF]
        early_run = block_rows(k, D, 16).astype(F32)[:, 0:1, :]
        late_run = (2 * X * Y * Z - 1) - early_run
        run = jnp.concatenate([early_run[:, None], late_run[:, None]], axis=1)
        angle = run * (2.0 * HALF * freq_ref[...])
        cp, sp = jnp.cos(angle), jnp.sin(angle)

        def over_tokens(v):
            return jnp.sum(v, axis=2, keepdims=True)

        plain = plain + jnp.sum(over_tokens(straight), axis=(0, 1))
        cosined = cosined + jnp.sum(
            cp * over_tokens(straight * ct) - sp * over_tokens(straight * st), axis=(0, 1)
        )
        sined = sined + jnp.sum(
            sp * over_tokens(crossed * ct) + cp * over_tokens(crossed * st), axis=(0, 1)
        )
        return plain, cosined, sined

    none = jnp.zeros((1, D), F32)
    plain, cosined, sined = lax.fori_loop(0, 4, key_share, (none, none, none))

    def swap_lanes(v):
        return pltpu.roll(jnp.broadcast_to(v, (8, D)), HALF, 1)[0:1]

    both_sines = sined + swap_lanes(sined)
    key_gain = plain + swap_lanes(plain) + cosined - swap_lanes(cosined)
    key_gain = key_gain + jnp.where(first_lanes, both_sines, -both_sines)
    key_gain = key_gain * (0.5 * SCALE) / kg_ref[...]

    row_id = lax.broadcasted_iota(jnp.int32, (2 * D, 2 * D), 0)
    lane_id = lax.broadcasted_iota(jnp.int32, (2 * D, 2 * D), 1)
    identity = jnp.where(row_id == lane_id, 1.0, 0.0).astype(BF16)

    def over_heads(v):
        return v[:, 0:D] + v[:, D:2 * D] + v[:, 2 * D:3 * D] + v[:, 3 * D:]

    def query_share(rel, carry):
        plain, turned = carry
        rot = dot(identity, qc[lax.rem(x + rel, X), 0:Q], NT)
        grad = dqacc[rel]
        for part in range(2):
            a, b = grad[part * D:part * D + HALF], grad[part * D + HALF:part * D + D]
            e, f = rot[part * D:part * D + HALF], rot[part * D + HALF:part * D + D]
            ae, bf = over_heads(a * e), over_heads(b * f)
            plain = plain + ae + bf
            turned = turned + qcos[rel, part] * (ae - bf) + qsin[rel, part] * over_heads(a * f + b * e)
        return plain, turned

    none = jnp.zeros((HALF, D), F32)
    plain, turned = lax.fori_loop(0, X, query_share, (none, none))
    query_gain = jnp.transpose(jnp.concatenate([plain + turned, plain - turned], axis=0))
    query_gain = jnp.sum(query_gain, axis=0, keepdims=True) * (0.5 * SCALE) / qg_ref[...]

    def gain_copies(stage):
        me, size, peer = groups[stage]
        return [
            pltpu.make_async_remote_copy(
                src_ref=gsum.at[stage], dst_ref=gbuf.at[stage, me],
                send_sem=gssem.at[stage, j], recv_sem=grsem.at[stage, j],
                device_id=peer(j), device_id_type=pl.DeviceIdType.MESH,
            )
            for j in range(1, size)
        ]

    def gain_start(stage, mine):
        gsum[stage] = mine
        gbuf[stage, groups[stage][0]] = mine
        copies = gain_copies(stage)
        for c in copies:
            c.start()
        return copies

    def gain_finish(stage, copies):
        for c in copies:
            c.wait()
        total = gbuf[stage, 0]
        for j in range(1, groups[stage][1]):
            total = total + gbuf[stage, j]
        return total

    copies = gain_start(0, jnp.concatenate([query_gain, key_gain, jnp.zeros((6, D), F32)], axis=0))

    def own_sum(r):
        total = jnp.concatenate([dkacc[0, ys[r]] * SCALE, dvacc[0, ys[r]]], axis=0)
        for wi in (0, 1):
            total = total + ring[wi, 3, r].astype(F32)
        return total

    def ring_end(r):
        for wi, way in enumerate("RL"):
            arrived(f"S{way}4{r}", ring.at[wi, 3, r])

    ring_step(2, 1)
    ring_step(2, 0)
    ring_step(3, 1)
    copies = gain_start(1, gain_finish(0, copies))
    ring_step(3, 0)

    def stored(lo, hi):
        return jnp.concatenate(
            [jnp.where(swapped, hi, lo), jnp.where(swapped, lo, hi)], axis=0
        )

    def norm_back(g, xn, inverse, gain):
        s = g * gain
        return inverse * (s - xn * jnp.mean(s * xn, axis=-1, keepdims=True))

    whole = dqacc[0]
    for m in (1, 2, 3):
        arrived(f"DQ{m}", dqr.at[m - 1])
        whole = whole + dqr[m - 1].astype(F32)
    turned = jnp.transpose(whole) * SCALE
    for h in range(HEADS):
        if h == 2:
            ring_end(1)
            ysend[...] = own_sum(1).astype(BF16)
            send("SY", ysend, yrecv, partner)
        if h == 5:
            copies = gain_start(2, gain_finish(1, copies))
        cols = slice(h * D, (h + 1) * D)
        rows = slice(h * HALF, (h + 1) * HALF)
        gq = unrope(stored(turned[rows, 0:D], turned[rows, D:]))
        qn, inverse = normed(q_ref[:, cols].astype(F32))
        dq_ref[:, cols] = norm_back(gq, qn, inverse, qg_ref[...]).astype(BF16)

    ring_end(0)
    arrived("SY", yrecv)
    own = own_sum(0) + yrecv[...].astype(F32)
    gk = unrope(stored(own[:HALF], own[HALF:D]))
    kn, inverse = normed(k_ref[...].astype(F32))
    dk_ref[...] = norm_back(gk, kn, inverse, kg_ref[...]).astype(BF16)
    dv_ref[...] = stored(own[D:D + HALF], own[D + HALF:]).astype(BF16)

    total = gain_finish(2, copies)
    qgain_ref[...] = total[0:1]
    kgain_ref[...] = total[1:2]

    for name, src, dst, to in started:
        copy(name, src, dst, to).wait_send()


def place(*refs):
    sems = refs[-1]
    copies = [pltpu.make_async_copy(refs[i], refs[5 + i], sems.at[i]) for i in range(5)]
    for c in copies:
        c.start()
    for c in copies:
        c.wait()


def shards(heads_axis, query_raw, key_before_norm, values, grads, q_gain, k_gain, tok_pos):
    frequency = np.power(np.float32(BASE), -(np.arange(HALF, dtype=np.float32) * np.float32(2.0 / D)))
    frequency = jnp.asarray(np.tile(frequency.astype(np.float32), 2).reshape(1, D))
    vmem = pl.BlockSpec(memory_space=pltpu.VMEM)
    count = len(MSG)
    shapes = (
        jax.ShapeDtypeStruct((D, HEADS * D), BF16),
        jax.ShapeDtypeStruct((D, D), BF16),
        jax.ShapeDtypeStruct((D, D), BF16),
        jax.ShapeDtypeStruct((1, D), F32),
        jax.ShapeDtypeStruct((1, D), F32),
    )
    results = pl.pallas_call(
        functools.partial(body, heads_axis),
        out_shape=shapes,
        in_specs=[vmem] * 8,
        out_specs=(vmem,) * 5,
        scratch_shapes=[
            pltpu.VMEM((D, D), F32),
            pltpu.VMEM((D, D), F32),
            pltpu.VMEM((Z, Y, KROWS + D, D), BF16),
            pltpu.VMEM((X, Q + 16, 2 * D), BF16),
            pltpu.VMEM((X, Q, 2 * D), BF16),
            pltpu.VMEM((16, 4 * HALF, Q), F32),
            pltpu.VMEM((16, 4 * HALF, Q), F32),
            pltpu.VMEM((16, 4 * HALF, Q), F32),
            pltpu.VMEM((16, 4 * HALF, Q), F32),
            pltpu.VMEM((D, Q), F32),
            pltpu.VMEM((D, Q), F32),
            pltpu.VMEM((4, 4, 8, Q), F32),
            pltpu.VMEM((X, X, 8, Q), F32),
            pltpu.VMEM((X, 8, Q), F32),
            pltpu.VMEM((X, 2 * D, Q), F32),
            pltpu.VMEM((4, 4, D, D), F32),
            pltpu.VMEM((4, 4, D, D), F32),
            pltpu.VMEM((D, D), F32),
            pltpu.VMEM((D, D), F32),
            pltpu.VMEM((X, 2, HALF, D), F32),
            pltpu.VMEM((X, 2, HALF, D), F32),
            pltpu.VMEM((HALF, D), F32),
            pltpu.VMEM((Z, Y, 2 * D, D), BF16),
            pltpu.VMEM((2, 4, 2, 2 * D, D), BF16),
            pltpu.VMEM((3, 2 * D, Q), BF16),
            pltpu.VMEM((3, 2 * D, Q), BF16),
            pltpu.VMEM((2 * D, D), BF16),
            pltpu.VMEM((2 * D, D), BF16),
            pltpu.VMEM((3, 8, 8, D), F32),
            pltpu.VMEM((3, 8, D), F32),
            pltpu.SemaphoreType.DMA((count,)),
            pltpu.SemaphoreType.DMA((count,)),
            pltpu.SemaphoreType.DMA((3, 8)),
            pltpu.SemaphoreType.DMA((3, 8)),
        ],
        compiler_params=pltpu.CompilerParams(
            collective_id=0, has_side_effects=True, vmem_limit_bytes=60 * 1024 * 1024
        ),
    )(
        query_raw, key_before_norm, values, grads,
        q_gain.reshape(1, D), k_gain.reshape(1, D), tok_pos.reshape(1, D), frequency,
    )
    anywhere = pl.BlockSpec(memory_space=pl.ANY)
    dq, dk, dv, query_gain, key_gain = pl.pallas_call(
        place,
        out_shape=shapes,
        in_specs=[vmem] * 5,
        out_specs=(anywhere,) * 5,
        scratch_shapes=[pltpu.SemaphoreType.DMA((5,))],
    )(*results)
    return dq, dk, dv, query_gain.reshape(D), key_gain.reshape(D)


def solution(mesh):
    split = P("ctx", "head")
    return jax.shard_map(
        functools.partial(shards, mesh.shape["head"]),
        mesh=mesh,
        in_specs=(split, split, split, split, P(), P(), P("ctx")),
        out_specs=(split, split, split, P(), P()),
        check_vma=False,
    )
```

```python
import functools

import jax
import jax.numpy as jnp
import numpy as np
from jax import lax
from jax.experimental import pallas as pl
from jax.experimental.pallas import tpu as pltpu
from jax.sharding import PartitionSpec as P

D = 128
HALF = 64
X, Y, Z = 4, 2, 8
HEADS = 8
Q = HEADS * HALF
EPS = 1e-06
BASE = 1000000.0
SCALE = D ** (-0.5)
LOG2E = 1.4426950408889634
KROWS = 144
F32, BF16 = jnp.float32, jnp.bfloat16
NT = (((1,), (1,)), ((), ()))
NN = (((1,), (0,)), ((), ()))
TN = (((0,), (0,)), ((), ()))


def dot(a, b, dims):
    return lax.dot_general(a, b, dims, preferred_element_type=F32)


def message_table():
    names = ["Y0", "Y1", "QR", "QL", "GR", "GL", "Q2", "G2"]
    for way in "RL":
        for step in (1, 2, 3):
            names += [f"Z{way}{step}{r}{h}" for r in (0, 1) for h in (0, 1)]
        names += [f"Z{way}4{0 if way == 'R' else 1}{h}" for h in (0, 1)]
        names.append(f"S{way}1{0 if way == 'R' else 1}")
        for step in (2, 3, 4):
            names += [f"S{way}{step}{r}" for r in (0, 1)]
    for j in range(4):
        names += [f"ST{j}{m}" for m in (1, 2, 3)]
    names += ["DQ1", "DQ2", "DQ3", "SY"]
    return {name: index for index, name in enumerate(names)}


MSG = message_table()


class Part:
    def __init__(self, ref, index=None):
        self.ref, self.index = ref, index

    def make(self):
        return self.ref if self.index is None else self.ref.at[self.index]

    @property
    def at(self):
        return Maker(self.ref)

    def __getitem__(self, index):
        return self.make()[index]

    def __setitem__(self, index, value):
        self.make()[index] = value


class Maker:
    def __init__(self, ref):
        self.ref = ref

    def __getitem__(self, index):
        return Part(self.ref, index)


def rel_of(j):
    return j + (j // 2) * (5 - 2 * j)


def body(
    heads_axis, q_ref, k_ref, v_ref, g_ref, qg_ref, kg_ref, pos_ref, freq_ref,
    dq_ref, dk_ref, dv_ref, qgain_ref, kgain_ref,
    cos_ref, sin_ref, kv, qc, gc, e_a, g_a, e_b, g_b, e_d, g_d, sums, stbuf, stats, dqacc, dkacc, dvacc, ct_ref, st_ref, qcos, qsin, freq_col,
    dkv, ring, dqs, dqr, ysend, yrecv, gbuf, gsum,
    ssem, rsem, gssem, grsem,
):
    kv, qc, gc, stbuf, dkv, ring, dqs, dqr, ysend, yrecv = (
        Part(ref) for ref in (kv, qc, gc, stbuf, dkv, ring, dqs, dqr, ysend, yrecv)
    )
    ctx = lax.axis_index("ctx")
    head = lax.axis_index("head")
    z, x, y = ctx // (X * Y), (ctx // Y) % X, ctx % Y
    w = ctx % (X * Y)
    ys = (y, 1 - y)

    zpos = [lax.rem(z + off, Z) for off in range(Z)]
    xpos = [lax.rem(x + off, X) for off in range(X)]

    def zm(off):
        return zpos[off % Z]

    def xm(off):
        return xpos[off % X]

    def dev(zz, xx, yy):
        return ((zz * X + xx) * Y + yy, head)

    groups = (
        (z, Z, lambda j: (lax.rem(z + j, Z) * (X * Y) + w, head)),
        (w, X * Y, lambda j: (z * (X * Y) + lax.rem(w + j, X * Y), head)),
        (head, heads_axis, lambda j: (ctx, lax.rem(head + j, heads_axis))),
    )
    all_peers = [peer(j) for _, size, peer in groups for j in range(1, size)]

    barrier = pltpu.get_barrier_semaphore()
    for peer in all_peers:
        pl.semaphore_signal(barrier, inc=1, device_id=peer, device_id_type=pl.DeviceIdType.MESH)

    started = []

    def copy(name, src, dst, to):
        i = MSG[name]
        return pltpu.make_async_remote_copy(
            src_ref=src.make(), dst_ref=dst.make(), send_sem=ssem.at[i], recv_sem=rsem.at[i],
            device_id=to, device_id_type=pl.DeviceIdType.MESH,
        )

    def send(name, src, dst, to):
        copy(name, src, dst, to).start()
        started.append((name, src, dst, to))

    def arrived(name, dst):
        copy(name, dst, dst, (ctx, head)).wait_recv()

    xdev = [dev(z, xpos[m], y) for m in range(X)]
    right_x, left_x = dev(z, xm(1), y), dev(z, xm(-1), y)
    partner = dev(z, x, ys[1])
    side = {"R": (dev(zm(1), x, y), -1), "L": (dev(zm(-1), x, y), 1)}
    last = {"R": 0, "L": 1}

    positions = jnp.broadcast_to(pos_ref[...].astype(F32), (8, D))
    in_first = lax.broadcasted_iota(jnp.int32, (8, D), 1) < HALF
    first_top = jnp.max(jnp.where(in_first, positions, -1.0), axis=1, keepdims=True)
    second_top = jnp.max(jnp.where(in_first, -1.0, positions), axis=1, keepdims=True)
    swapped = jnp.broadcast_to(first_top > second_top, (8, D))[0:1]
    lowest = jnp.min(positions, axis=1, keepdims=True)
    p_me = jnp.broadcast_to(jnp.floor(lowest * (1.0 / HALF)), (8, D))
    p_rows = jnp.concatenate([p_me, p_me], axis=0).astype(BF16)

    def halves(v):
        first, second = v[:HALF], v[HALF:]
        return jnp.where(swapped, second, first), jnp.where(swapped, first, second)

    def rope(v):
        return v * cos_ref[...] + pltpu.roll(v, HALF, 1) * sin_ref[...]

    def unrope(v):
        return v * cos_ref[...] - pltpu.roll(v, HALF, 1) * sin_ref[...]

    def normed(v):
        inverse = lax.rsqrt(jnp.mean(v * v, axis=-1, keepdims=True) + EPS)
        return v * inverse, inverse


    angles = jnp.transpose(jnp.broadcast_to(positions[0:1], (D, D))) * freq_ref[...]
    cos_ref[...] = jnp.cos(angles)
    turn = jnp.sin(angles)
    sin_ref[...] = jnp.where(lax.broadcasted_iota(jnp.int32, (D, D), 1) < HALF, -turn, turn)

    kn, _ = normed(k_ref[...].astype(F32))
    k_lo, k_hi = halves(rope(kn * kg_ref[...]))
    v_lo, v_hi = halves(v_ref[...].astype(F32))
    kv[z, y, 0:HALF] = k_lo.astype(BF16)
    kv[z, y, HALF:D] = k_hi.astype(BF16)
    kv[z, y, D:KROWS] = p_rows
    kv[z, y, KROWS:KROWS + HALF] = v_lo.astype(BF16)
    kv[z, y, KROWS + HALF:KROWS + D] = v_hi.astype(BF16)
    pl.semaphore_wait(barrier, len(all_peers))

    def kv_part(zz, yy, h):
        return kv.at[zz, yy, pl.ds(0, KROWS) if h == 0 else pl.ds(KROWS, D)]

    for h in (0, 1):
        part = kv_part(z, y, h)
        send(f"Y{h}", part, part, partner)
        for way in "RL":
            send(f"Z{way}10{h}", part, part, side[way][0])

    for h in range(HEADS):
        rows = slice(h * HALF, (h + 1) * HALF)
        lo, hi = halves(g_ref[:, h * D:(h + 1) * D].astype(F32))
        gc[x, rows, 0:D] = lo.astype(BF16)
        gc[x, rows, D:] = hi.astype(BF16)

    send("GL", gc.at[x], gc.at[x], left_x)
    send("GR", gc.at[x], gc.at[x], right_x)

    for h in range(HEADS):
        rows = slice(h * HALF, (h + 1) * HALF)
        qn, _ = normed(q_ref[:, h * D:(h + 1) * D].astype(F32))
        lo, hi = halves(rope(qn * qg_ref[...]))
        qc[x, rows, 0:D] = lo.astype(BF16)
        qc[x, rows, D:] = hi.astype(BF16)
    qc[x, Q:, 0:D] = p_rows
    qc[x, Q:, D:] = p_rows
    send("QR", qc.at[x], qc.at[x], right_x)
    send("QL", qc.at[x], qc.at[x], left_x)

    zero = jnp.zeros((HALF, D), BF16)

    def diagonal(lo, hi):
        return jnp.concatenate(
            [jnp.concatenate([lo, zero], axis=1), jnp.concatenate([zero, hi], axis=1)], axis=0
        )

    def own_k():
        return diagonal(kv[z, y, 0:HALF], kv[z, y, HALF:D])

    scores = dot(own_k(), qc[x, 0:Q], NT)
    key_row = lax.broadcasted_iota(jnp.int32, (D, Q), 0) % HALF
    query_lane = lax.broadcasted_iota(jnp.int32, (D, Q), 1) % HALF
    exps = jnp.where(key_row <= query_lane, jnp.exp2(scores * (SCALE * LOG2E)), 0.0)
    own_v = diagonal(kv[z, y, KROWS:KROWS + HALF], kv[z, y, KROWS + HALF:KROWS + D])
    probs_grad = dot(own_v, gc[x], NT)
    e_d[...] = exps
    g_d[...] = probs_grad
    both = exps * probs_grad
    for j in (1, 2, 3):
        sums[j] = jnp.zeros((4, 8, Q), F32)
    for part in range(2):
        rows = slice(part * HALF, (part + 1) * HALF)
        sums[0, part] = exps[rows].reshape(8, 8, Q).sum(0)
        sums[0, 2 + part] = both[rows].reshape(8, 8, Q).sum(0)

    def kv_progress(r, d):
        for h in (0, 1):
            for way in "RL":
                to, sign = side[way]
                if d == 4 and r != last[way]:
                    continue
                part = kv_part(zm(sign * d), ys[r], h)
                arrived(f"Z{way}{d}{r}{h}", part)
                if d < 3 or (d == 3 and r == last[way]):
                    send(f"Z{way}{d + 1}{r}{h}", part, part, to)

    def y_progress():
        for h in (0, 1):
            part = kv_part(z, ys[1], h)
            arrived(f"Y{h}", part)
            for way in "RL":
                send(f"Z{way}11{h}", part, part, side[way][0])

    def gradient_forward():
        arrived("GL", gc.at[xm(1)])
        send("G2", gc.at[xm(1)], gc.at[xm(1)], left_x)

    def query_forward():
        arrived("QR", qc.at[xm(-1)])
        send("Q2", qc.at[xm(-1)], qc.at[xm(-1)], right_x)

    def far_queries():
        arrived("Q2", qc.at[xm(2)])
        arrived("G2", gc.at[xm(2)])

    def key_event(r, d):
        return lambda: kv_progress(r, d)

    events = {
        0: (key_event(0, 1), y_progress, key_event(0, 2), gradient_forward, key_event(1, 1)),
        1: (
            key_event(0, 3), key_event(1, 2), query_forward,
            lambda: arrived("QL", qc.at[xm(1)]),
        ),
        2: (lambda: arrived("GR", gc.at[xm(-1)]),),
        3: (key_event(0, 4),),
        6: (key_event(1, 3),),
        9: (key_event(1, 4),),
        12: (far_queries,),
    }

    def block_rows(k, first, count):
        near = lax.rem(z + k, Z)
        far = lax.rem(z + (Z - 1) - k, Z)
        return jnp.concatenate(
            [kv[near, :, first:first + count, :], kv[far, :, first:first + count, :]], axis=0
        )

    def block_masks(k, b):
        pj = block_rows(k, D, 16).astype(F32)[:, 0:8, :]
        pq = qc[b, Q:, 0:D].astype(F32)[None, 0:8]
        early = jnp.where(pj < pq, 1.0, 0.0)
        other = jnp.where(pj == pq, 0.0, 1.0)
        return early, other

    def wide(v):
        return jnp.concatenate([v, v, v, v], axis=-1)

    def joined(lo, hi, early):
        e = early[:, 0:1, :].astype(BF16)
        return jnp.concatenate([lo * e, hi * (1.0 - e).astype(BF16)], axis=-1).reshape(4 * HALF, 2 * D)

    def pass_one(k, j, b, u):
        early, other = block_masks(k, b)
        klo, khi = block_rows(k, 0, HALF), block_rows(k, HALF, HALF)
        vlo, vhi = block_rows(k, KROWS, HALF), block_rows(k, KROWS + HALF, HALF)
        ex = jnp.exp2(dot(klo.reshape(4 * HALF, D), qc[b, 0:Q, D:], NT) * (SCALE * LOG2E))
        gp = dot(vlo.reshape(4 * HALF, D), gc[b, :, D:], NT)
        e_a[u] = ex
        g_a[u] = gp
        sums[j, 1] += ex.reshape(32, 8, Q).sum(0)
        sums[j, 3] += (ex * gp).reshape(32, 8, Q).sum(0)
        ex = jnp.exp2(dot(joined(klo, khi, early), qc[b, 0:Q], NT) * (SCALE * LOG2E))
        ex = ex.reshape(4, HALF, Q) * wide(other[:, 0:1, :])
        gp = dot(joined(vlo, vhi, early), gc[b], NT).reshape(4, HALF, Q)
        e_b[u] = ex.reshape(4 * HALF, Q)
        g_b[u] = gp.reshape(4 * HALF, Q)
        part = ex.reshape(4, 8, 8, Q).sum(1)
        partg = (ex * gp).reshape(4, 8, 8, Q).sum(1)
        ew = wide(early)
        sums[j, 0] += (part * ew).sum(0)
        sums[j, 1] += (part * (1.0 - ew)).sum(0)
        sums[j, 2] += (partg * ew).sum(0)
        sums[j, 3] += (partg * (1.0 - ew)).sum(0)

    def statistics_out(j):
        b = xm(rel_of(j))
        slot = stbuf.at[b, x]
        slot[...] = jnp.concatenate(
            [jnp.sum(sums[j], axis=1), jnp.zeros((4, Q), F32)], axis=0
        )
        for m in (1, 2, 3):
            send(f"ST{j}{m}", slot, slot, xdev[m])

    def first_loop(i, carry):
        far = i // 12
        k = (1 - far) * (i // 3) + far * (i - 12)
        j = (1 - far) * (i % 3) + far * 3
        for case, steps in events.items():
            @pl.when(i == case)
            def _(steps=steps):
                for step in steps:
                    step()
        rel = rel_of(j)
        pass_one(k, j, lax.rem(x + rel, X), k * 4 + rel)
        for case, done in ((9, 0), (10, 1), (11, 2), (15, 3)):
            @pl.when(i == case)
            def _(done=done):
                statistics_out(done)
        return carry

    lax.fori_loop(0, 16, first_loop, 0)

    token_row = (lax.broadcasted_iota(jnp.int32, (D, D), 0) % HALF).astype(F32)
    twice = token_row * (2.0 * freq_ref[...])
    ct_ref[...] = jnp.cos(twice)
    st_ref[...] = jnp.sin(twice)
    freq_col[...] = jnp.transpose(jnp.broadcast_to(freq_ref[...], (D, D)))[0:HALF]
    token_lane = (lax.broadcasted_iota(jnp.int32, (HALF, D), 1) % HALF).astype(F32)

    def query_tables(rel, carry):
        early_run = jnp.max(qc[lax.rem(x + rel, X), Q:, 0:D].astype(F32), axis=0, keepdims=True)
        for part in range(2):
            run = early_run if part == 0 else (2 * X * Y * Z - 1) - early_run
            angle = (run * HALF + token_lane) * (2.0 * freq_col[...])
            qcos[rel, part] = jnp.cos(angle)
            qsin[rel, part] = jnp.sin(angle)
        return carry

    lax.fori_loop(0, X, query_tables, 0)

    for k in range(4):
        dkacc[k] = jnp.zeros((4, D, D), F32)
        dvacc[k] = jnp.zeros((4, D, D), F32)
    for m in (1, 2, 3):
        dqacc[m] = jnp.zeros((2 * D, Q), F32)

    for j in range(4):
        for m in (1, 2, 3):
            arrived(f"ST{j}{m}", stbuf.at[xm(rel_of(j) - m), xm(-m)])
    for b in range(4):
        total = stbuf[b, 0]
        for s in range(1, 4):
            total = total + stbuf[b, s]
        inv = 1.0 / total[0:2]
        stats[b] = jnp.concatenate([inv, total[2:4] * inv, jnp.zeros((4, Q), F32)], axis=0)

    rowsel = lax.broadcasted_iota(jnp.int32, (D, Q), 0) < HALF
    pr = e_d[...] * jnp.where(rowsel, stats[x, 0:1], stats[x, 1:2])
    gs = (pr * (g_d[...] - jnp.where(rowsel, stats[x, 2:3], stats[x, 3:4]))).astype(BF16)
    pr = pr.astype(BF16)
    top = lax.broadcasted_iota(jnp.int32, (D, D), 0) < HALF
    full = dot(pr, gc[x], NN)
    dvacc[0, y] = jnp.where(top, full[:, 0:D], full[:, D:])
    full = dot(gs, qc[x, 0:Q], NN)
    dkacc[0, y] = jnp.where(top, full[:, 0:D], full[:, D:])
    dqacc[0] = dot(own_k(), gs, TN)

    def pass_two(k, b, rel, u):
        early, _ = block_masks(k, b)
        klo, khi = block_rows(k, 0, HALF), block_rows(k, HALF, HALF)
        pr = e_a[u] * stats[b, 1:2]
        gs = (pr * (g_a[u] - stats[b, 3:4])).astype(BF16)
        pr = pr.astype(BF16)
        dva = dot(pr, gc[b, :, D:], NN).reshape(4, HALF, D)
        dka = dot(gs, qc[b, 0:Q, D:], NN).reshape(4, HALF, D)
        dqacc[rel, D:, :] += dot(klo.reshape(4 * HALF, D), gs, TN)
        ew = wide(early[:, 0:1, :]) > 0.5
        invb = jnp.where(ew, stats[b, 0:1][None], stats[b, 1:2][None])
        delb = jnp.where(ew, stats[b, 2:3][None], stats[b, 3:4][None])
        pr = e_b[u].reshape(4, HALF, Q) * invb
        gs = (pr * (g_b[u].reshape(4, HALF, Q) - delb)).astype(BF16).reshape(4 * HALF, Q)
        pr = pr.astype(BF16).reshape(4 * HALF, Q)
        dvc = dot(pr, gc[b], NN).reshape(4, HALF, 2 * D)
        dkc = dot(gs, qc[b, 0:Q], NN).reshape(4, HALF, 2 * D)
        dqacc[rel] += dot(joined(klo, khi, early), gs, TN)
        e1 = early[:, 0:1, :]
        dkacc[k, :, 0:HALF] += dka + dkc[..., 0:D] * e1
        dkacc[k, :, HALF:] += dkc[..., D:] * (1.0 - e1)
        dvacc[k, :, 0:HALF] += dva + dvc[..., 0:D] * e1
        dvacc[k, :, HALF:] += dvc[..., D:] * (1.0 - e1)

    def pair_done(k):
        for place, zz in enumerate((zm(k), zm(-k - 1))):
            if zz is zpos[0]:
                continue
            rows = slice(2 * place, 2 * place + 2)
            dkv[zz, :, 0:D, :] = (dkacc[k, rows] * SCALE).astype(BF16)
            dkv[zz, :, D:, :] = dvacc[k, rows].astype(BF16)
        if k == 3:
            for wi, way in enumerate("RL"):
                r = last[way]
                send(f"S{way}1{r}", dkv.at[zm(4), ys[r]], ring.at[wi, 0, r], side[way][0])

    def ring_step(step, r):
        off = 4 - step
        for wi, way in enumerate("RL"):
            part = dkv.at[zm(off if way == "R" else -off), ys[r]]
            if step > 1 or r == last[way]:
                came = ring.at[wi, step - 1, r]
                arrived(f"S{way}{step}{r}", came)
                part[...] = (part[...].astype(F32) + came[...].astype(F32)).astype(BF16)
            send(f"S{way}{step + 1}{r}", part, ring.at[wi, step, r], side[way][0])

    def queries_out(m):
        dqs[m - 1] = dqacc[m].astype(BF16)
        send(f"DQ{m}", dqs.at[m - 1], dqr.at[m - 1], xdev[m])

    def second_loop(i, carry):
        a, c = (i + 12) // 16, (i + 9) // 16
        k = (1 - a) * 3 + (a - c) * (6 - i) + c * (5 - (i + 2) // 3)
        j = (1 - a) * (3 - i) + (a - c) * 3 + c * (2 - (i + 2) % 3)
        rel = rel_of(j)
        pass_two(k, lax.rem(x + rel, X), rel, k * 4 + rel)
        for case, m in ((6, 2), (13, 3), (14, 1)):
            @pl.when(i == case)
            def _(m=m):
                queries_out(m)
        for case in range(4):
            @pl.when(i == (3 if case == 0 else 3 * case + 6))
            def _(case=case):
                pair_done(3 - case)
                if case == 1:
                    ring_step(1, 1)
                    ring_step(1, 0)
        return carry

    lax.fori_loop(0, 16, second_loop, 0)

    ring_step(2, 1)

    first_lanes = lax.broadcasted_iota(jnp.int32, (1, D), 1) < HALF

    def key_share(k, carry):
        plain, cosined, sined = carry
        grad = dkacc[k].reshape(4 * D, D)
        rot = block_rows(k, 0, D).astype(F32).reshape(4 * D, D)
        straight = (grad * rot).reshape(4, 2, HALF, D)
        crossed = (grad * pltpu.roll(rot, HALF, 1)).reshape(4, 2, HALF, D)
        ct, st = ct_ref[0:HALF], st_ref[0:HALF]
        early_run = block_rows(k, D, 16).astype(F32)[:, 0:1, :]
        late_run = (2 * X * Y * Z - 1) - early_run
        run = jnp.concatenate([early_run[:, None], late_run[:, None]], axis=1)
        angle = run * (2.0 * HALF * freq_ref[...])
        cp, sp = jnp.cos(angle), jnp.sin(angle)

        def over_tokens(v):
            return jnp.sum(v, axis=2, keepdims=True)

        plain = plain + jnp.sum(over_tokens(straight), axis=(0, 1))
        cosined = cosined + jnp.sum(
            cp * over_tokens(straight * ct) - sp * over_tokens(straight * st), axis=(0, 1)
        )
        sined = sined + jnp.sum(
            sp * over_tokens(crossed * ct) + cp * over_tokens(crossed * st), axis=(0, 1)
        )
        return plain, cosined, sined

    none = jnp.zeros((1, D), F32)
    plain, cosined, sined = lax.fori_loop(0, 4, key_share, (none, none, none))

    def swap_lanes(v):
        return pltpu.roll(jnp.broadcast_to(v, (8, D)), HALF, 1)[0:1]

    both_sines = sined + swap_lanes(sined)
    key_gain = plain + swap_lanes(plain) + cosined - swap_lanes(cosined)
    key_gain = key_gain + jnp.where(first_lanes, both_sines, -both_sines)
    key_gain = key_gain * (0.5 * SCALE) / kg_ref[...]

    row_id = lax.broadcasted_iota(jnp.int32, (2 * D, 2 * D), 0)
    lane_id = lax.broadcasted_iota(jnp.int32, (2 * D, 2 * D), 1)
    identity = jnp.where(row_id == lane_id, 1.0, 0.0).astype(BF16)

    def over_heads(v):
        return v[:, 0:D] + v[:, D:2 * D] + v[:, 2 * D:3 * D] + v[:, 3 * D:]

    def query_share(rel, carry):
        plain, turned = carry
        rot = dot(identity, qc[lax.rem(x + rel, X), 0:Q], NT)
        grad = dqacc[rel]
        for part in range(2):
            a, b = grad[part * D:part * D + HALF], grad[part * D + HALF:part * D + D]
            e, f = rot[part * D:part * D + HALF], rot[part * D + HALF:part * D + D]
            ae, bf = over_heads(a * e), over_heads(b * f)
            plain = plain + ae + bf
            turned = turned + qcos[rel, part] * (ae - bf) + qsin[rel, part] * over_heads(a * f + b * e)
        return plain, turned

    none = jnp.zeros((HALF, D), F32)
    plain, turned = lax.fori_loop(0, X, query_share, (none, none))
    query_gain = jnp.transpose(jnp.concatenate([plain + turned, plain - turned], axis=0))
    query_gain = jnp.sum(query_gain, axis=0, keepdims=True) * (0.5 * SCALE) / qg_ref[...]

    def gain_copies(stage):
        me, size, peer = groups[stage]
        return [
            pltpu.make_async_remote_copy(
                src_ref=gsum.at[stage], dst_ref=gbuf.at[stage, me],
                send_sem=gssem.at[stage, j], recv_sem=grsem.at[stage, j],
                device_id=peer(j), device_id_type=pl.DeviceIdType.MESH,
            )
            for j in range(1, size)
        ]

    def gain_start(stage, mine):
        gsum[stage] = mine
        gbuf[stage, groups[stage][0]] = mine
        copies = gain_copies(stage)
        for c in copies:
            c.start()
        return copies

    def gain_finish(stage, copies):
        for c in copies:
            c.wait()
        total = gbuf[stage, 0]
        for j in range(1, groups[stage][1]):
            total = total + gbuf[stage, j]
        return total

    copies = gain_start(0, jnp.concatenate([query_gain, key_gain, jnp.zeros((6, D), F32)], axis=0))

    def own_sum(r):
        total = jnp.concatenate([dkacc[0, ys[r]] * SCALE, dvacc[0, ys[r]]], axis=0)
        for wi in (0, 1):
            total = total + ring[wi, 3, r].astype(F32)
        return total

    def ring_end(r):
        for wi, way in enumerate("RL"):
            arrived(f"S{way}4{r}", ring.at[wi, 3, r])

    ring_step(2, 0)
    ring_step(3, 1)
    copies = gain_start(1, gain_finish(0, copies))
    ring_step(3, 0)

    def stored(lo, hi):
        return jnp.concatenate(
            [jnp.where(swapped, hi, lo), jnp.where(swapped, lo, hi)], axis=0
        )

    def norm_back(g, xn, inverse, gain):
        s = g * gain
        return inverse * (s - xn * jnp.mean(s * xn, axis=-1, keepdims=True))

    whole = dqacc[0]
    for m in (1, 2, 3):
        arrived(f"DQ{m}", dqr.at[m - 1])
        whole = whole + dqr[m - 1].astype(F32)
    turned = jnp.transpose(whole) * SCALE
    for h in range(HEADS):
        if h == 2:
            ring_end(1)
            ysend[...] = own_sum(1).astype(BF16)
            send("SY", ysend, yrecv, partner)
        if h == 5:
            copies = gain_start(2, gain_finish(1, copies))
        cols = slice(h * D, (h + 1) * D)
        rows = slice(h * HALF, (h + 1) * HALF)
        gq = unrope(stored(turned[rows, 0:D], turned[rows, D:]))
        qn, inverse = normed(q_ref[:, cols].astype(F32))
        dq_ref[:, cols] = norm_back(gq, qn, inverse, qg_ref[...]).astype(BF16)

    ring_end(0)
    arrived("SY", yrecv)
    own = own_sum(0) + yrecv[...].astype(F32)
    gk = unrope(stored(own[:HALF], own[HALF:D]))
    kn, inverse = normed(k_ref[...].astype(F32))
    dk_ref[...] = norm_back(gk, kn, inverse, kg_ref[...]).astype(BF16)
    dv_ref[...] = stored(own[D:D + HALF], own[D + HALF:]).astype(BF16)

    total = gain_finish(2, copies)
    qgain_ref[...] = total[0:1]
    kgain_ref[...] = total[1:2]

    for name, src, dst, to in started:
        copy(name, src, dst, to).wait_send()


def place(*refs):
    sems = refs[-1]
    copies = [pltpu.make_async_copy(refs[i], refs[5 + i], sems.at[i]) for i in range(5)]
    for c in copies:
        c.start()
    for c in copies:
        c.wait()


def shards(heads_axis, query_raw, key_before_norm, values, grads, q_gain, k_gain, tok_pos):
    frequency = np.power(np.float32(BASE), -(np.arange(HALF, dtype=np.float32) * np.float32(2.0 / D)))
    frequency = jnp.asarray(np.tile(frequency.astype(np.float32), 2).reshape(1, D))
    vmem = pl.BlockSpec(memory_space=pltpu.VMEM)
    count = len(MSG)
    shapes = (
        jax.ShapeDtypeStruct((D, HEADS * D), BF16),
        jax.ShapeDtypeStruct((D, D), BF16),
        jax.ShapeDtypeStruct((D, D), BF16),
        jax.ShapeDtypeStruct((1, D), F32),
        jax.ShapeDtypeStruct((1, D), F32),
    )
    results = pl.pallas_call(
        functools.partial(body, heads_axis),
        out_shape=shapes,
        in_specs=[vmem] * 8,
        out_specs=(vmem,) * 5,
        scratch_shapes=[
            pltpu.VMEM((D, D), F32),
            pltpu.VMEM((D, D), F32),
            pltpu.VMEM((Z, Y, KROWS + D, D), BF16),
            pltpu.VMEM((X, Q + 16, 2 * D), BF16),
            pltpu.VMEM((X, Q, 2 * D), BF16),
            pltpu.VMEM((16, 4 * HALF, Q), F32),
            pltpu.VMEM((16, 4 * HALF, Q), F32),
            pltpu.VMEM((16, 4 * HALF, Q), F32),
            pltpu.VMEM((16, 4 * HALF, Q), F32),
            pltpu.VMEM((D, Q), F32),
            pltpu.VMEM((D, Q), F32),
            pltpu.VMEM((4, 4, 8, Q), F32),
            pltpu.VMEM((X, X, 8, Q), F32),
            pltpu.VMEM((X, 8, Q), F32),
            pltpu.VMEM((X, 2 * D, Q), F32),
            pltpu.VMEM((4, 4, D, D), F32),
            pltpu.VMEM((4, 4, D, D), F32),
            pltpu.VMEM((D, D), F32),
            pltpu.VMEM((D, D), F32),
            pltpu.VMEM((X, 2, HALF, D), F32),
            pltpu.VMEM((X, 2, HALF, D), F32),
            pltpu.VMEM((HALF, D), F32),
            pltpu.VMEM((Z, Y, 2 * D, D), BF16),
            pltpu.VMEM((2, 4, 2, 2 * D, D), BF16),
            pltpu.VMEM((3, 2 * D, Q), BF16),
            pltpu.VMEM((3, 2 * D, Q), BF16),
            pltpu.VMEM((2 * D, D), BF16),
            pltpu.VMEM((2 * D, D), BF16),
            pltpu.VMEM((3, 8, 8, D), F32),
            pltpu.VMEM((3, 8, D), F32),
            pltpu.SemaphoreType.DMA((count,)),
            pltpu.SemaphoreType.DMA((count,)),
            pltpu.SemaphoreType.DMA((3, 8)),
            pltpu.SemaphoreType.DMA((3, 8)),
        ],
        compiler_params=pltpu.CompilerParams(
            collective_id=0, has_side_effects=True, vmem_limit_bytes=60 * 1024 * 1024
        ),
    )(
        query_raw, key_before_norm, values, grads,
        q_gain.reshape(1, D), k_gain.reshape(1, D), tok_pos.reshape(1, D), frequency,
    )
    anywhere = pl.BlockSpec(memory_space=pl.ANY)
    dq, dk, dv, query_gain, key_gain = pl.pallas_call(
        place,
        out_shape=shapes,
        in_specs=[vmem] * 5,
        out_specs=(anywhere,) * 5,
        scratch_shapes=[pltpu.SemaphoreType.DMA((5,))],
    )(*results)
    return dq, dk, dv, query_gain.reshape(D), key_gain.reshape(D)


def solution(mesh):
    split = P("ctx", "head")
    return jax.shard_map(
        functools.partial(shards, mesh.shape["head"]),
        mesh=mesh,
        in_specs=(split, split, split, split, P(), P(), P("ctx")),
        out_specs=(split, split, split, P(), P()),
        check_vma=False,
    )
```

```python
import functools

import jax
import jax.numpy as jnp
import numpy as np
from jax import lax
from jax.experimental import pallas as pl
from jax.experimental.pallas import tpu as pltpu
from jax.sharding import PartitionSpec as P

D = 128
HALF = 64
X, Y, Z = 4, 2, 8
HEADS = 8
Q = HEADS * HALF
EPS = 1e-06
BASE = 1000000.0
SCALE = D ** (-0.5)
LOG2E = 1.4426950408889634
KROWS = 144
F32, BF16 = jnp.float32, jnp.bfloat16
NT = (((1,), (1,)), ((), ()))
NN = (((1,), (0,)), ((), ()))
TN = (((0,), (0,)), ((), ()))


def dot(a, b, dims):
    return lax.dot_general(a, b, dims, preferred_element_type=F32)


def message_table():
    names = ["Y0", "Y1", "QR", "QL", "GR", "GL", "Q2", "G2"]
    for way in "RL":
        for step in (1, 2, 3):
            names += [f"Z{way}{step}{r}{h}" for r in (0, 1) for h in (0, 1)]
        names += [f"Z{way}4{0 if way == 'R' else 1}{h}" for h in (0, 1)]
        names.append(f"S{way}1{0 if way == 'R' else 1}")
        for step in (2, 3, 4):
            names += [f"S{way}{step}{r}" for r in (0, 1)]
    for j in range(4):
        names += [f"ST{j}{m}" for m in (1, 2, 3)]
    names += ["DQ1", "DQ2", "DQ3", "SY"]
    return {name: index for index, name in enumerate(names)}


MSG = message_table()


class Part:
    def __init__(self, ref, index=None):
        self.ref, self.index = ref, index

    def make(self):
        return self.ref if self.index is None else self.ref.at[self.index]

    @property
    def at(self):
        return Maker(self.ref)

    def __getitem__(self, index):
        return self.make()[index]

    def __setitem__(self, index, value):
        self.make()[index] = value


class Maker:
    def __init__(self, ref):
        self.ref = ref

    def __getitem__(self, index):
        return Part(self.ref, index)


def rel_of(j):
    return j + (j // 2) * (5 - 2 * j)


def body(
    heads_axis, q_ref, k_ref, v_ref, g_ref, qg_ref, kg_ref, pos_ref, freq_ref,
    dq_ref, dk_ref, dv_ref, qgain_ref, kgain_ref,
    cos_ref, sin_ref, kv, qc, gc, e_a, g_a, e_b, g_b, e_d, g_d, sums, stbuf, stats, dqacc, dkacc, dvacc, ct_ref, st_ref, qcos, qsin, freq_col,
    dkv, ring, dqs, dqr, ysend, yrecv, gbuf, gsum,
    ssem, rsem, gssem, grsem,
):
    kv, qc, gc, stbuf, dkv, ring, dqs, dqr, ysend, yrecv = (
        Part(ref) for ref in (kv, qc, gc, stbuf, dkv, ring, dqs, dqr, ysend, yrecv)
    )
    ctx = lax.axis_index("ctx")
    head = lax.axis_index("head")
    z, x, y = ctx // (X * Y), (ctx // Y) % X, ctx % Y
    w = ctx % (X * Y)
    ys = (y, 1 - y)

    zpos = [lax.rem(z + off, Z) for off in range(Z)]
    xpos = [lax.rem(x + off, X) for off in range(X)]

    def zm(off):
        return zpos[off % Z]

    def xm(off):
        return xpos[off % X]

    def dev(zz, xx, yy):
        return ((zz * X + xx) * Y + yy, head)

    groups = (
        (z, Z, lambda j: (lax.rem(z + j, Z) * (X * Y) + w, head)),
        (w, X * Y, lambda j: (z * (X * Y) + lax.rem(w + j, X * Y), head)),
        (head, heads_axis, lambda j: (ctx, lax.rem(head + j, heads_axis))),
    )
    all_peers = [peer(j) for _, size, peer in groups for j in range(1, size)]

    barrier = pltpu.get_barrier_semaphore()
    for peer in all_peers:
        pl.semaphore_signal(barrier, inc=1, device_id=peer, device_id_type=pl.DeviceIdType.MESH)

    started = []

    def copy(name, src, dst, to):
        i = MSG[name]
        return pltpu.make_async_remote_copy(
            src_ref=src.make(), dst_ref=dst.make(), send_sem=ssem.at[i], recv_sem=rsem.at[i],
            device_id=to, device_id_type=pl.DeviceIdType.MESH,
        )

    def send(name, src, dst, to):
        copy(name, src, dst, to).start()
        started.append((name, src, dst, to))

    def arrived(name, dst):
        copy(name, dst, dst, (ctx, head)).wait_recv()

    xdev = [dev(z, xpos[m], y) for m in range(X)]
    right_x, left_x = dev(z, xm(1), y), dev(z, xm(-1), y)
    partner = dev(z, x, ys[1])
    side = {"R": (dev(zm(1), x, y), -1), "L": (dev(zm(-1), x, y), 1)}
    last = {"R": 0, "L": 1}

    positions = jnp.broadcast_to(pos_ref[...].astype(F32), (8, D))
    in_first = lax.broadcasted_iota(jnp.int32, (8, D), 1) < HALF
    first_top = jnp.max(jnp.where(in_first, positions, -1.0), axis=1, keepdims=True)
    second_top = jnp.max(jnp.where(in_first, -1.0, positions), axis=1, keepdims=True)
    swapped = jnp.broadcast_to(first_top > second_top, (8, D))[0:1]
    lowest = jnp.min(positions, axis=1, keepdims=True)
    p_me = jnp.broadcast_to(jnp.floor(lowest * (1.0 / HALF)), (8, D))
    p_rows = jnp.concatenate([p_me, p_me], axis=0).astype(BF16)

    def halves(v):
        first, second = v[:HALF], v[HALF:]
        return jnp.where(swapped, second, first), jnp.where(swapped, first, second)

    def rope(v):
        return v * cos_ref[...] + pltpu.roll(v, HALF, 1) * sin_ref[...]

    def unrope(v):
        return v * cos_ref[...] - pltpu.roll(v, HALF, 1) * sin_ref[...]

    def normed(v):
        inverse = lax.rsqrt(jnp.mean(v * v, axis=-1, keepdims=True) + EPS)
        return v * inverse, inverse


    angles = jnp.transpose(jnp.broadcast_to(positions[0:1], (D, D))) * freq_ref[...]
    cos_ref[...] = jnp.cos(angles)
    turn = jnp.sin(angles)
    sin_ref[...] = jnp.where(lax.broadcasted_iota(jnp.int32, (D, D), 1) < HALF, -turn, turn)

    kn, _ = normed(k_ref[...].astype(F32))
    k_lo, k_hi = halves(rope(kn * kg_ref[...]))
    v_lo, v_hi = halves(v_ref[...].astype(F32))
    kv[z, y, 0:HALF] = k_lo.astype(BF16)
    kv[z, y, HALF:D] = k_hi.astype(BF16)
    kv[z, y, D:KROWS] = p_rows
    kv[z, y, KROWS:KROWS + HALF] = v_lo.astype(BF16)
    kv[z, y, KROWS + HALF:KROWS + D] = v_hi.astype(BF16)
    pl.semaphore_wait(barrier, len(all_peers))

    def kv_part(zz, yy, h):
        return kv.at[zz, yy, pl.ds(0, KROWS) if h == 0 else pl.ds(KROWS, D)]

    for h in (0, 1):
        part = kv_part(z, y, h)
        send(f"Y{h}", part, part, partner)
        for way in "RL":
            send(f"Z{way}10{h}", part, part, side[way][0])

    for h in range(HEADS):
        rows = slice(h * HALF, (h + 1) * HALF)
        lo, hi = halves(g_ref[:, h * D:(h + 1) * D].astype(F32))
        gc[x, rows, 0:D] = lo.astype(BF16)
        gc[x, rows, D:] = hi.astype(BF16)

    send("GL", gc.at[x], gc.at[x], left_x)
    send("GR", gc.at[x], gc.at[x], right_x)

    for h in range(HEADS):
        rows = slice(h * HALF, (h + 1) * HALF)
        qn, _ = normed(q_ref[:, h * D:(h + 1) * D].astype(F32))
        lo, hi = halves(rope(qn * qg_ref[...]))
        qc[x, rows, 0:D] = lo.astype(BF16)
        qc[x, rows, D:] = hi.astype(BF16)
    qc[x, Q:, 0:D] = p_rows
    qc[x, Q:, D:] = p_rows
    send("QR", qc.at[x], qc.at[x], right_x)
    send("QL", qc.at[x], qc.at[x], left_x)

    zero = jnp.zeros((HALF, D), BF16)

    def diagonal(lo, hi):
        return jnp.concatenate(
            [jnp.concatenate([lo, zero], axis=1), jnp.concatenate([zero, hi], axis=1)], axis=0
        )

    def own_k():
        return diagonal(kv[z, y, 0:HALF], kv[z, y, HALF:D])

    scores = dot(own_k(), qc[x, 0:Q], NT)
    key_row = lax.broadcasted_iota(jnp.int32, (D, Q), 0) % HALF
    query_lane = lax.broadcasted_iota(jnp.int32, (D, Q), 1) % HALF
    exps = jnp.where(key_row <= query_lane, jnp.exp2(scores * (SCALE * LOG2E)), 0.0)
    own_v = diagonal(kv[z, y, KROWS:KROWS + HALF], kv[z, y, KROWS + HALF:KROWS + D])
    probs_grad = dot(own_v, gc[x], NT)
    e_d[...] = exps
    g_d[...] = probs_grad
    both = exps * probs_grad
    for j in (1, 2, 3):
        sums[j] = jnp.zeros((4, 8, Q), F32)
    for part in range(2):
        rows = slice(part * HALF, (part + 1) * HALF)
        sums[0, part] = exps[rows].reshape(8, 8, Q).sum(0)
        sums[0, 2 + part] = both[rows].reshape(8, 8, Q).sum(0)

    def kv_progress(r, d):
        for h in (0, 1):
            for way in "RL":
                to, sign = side[way]
                if d == 4 and r != last[way]:
                    continue
                part = kv_part(zm(sign * d), ys[r], h)
                arrived(f"Z{way}{d}{r}{h}", part)
                if d < 3 or (d == 3 and r == last[way]):
                    send(f"Z{way}{d + 1}{r}{h}", part, part, to)

    def y_progress():
        for h in (0, 1):
            part = kv_part(z, ys[1], h)
            arrived(f"Y{h}", part)
            for way in "RL":
                send(f"Z{way}11{h}", part, part, side[way][0])

    def gradient_forward():
        arrived("GL", gc.at[xm(1)])
        send("G2", gc.at[xm(1)], gc.at[xm(1)], left_x)

    def query_forward():
        arrived("QR", qc.at[xm(-1)])
        send("Q2", qc.at[xm(-1)], qc.at[xm(-1)], right_x)

    def far_queries():
        arrived("Q2", qc.at[xm(2)])
        arrived("G2", gc.at[xm(2)])

    def key_event(r, d):
        return lambda: kv_progress(r, d)

    events = {
        0: (key_event(0, 1), y_progress, key_event(0, 2), gradient_forward, key_event(1, 1)),
        1: (
            key_event(0, 3), key_event(1, 2), query_forward,
            lambda: arrived("QL", qc.at[xm(1)]),
        ),
        2: (lambda: arrived("GR", gc.at[xm(-1)]),),
        3: (key_event(0, 4),),
        6: (key_event(1, 3),),
        9: (key_event(1, 4),),
        12: (far_queries,),
    }

    def block_rows(k, first, count):
        near = lax.rem(z + k, Z)
        far = lax.rem(z + (Z - 1) - k, Z)
        return jnp.concatenate(
            [kv[near, :, first:first + count, :], kv[far, :, first:first + count, :]], axis=0
        )

    def block_masks(k, b):
        pj = block_rows(k, D, 16).astype(F32)[:, 0:8, :]
        pq = qc[b, Q:, 0:D].astype(F32)[None, 0:8]
        early = jnp.where(pj < pq, 1.0, 0.0)
        other = jnp.where(pj == pq, 0.0, 1.0)
        return early, other

    def wide(v):
        return jnp.concatenate([v, v, v, v], axis=-1)

    def joined(lo, hi, early):
        e = early[:, 0:1, :].astype(BF16)
        return jnp.concatenate([lo * e, hi * (1.0 - e).astype(BF16)], axis=-1).reshape(4 * HALF, 2 * D)

    def pass_one(k, j, b, u):
        early, other = block_masks(k, b)
        klo, khi = block_rows(k, 0, HALF), block_rows(k, HALF, HALF)
        vlo, vhi = block_rows(k, KROWS, HALF), block_rows(k, KROWS + HALF, HALF)
        ex = jnp.exp2(dot(klo.reshape(4 * HALF, D), qc[b, 0:Q, D:], NT) * (SCALE * LOG2E))
        gp = dot(vlo.reshape(4 * HALF, D), gc[b, :, D:], NT)
        e_a[u] = ex
        g_a[u] = gp
        sums[j, 1] += ex.reshape(32, 8, Q).sum(0)
        sums[j, 3] += (ex * gp).reshape(32, 8, Q).sum(0)
        ex = jnp.exp2(dot(joined(klo, khi, early), qc[b, 0:Q], NT) * (SCALE * LOG2E))
        ex = ex.reshape(4, HALF, Q) * wide(other[:, 0:1, :])
        gp = dot(joined(vlo, vhi, early), gc[b], NT).reshape(4, HALF, Q)
        e_b[u] = ex.reshape(4 * HALF, Q)
        g_b[u] = gp.reshape(4 * HALF, Q)
        part = ex.reshape(4, 8, 8, Q).sum(1)
        partg = (ex * gp).reshape(4, 8, 8, Q).sum(1)
        ew = wide(early)
        sums[j, 0] += (part * ew).sum(0)
        sums[j, 1] += (part * (1.0 - ew)).sum(0)
        sums[j, 2] += (partg * ew).sum(0)
        sums[j, 3] += (partg * (1.0 - ew)).sum(0)

    def statistics_out(j):
        b = xm(rel_of(j))
        slot = stbuf.at[b, x]
        slot[...] = jnp.concatenate(
            [jnp.sum(sums[j], axis=1), jnp.zeros((4, Q), F32)], axis=0
        )
        for m in (1, 2, 3):
            send(f"ST{j}{m}", slot, slot, xdev[m])

    def first_loop(i, carry):
        far = i // 12
        k = (1 - far) * (i // 3) + far * (i - 12)
        j = (1 - far) * (i % 3) + far * 3
        for case, steps in events.items():
            @pl.when(i == case)
            def _(steps=steps):
                for step in steps:
                    step()
        rel = rel_of(j)
        pass_one(k, j, lax.rem(x + rel, X), k * 4 + rel)
        for case, done in ((9, 0), (10, 1), (11, 2), (15, 3)):
            @pl.when(i == case)
            def _(done=done):
                statistics_out(done)
        return carry

    lax.fori_loop(0, 16, first_loop, 0)

    token_row = (lax.broadcasted_iota(jnp.int32, (D, D), 0) % HALF).astype(F32)
    twice = token_row * (2.0 * freq_ref[...])
    ct_ref[...] = jnp.cos(twice)
    st_ref[...] = jnp.sin(twice)
    freq_col[...] = jnp.transpose(jnp.broadcast_to(freq_ref[...], (D, D)))[0:HALF]
    token_lane = (lax.broadcasted_iota(jnp.int32, (HALF, D), 1) % HALF).astype(F32)

    def query_tables(rel, carry):
        early_run = jnp.max(qc[lax.rem(x + rel, X), Q:, 0:D].astype(F32), axis=0, keepdims=True)
        for part in range(2):
            run = early_run if part == 0 else (2 * X * Y * Z - 1) - early_run
            angle = (run * HALF + token_lane) * (2.0 * freq_col[...])
            qcos[rel, part] = jnp.cos(angle)
            qsin[rel, part] = jnp.sin(angle)
        return carry

    lax.fori_loop(0, X, query_tables, 0)

    for k in range(4):
        dkacc[k] = jnp.zeros((4, D, D), F32)
        dvacc[k] = jnp.zeros((4, D, D), F32)
    for m in (1, 2, 3):
        dqacc[m] = jnp.zeros((2 * D, Q), F32)

    for j in range(4):
        for m in (1, 2, 3):
            arrived(f"ST{j}{m}", stbuf.at[xm(rel_of(j) - m), xm(-m)])
    for b in range(4):
        total = stbuf[b, 0]
        for s in range(1, 4):
            total = total + stbuf[b, s]
        inv = 1.0 / total[0:2]
        stats[b] = jnp.concatenate([inv, total[2:4] * inv, jnp.zeros((4, Q), F32)], axis=0)

    rowsel = lax.broadcasted_iota(jnp.int32, (D, Q), 0) < HALF
    pr = e_d[...] * jnp.where(rowsel, stats[x, 0:1], stats[x, 1:2])
    gs = (pr * (g_d[...] - jnp.where(rowsel, stats[x, 2:3], stats[x, 3:4]))).astype(BF16)
    pr = pr.astype(BF16)
    top = lax.broadcasted_iota(jnp.int32, (D, D), 0) < HALF
    full = dot(pr, gc[x], NN)
    dvacc[0, y] = jnp.where(top, full[:, 0:D], full[:, D:])
    full = dot(gs, qc[x, 0:Q], NN)
    dkacc[0, y] = jnp.where(top, full[:, 0:D], full[:, D:])
    dqacc[0] = dot(own_k(), gs, TN)

    def pass_two(k, b, rel, u):
        early, _ = block_masks(k, b)
        klo, khi = block_rows(k, 0, HALF), block_rows(k, HALF, HALF)
        pr = e_a[u] * stats[b, 1:2]
        gs = (pr * (g_a[u] - stats[b, 3:4])).astype(BF16)
        pr = pr.astype(BF16)
        dva = dot(pr, gc[b, :, D:], NN).reshape(4, HALF, D)
        dka = dot(gs, qc[b, 0:Q, D:], NN).reshape(4, HALF, D)
        dqacc[rel, D:, :] += dot(klo.reshape(4 * HALF, D), gs, TN)
        ew = wide(early[:, 0:1, :]) > 0.5
        invb = jnp.where(ew, stats[b, 0:1][None], stats[b, 1:2][None])
        delb = jnp.where(ew, stats[b, 2:3][None], stats[b, 3:4][None])
        pr = e_b[u].reshape(4, HALF, Q) * invb
        gs = (pr * (g_b[u].reshape(4, HALF, Q) - delb)).astype(BF16).reshape(4 * HALF, Q)
        pr = pr.astype(BF16).reshape(4 * HALF, Q)
        dvc = dot(pr, gc[b], NN).reshape(4, HALF, 2 * D)
        dkc = dot(gs, qc[b, 0:Q], NN).reshape(4, HALF, 2 * D)
        dqacc[rel] += dot(joined(klo, khi, early), gs, TN)
        e1 = early[:, 0:1, :]
        dkacc[k, :, 0:HALF] += dka + dkc[..., 0:D] * e1
        dkacc[k, :, HALF:] += dkc[..., D:] * (1.0 - e1)
        dvacc[k, :, 0:HALF] += dva + dvc[..., 0:D] * e1
        dvacc[k, :, HALF:] += dvc[..., D:] * (1.0 - e1)

    def pair_done(k):
        for place, zz in enumerate((zm(k), zm(-k - 1))):
            if zz is zpos[0]:
                continue
            rows = slice(2 * place, 2 * place + 2)
            dkv[zz, :, 0:D, :] = (dkacc[k, rows] * SCALE).astype(BF16)
            dkv[zz, :, D:, :] = dvacc[k, rows].astype(BF16)
        if k == 3:
            for wi, way in enumerate("RL"):
                r = last[way]
                send(f"S{way}1{r}", dkv.at[zm(4), ys[r]], ring.at[wi, 0, r], side[way][0])

    def ring_step(step, r):
        off = 4 - step
        for wi, way in enumerate("RL"):
            part = dkv.at[zm(off if way == "R" else -off), ys[r]]
            if step > 1 or r == last[way]:
                came = ring.at[wi, step - 1, r]
                arrived(f"S{way}{step}{r}", came)
                part[...] = (part[...].astype(F32) + came[...].astype(F32)).astype(BF16)
            send(f"S{way}{step + 1}{r}", part, ring.at[wi, step, r], side[way][0])

    def queries_out(m):
        dqs[m - 1] = dqacc[m].astype(BF16)
        send(f"DQ{m}", dqs.at[m - 1], dqr.at[m - 1], xdev[m])

    def second_loop(i, carry):
        a, c = (i + 12) // 16, (i + 9) // 16
        k = (1 - a) * 3 + (a - c) * (6 - i) + c * (5 - (i + 2) // 3)
        j = (1 - a) * (3 - i) + (a - c) * 3 + c * (2 - (i + 2) % 3)
        rel = rel_of(j)
        pass_two(k, lax.rem(x + rel, X), rel, k * 4 + rel)
        for case, m in ((6, 2), (13, 3), (14, 1)):
            @pl.when(i == case)
            def _(m=m):
                queries_out(m)
        for case in range(4):
            @pl.when(i == (3 if case == 0 else 3 * case + 6))
            def _(case=case):
                pair_done(3 - case)
                if case == 1:
                    ring_step(1, 1)
                    ring_step(1, 0)
        return carry

    lax.fori_loop(0, 16, second_loop, 0)

    ring_step(2, 1)

    first_lanes = lax.broadcasted_iota(jnp.int32, (1, D), 1) < HALF

    def key_share(k, carry):
        plain, cosined, sined = carry
        grad = dkacc[k].reshape(4 * D, D)
        rot = block_rows(k, 0, D).astype(F32).reshape(4 * D, D)
        straight = (grad * rot).reshape(4, 2, HALF, D)
        crossed = (grad * pltpu.roll(rot, HALF, 1)).reshape(4, 2, HALF, D)
        ct, st = ct_ref[0:HALF], st_ref[0:HALF]
        early_run = block_rows(k, D, 16).astype(F32)[:, 0:1, :]
        late_run = (2 * X * Y * Z - 1) - early_run
        run = jnp.concatenate([early_run[:, None], late_run[:, None]], axis=1)
        angle = run * (2.0 * HALF * freq_ref[...])
        cp, sp = jnp.cos(angle), jnp.sin(angle)

        def over_tokens(v):
            return jnp.sum(v, axis=2, keepdims=True)

        plain = plain + jnp.sum(over_tokens(straight), axis=(0, 1))
        cosined = cosined + jnp.sum(
            cp * over_tokens(straight * ct) - sp * over_tokens(straight * st), axis=(0, 1)
        )
        sined = sined + jnp.sum(
            sp * over_tokens(crossed * ct) + cp * over_tokens(crossed * st), axis=(0, 1)
        )
        return plain, cosined, sined

    none = jnp.zeros((1, D), F32)
    plain, cosined, sined = lax.fori_loop(0, 4, key_share, (none, none, none))

    def swap_lanes(v):
        return pltpu.roll(jnp.broadcast_to(v, (8, D)), HALF, 1)[0:1]

    both_sines = sined + swap_lanes(sined)
    key_gain = plain + swap_lanes(plain) + cosined - swap_lanes(cosined)
    key_gain = key_gain + jnp.where(first_lanes, both_sines, -both_sines)
    key_gain = key_gain * (0.5 * SCALE) / kg_ref[...]

    row_id = lax.broadcasted_iota(jnp.int32, (2 * D, 2 * D), 0)
    lane_id = lax.broadcasted_iota(jnp.int32, (2 * D, 2 * D), 1)
    identity = jnp.where(row_id == lane_id, 1.0, 0.0).astype(BF16)

    def over_heads(v):
        return v[:, 0:D] + v[:, D:2 * D] + v[:, 2 * D:3 * D] + v[:, 3 * D:]

    def query_share(rel, carry):
        plain, turned = carry
        rot = dot(identity, qc[lax.rem(x + rel, X), 0:Q], NT)
        grad = dqacc[rel]
        for part in range(2):
            a, b = grad[part * D:part * D + HALF], grad[part * D + HALF:part * D + D]
            e, f = rot[part * D:part * D + HALF], rot[part * D + HALF:part * D + D]
            ae, bf = over_heads(a * e), over_heads(b * f)
            plain = plain + ae + bf
            turned = turned + qcos[rel, part] * (ae - bf) + qsin[rel, part] * over_heads(a * f + b * e)
        return plain, turned

    none = jnp.zeros((HALF, D), F32)
    plain, turned = lax.fori_loop(0, X, query_share, (none, none))
    query_gain = jnp.transpose(jnp.concatenate([plain + turned, plain - turned], axis=0))
    query_gain = jnp.sum(query_gain, axis=0, keepdims=True) * (0.5 * SCALE) / qg_ref[...]

    def gain_copies(stage):
        me, size, peer = groups[stage]
        return [
            pltpu.make_async_remote_copy(
                src_ref=gsum.at[stage], dst_ref=gbuf.at[stage, me],
                send_sem=gssem.at[stage, j], recv_sem=grsem.at[stage, j],
                device_id=peer(j), device_id_type=pl.DeviceIdType.MESH,
            )
            for j in range(1, size)
        ]

    def gain_start(stage, mine):
        gsum[stage] = mine
        gbuf[stage, groups[stage][0]] = mine
        copies = gain_copies(stage)
        for c in copies:
            c.start()
        return copies

    def gain_finish(stage, copies):
        for c in copies:
            c.wait()
        total = gbuf[stage, 0]
        for j in range(1, groups[stage][1]):
            total = total + gbuf[stage, j]
        return total

    copies = gain_start(0, jnp.concatenate([query_gain, key_gain, jnp.zeros((6, D), F32)], axis=0))

    def own_sum(r):
        total = jnp.concatenate([dkacc[0, ys[r]] * SCALE, dvacc[0, ys[r]]], axis=0)
        for wi in (0, 1):
            total = total + ring[wi, 3, r].astype(F32)
        return total

    def ring_end(r):
        for wi, way in enumerate("RL"):
            arrived(f"S{way}4{r}", ring.at[wi, 3, r])

    ring_step(2, 0)
    ring_step(3, 1)
    copies = gain_start(1, gain_finish(0, copies))
    ring_step(3, 0)

    def stored(lo, hi):
        return jnp.concatenate(
            [jnp.where(swapped, hi, lo), jnp.where(swapped, lo, hi)], axis=0
        )

    def norm_back(g, xn, inverse, gain):
        s = g * gain
        return inverse * (s - xn * jnp.mean(s * xn, axis=-1, keepdims=True))

    ring_end(1)
    ysend[...] = own_sum(1).astype(BF16)
    send("SY", ysend, yrecv, partner)
    whole = dqacc[0]
    for m in (1, 2, 3):
        arrived(f"DQ{m}", dqr.at[m - 1])
        whole = whole + dqr[m - 1].astype(F32)
    turned = jnp.transpose(whole) * SCALE
    for h in range(HEADS):
        if h == 5:
            copies = gain_start(2, gain_finish(1, copies))
        cols = slice(h * D, (h + 1) * D)
        rows = slice(h * HALF, (h + 1) * HALF)
        gq = unrope(stored(turned[rows, 0:D], turned[rows, D:]))
        qn, inverse = normed(q_ref[:, cols].astype(F32))
        dq_ref[:, cols] = norm_back(gq, qn, inverse, qg_ref[...]).astype(BF16)

    ring_end(0)
    arrived("SY", yrecv)
    own = own_sum(0) + yrecv[...].astype(F32)
    gk = unrope(stored(own[:HALF], own[HALF:D]))
    kn, inverse = normed(k_ref[...].astype(F32))
    dk_ref[...] = norm_back(gk, kn, inverse, kg_ref[...]).astype(BF16)
    dv_ref[...] = stored(own[D:D + HALF], own[D + HALF:]).astype(BF16)

    total = gain_finish(2, copies)
    qgain_ref[...] = total[0:1]
    kgain_ref[...] = total[1:2]

    for name, src, dst, to in started:
        copy(name, src, dst, to).wait_send()


def place(*refs):
    sems = refs[-1]
    copies = [pltpu.make_async_copy(refs[i], refs[5 + i], sems.at[i]) for i in range(5)]
    for c in copies:
        c.start()
    for c in copies:
        c.wait()


def shards(heads_axis, query_raw, key_before_norm, values, grads, q_gain, k_gain, tok_pos):
    frequency = np.power(np.float32(BASE), -(np.arange(HALF, dtype=np.float32) * np.float32(2.0 / D)))
    frequency = jnp.asarray(np.tile(frequency.astype(np.float32), 2).reshape(1, D))
    vmem = pl.BlockSpec(memory_space=pltpu.VMEM)
    count = len(MSG)
    shapes = (
        jax.ShapeDtypeStruct((D, HEADS * D), BF16),
        jax.ShapeDtypeStruct((D, D), BF16),
        jax.ShapeDtypeStruct((D, D), BF16),
        jax.ShapeDtypeStruct((1, D), F32),
        jax.ShapeDtypeStruct((1, D), F32),
    )
    results = pl.pallas_call(
        functools.partial(body, heads_axis),
        out_shape=shapes,
        in_specs=[vmem] * 8,
        out_specs=(vmem,) * 5,
        scratch_shapes=[
            pltpu.VMEM((D, D), F32),
            pltpu.VMEM((D, D), F32),
            pltpu.VMEM((Z, Y, KROWS + D, D), BF16),
            pltpu.VMEM((X, Q + 16, 2 * D), BF16),
            pltpu.VMEM((X, Q, 2 * D), BF16),
            pltpu.VMEM((16, 4 * HALF, Q), F32),
            pltpu.VMEM((16, 4 * HALF, Q), F32),
            pltpu.VMEM((16, 4 * HALF, Q), F32),
            pltpu.VMEM((16, 4 * HALF, Q), F32),
            pltpu.VMEM((D, Q), F32),
            pltpu.VMEM((D, Q), F32),
            pltpu.VMEM((4, 4, 8, Q), F32),
            pltpu.VMEM((X, X, 8, Q), F32),
            pltpu.VMEM((X, 8, Q), F32),
            pltpu.VMEM((X, 2 * D, Q), F32),
            pltpu.VMEM((4, 4, D, D), F32),
            pltpu.VMEM((4, 4, D, D), F32),
            pltpu.VMEM((D, D), F32),
            pltpu.VMEM((D, D), F32),
            pltpu.VMEM((X, 2, HALF, D), F32),
            pltpu.VMEM((X, 2, HALF, D), F32),
            pltpu.VMEM((HALF, D), F32),
            pltpu.VMEM((Z, Y, 2 * D, D), BF16),
            pltpu.VMEM((2, 4, 2, 2 * D, D), BF16),
            pltpu.VMEM((3, 2 * D, Q), BF16),
            pltpu.VMEM((3, 2 * D, Q), BF16),
            pltpu.VMEM((2 * D, D), BF16),
            pltpu.VMEM((2 * D, D), BF16),
            pltpu.VMEM((3, 8, 8, D), F32),
            pltpu.VMEM((3, 8, D), F32),
            pltpu.SemaphoreType.DMA((count,)),
            pltpu.SemaphoreType.DMA((count,)),
            pltpu.SemaphoreType.DMA((3, 8)),
            pltpu.SemaphoreType.DMA((3, 8)),
        ],
        compiler_params=pltpu.CompilerParams(
            collective_id=0, has_side_effects=True, vmem_limit_bytes=60 * 1024 * 1024
        ),
    )(
        query_raw, key_before_norm, values, grads,
        q_gain.reshape(1, D), k_gain.reshape(1, D), tok_pos.reshape(1, D), frequency,
    )
    anywhere = pl.BlockSpec(memory_space=pl.ANY)
    dq, dk, dv, query_gain, key_gain = pl.pallas_call(
        place,
        out_shape=shapes,
        in_specs=[vmem] * 5,
        out_specs=(anywhere,) * 5,
        scratch_shapes=[pltpu.SemaphoreType.DMA((5,))],
    )(*results)
    return dq, dk, dv, query_gain.reshape(D), key_gain.reshape(D)


def solution(mesh):
    split = P("ctx", "head")
    return jax.shard_map(
        functools.partial(shards, mesh.shape["head"]),
        mesh=mesh,
        in_specs=(split, split, split, split, P(), P(), P("ctx")),
        out_specs=(split, split, split, P(), P()),
        check_vma=False,
    )
```
